32 devices in a mesh: expert: 8 (over z, y), shard: 4 (over x, core).
Axes of the slice: x: 2, y: 2, z: 4, core: 2. Of those that a mesh axis runs over, the one named last changes fastest.
Arguments:
- tokens: bfloat16 [8, 1024, 768], P('expert', 'shard'), may hold values from -6 to 6
- gain_attn: bfloat16 [768], P('shard'), may hold values from 0.5 to 1.5
- pos_table: bfloat16 [32, 12], P('shard'), may hold values from -4 to 4
- buckets: int32 [2047], replicated, may hold values from 0 to 31
- w_query: bfloat16 [768, 768], P('shard'), may hold values from -0.21875 to 0.21875
- w_key: bfloat16 [768, 768], P('shard'), may hold values from -0.21875 to 0.21875
- w_value: bfloat16 [768, 768], P('shard'), may hold values from -0.21875 to 0.21875
- w_attn_out: bfloat16 [768, 768], P('shard'), may hold values from -0.875 to 0.875
- w_router: bfloat16 [768, 8], P('shard'), may hold values from -0.109375 to 0.109375
- gain_ffn: bfloat16 [768], P('shard'), may hold values from 0.5 to 1.5
- w_in: bfloat16 [8, 768, 3072], P('expert', None, 'shard'), may hold values from -0.21875 to 0.21875
- w_out: bfloat16 [8, 3072, 768], P('expert', 'shard'), may hold values from -10 to 10
- expert_ids: int32 [8, 1024], P('expert', 'shard'), may hold values from 0 to 7, as said below
- slots: int32 [8, 1024], P('expert', 'shard'), may hold values from 0 to 3, as said below
- keep: int32 [8, 1024], P('expert', 'shard'), may hold values from 0 to 1, as said below
- grad_out: bfloat16 [8, 1024, 768], P('expert', 'shard'), may hold values from -6 to 6
Outputs:
- output: bfloat16 [8, 1024, 768], P('expert', 'shard')
- grad_tokens: float32 [8, 1024, 768], P('expert', 'shard')
- grad_gain_attn: float32 [768], P('shard')
- grad_pos_table: float32 [32, 12], P('shard')
- grad_w_query: float32 [768, 768], P('shard')
- grad_w_key: float32 [768, 768], P('shard')
- grad_w_value: float32 [768, 768], P('shard')
- grad_w_attn_out: float32 [768, 768], P('shard')
- grad_w_router: float32 [768, 8], P('shard')
- grad_gain_ffn: float32 [768], P('shard')
- grad_w_in: float32 [8, 768, 3072], P('expert', None, 'shard')
- grad_w_out: float32 [8, 3072, 768], P('expert', 'shard')
The draws below stay inside these ranges and needn't reach their ends.
Inputs may be any that keep to these rules, and one draw needn't show every extreme that they name: `expert_ids`: one expert, drawn from the seed, is chosen by 4 or more tokens in every aligned block of 256 tokens of a sequence. For a kept token, slots counts the earlier tokens of its aligned block of 256 tokens that chose the same expert; for a dropped token it is 3. keep is 1 exactly for the first 4 tokens of each aligned block of 256 tokens that choose a given expert, so the kept tokens of a block and expert have distinct slots, and in every block some expert has 4 kept tokens.
All inputs are finite; a program needn't handle non-finite values.
Results may differ from the reference program's by a relative error of at most 0.02.
Values may be sent and summed in bfloat16 or wider, within the bound.
No kernel may reach another device: no remote copies, remote signals or barrier semaphores. Data moves between devices by JAX's collectives and lax.ppermute only.
A program may use at most 320 MiB of HBM per device.

```python
import jax
import jax.numpy as jnp
from jax import lax

D = 768
HEADS = 12
HEAD_DIM = 64
FF = 3072
BUCKETS = 32
CAP = 4
TOK_DEV = 256
LEN = 1024
SEQS = 8
EXPERTS = 8
OFFSETS = 2047
N_SHARD = 4


def routing(key):
    blocks = SEQS * LEN // TOK_DEV
    weight_key, pick_key, hot_key, order_key = jax.random.split(key, 4)
    loads = 2 ** jax.random.randint(weight_key, (EXPERTS,), 0, 4)
    bounds = jnp.cumsum(loads)
    picks = jax.random.randint(pick_key, (blocks, TOK_DEV), 0, bounds[-1])
    picked = jnp.searchsorted(bounds, picks, side='right').astype(jnp.int32)
    hot_expert = jax.random.randint(hot_key, (), 0, EXPERTS)
    order_keys = jax.random.split(order_key, blocks)
    ranks = jax.vmap(lambda one_key: jax.random.permutation(one_key, TOK_DEV))(order_keys)
    picked = jnp.where(ranks < CAP, hot_expert, picked).astype(jnp.int32)
    onehot = (picked[:, :, None] == jnp.arange(EXPERTS)[None, None, :]).astype(jnp.int32)
    earlier = jnp.cumsum(onehot, axis=1) - onehot
    position = jnp.sum(earlier * onehot, axis=-1)
    kept = (position < CAP).astype(jnp.int32)
    slot_of = jnp.minimum(position, CAP - 1).astype(jnp.int32)
    return (picked.reshape(SEQS, LEN), slot_of.reshape(SEQS, LEN), kept.reshape(SEQS, LEN))


def draw_expert_ids(key, part):
    return routing(key)[0]


def draw_slots(key, part):
    return routing(key)[1]


def draw_keep(key, part):
    return routing(key)[2]


def plant(values, stream_key, low, largest):
    longest = values.shape.index(max(values.shape))
    spots = []
    for shift in (0, 1):
        where = [jax.random.randint(jax.random.fold_in(stream_key, axis), (), 0, length) for axis, length in enumerate(values.shape)]
        where[longest] = (where[longest] + shift) % values.shape[longest]
        spots.append(tuple(where))
    return values.at[spots[0]].set(low).at[spots[1]].set(largest)


def steps_of(rng, extent, cuts, low, top_value):
    loudness, own = 1.0, jax.random.fold_in(rng, 6)
    for dim, parts in cuts:
        draws = jnp.exp(jax.random.uniform(jax.random.fold_in(own, dim), (parts,), jnp.float32, low / len(cuts), top_value / len(cuts)))
        loudness = loudness * jnp.repeat(draws, extent[dim] // parts).reshape([-1 if axis == dim else 1 for axis in range(len(extent))])
    return loudness


def bell_draw(rng, extent, width, most, cuts=(), held_as=jnp.bfloat16):
    array = jax.random.normal(rng, extent, jnp.float32) * width
    if len(cuts) > 0:
        array = steps_of(rng, extent, cuts, -0.22, 0.18) * array
    return jnp.clip(array, min=-most, max=most).astype(held_as)


def setup_inputs(seed: int = 0) -> dict:
    seeds = jax.random.split(jax.random.key(seed), 17)
    tokens = bell_draw(seeds[0], (SEQS, LEN, D), 1.0, 6.0, ((0, 8), (1, 4)))
    gain_attn = jnp.clip(1.0 + 0.1 * jax.random.normal(seeds[1], (D,), jnp.float32), 0.5, 1.5).astype(jnp.bfloat16)
    pos_table = bell_draw(seeds[2], (BUCKETS, HEADS), 1.0, 4.0, ((0, 4),))
    buckets = plant(jax.random.randint(seeds[3], (OFFSETS,), 0, BUCKETS), jax.random.fold_in(seeds[3], 1), 0, BUCKETS - 1).astype(jnp.int32)
    w_query = bell_draw(seeds[4], (D, D), D ** -0.5, 0.21875, ((0, 4),))
    w_key = bell_draw(seeds[5], (D, D), D ** -0.5, 0.21875, ((0, 4),))
    w_value = bell_draw(seeds[6], (D, D), D ** -0.5, 0.21875, ((0, 4),))
    w_attn_out = bell_draw(seeds[7], (D, D), (D // 16) ** -0.5, 0.875, ((0, 4),))
    w_router = bell_draw(seeds[8], (D, EXPERTS), (4 * D) ** -0.5, 0.109375, ((0, 4),))
    gain_ffn = jnp.clip(1.0 + 0.1 * jax.random.normal(seeds[9], (D,), jnp.float32), 0.5, 1.5).astype(jnp.bfloat16)
    w_in = bell_draw(seeds[10], (EXPERTS, D, FF), D ** -0.5, 0.21875, ((0, 8), (2, 4)))
    w_out = bell_draw(seeds[11], (EXPERTS, FF, D), 1.7, 10.0, ((0, 8), (1, 4)))
    expert_ids = draw_expert_ids(jax.random.fold_in(seeds[16], 71), 0)
    slots = draw_slots(jax.random.fold_in(seeds[16], 71), 0)
    keep = draw_keep(jax.random.fold_in(seeds[16], 71), 0)
    grad_out = bell_draw(seeds[15], (SEQS, LEN, D), 1.0, 6.0, ((0, 8), (1, 4)))
    return {"tokens": tokens, "gain_attn": gain_attn, "pos_table": pos_table, "buckets": buckets, "w_query": w_query, "w_key": w_key, "w_value": w_value, "w_attn_out": w_attn_out, "w_router": w_router, "gain_ffn": gain_ffn, "w_in": w_in, "w_out": w_out, "expert_ids": expert_ids, "slots": slots, "keep": keep, "grad_out": grad_out}


best_expert = lax.Precision.HIGHEST
epsilon = 1e-06

@jax.custom_vjp
def low(v):
    return lax.optimization_barrier(v.astype(jnp.bfloat16)).astype(jnp.float32)

@jax.custom_vjp
def low_back(v):
    return v

def low_keep(v):
    return (low(v), None)

def low_pass(kept, grad):
    return (grad,)

def back_keep(v):
    return (v, None)

def back_low(kept, grad):
    return (low(grad),)
low.defvjp(low_keep, low_pass)
low_back.defvjp(back_keep, back_low)

def rms_factor(values):
    return lax.rsqrt(lax.optimization_barrier(jnp.mean(values * values, axis=-1, keepdims=True)) + epsilon)

def expert_block(item):
    rows_in, first_w, second_w = item
    hidden = low_back(jnp.dot(rows_in, first_w, precision=best_expert))
    activation = low(jax.nn.gelu(hidden))
    return low_back(low(jnp.dot(activation, second_w, precision=best_expert)))

def reference(tokens, gain_attn, pos_table, buckets, w_query, w_key, w_value, w_attn_out, w_router, gain_ffn, w_in, w_out, expert_ids, slots, keep, grad_out):
    length = tokens.shape[1]
    places = jnp.arange(length)
    bucket_grid = buckets[places[None, :] - places[:, None] + length - 1]
    experts = w_router.shape[1]
    target_slot = (expert_ids * CAP + slots).reshape(SEQS, N_SHARD, TOK_DEV)
    kept_mask = keep.reshape(SEQS, N_SHARD, TOK_DEV)
    placing = ((target_slot[:, :, None, :] == jnp.arange(experts * CAP)[None, None, :, None]) & (kept_mask[:, :, None, :] > 0)).astype(jnp.float32)
    chosen = (expert_ids[..., None] == jnp.arange(experts)).astype(jnp.float32)

    def forward(tokens_f, gain_one, table_f, query_w, key_w, value_w, out_w, router_weight, gain_two, first_w, second_w):

        def mixer(sequence):
            normed = low(sequence * rms_factor(sequence) * gain_one)
            queries = low_back(low(jnp.dot(normed, query_w, precision=best_expert)))
            keys = low_back(low(jnp.dot(normed, key_w, precision=best_expert)))
            values = low_back(low(jnp.dot(normed, value_w, precision=best_expert)))
            q_heads = queries.reshape(length, HEADS, HEAD_DIM)
            key_head_rows = keys.reshape(length, HEADS, HEAD_DIM)
            v_heads = values.reshape(length, HEADS, HEAD_DIM)
            offset_bias = jnp.transpose(table_f[bucket_grid], (2, 0, 1))
            scores = jnp.einsum('ihd,jhd->hij', q_heads, key_head_rows, precision=best_expert) * HEAD_DIM ** (-0.5) + offset_bias
            scores = low_back(scores)
            probs_low = low(jax.nn.softmax(scores, axis=-1))
            mixed_heads = jnp.einsum('hij,jhd->ihd', probs_low, v_heads, precision=best_expert).reshape(length, D)
            mixed_heads = low_back(low(mixed_heads))
            return sequence + low_back(jnp.dot(mixed_heads, out_w, precision=best_expert))
        residual = lax.map(jax.checkpoint(mixer), tokens_f)
        feedforward_input = low(residual * rms_factor(residual) * gain_two)
        router_scores = jnp.einsum('wrt,ty->wry', feedforward_input, router_weight, precision=best_expert)
        gating = lax.optimization_barrier(jnp.sum(jax.nn.softmax(router_scores, axis=-1) * chosen, axis=-1))
        grouped = feedforward_input.reshape(SEQS, N_SHARD, TOK_DEV, D)
        slot_rows = jnp.einsum('abrt,abtd->abrd', placing, grouped, precision=best_expert)
        by_expert = slot_rows.reshape(SEQS, N_SHARD, experts, CAP, D).transpose(2, 0, 1, 3, 4).reshape(experts, SEQS * N_SHARD * CAP, D)
        by_expert = low_back(by_expert)
        expert_out = lax.map(jax.checkpoint(expert_block), (by_expert, first_w, second_w))
        regrouped = expert_out.reshape(experts, SEQS, N_SHARD, CAP, D).transpose(1, 2, 0, 3, 4).reshape(SEQS, N_SHARD, experts * CAP, D)
        token_out = jnp.einsum('abrt,abrd->abtd', placing, regrouped, precision=best_expert).reshape(SEQS, length, D)
        return residual + gating[..., None] * token_out
    floats = tuple((a.astype(jnp.float32) for a in (tokens, gain_attn, pos_table, w_query, w_key, w_value, w_attn_out, w_router, gain_ffn, w_in, w_out)))
    result, pull = jax.vjp(forward, *floats)
    grads = pull(grad_out.astype(jnp.float32))
    return (result.astype(jnp.bfloat16), grads[0], grads[1], grads[2], grads[3], grads[4], grads[5], grads[6], grads[7], grads[8], grads[9], grads[10])
```

```python
import functools

import jax
import jax.numpy as jnp
from jax import lax
from jax.experimental import pallas as pl
from jax.experimental.pallas import tpu as pltpu
from jax.sharding import PartitionSpec as P

HEADS = 12
HEAD_DIM = 64
CAP = 4
QBLOCK = 256

bf16 = jnp.bfloat16
f32 = jnp.float32
highest = lax.Precision.HIGHEST
epsilon = 1e-06
score_scale = HEAD_DIM ** (-0.5)

NN = (((1,), (0,)), ((), ()))
NT = (((1,), (1,)), ((), ()))
TN = (((0,), (0,)), ((), ()))


def mm(a, b, dims=NN):
    return lax.dot_general(a, b, dims, preferred_element_type=f32)


def mm_exact(a, b, dims=NN):
    return lax.dot_general(a, b, dims, precision=highest, preferred_element_type=f32)


def rms_factor(values):
    return lax.rsqrt(jnp.mean(values * values, axis=-1, keepdims=True) + epsilon)


def norm_back(grad_normed, normed_pre, factor):
    return factor * (
        grad_normed - normed_pre * jnp.mean(grad_normed * normed_pre, axis=-1, keepdims=True)
    )


def gelu_back(hidden, grad_act):
    return jax.vjp(jax.nn.gelu, hidden)[1](grad_act)[0]


def swap(value, axis, bits):
    count = lax.axis_size(axis)
    return lax.ppermute(value, axis, [(i, i ^ bits) for i in range(count)])


def partner(axis, bits):
    return jnp.bitwise_xor(lax.axis_index(axis), bits)


def take(stacked, index):
    return lax.dynamic_index_in_dim(stacked, index, axis=0, keepdims=False)


def gather_pairs(value, axis):
    count = lax.axis_size(axis)
    held = value[None]
    step = count // 2
    order = [0]
    while step >= 1:
        held = jnp.concatenate([held, swap(held, axis, step)], axis=0)
        order = order + [o ^ step for o in order]
        step //= 2
    return [held[order.index(t)] for t in range(count)]


def in_order(blocks, axis):
    out = jnp.zeros((len(blocks),) + blocks[0].shape, blocks[0].dtype)
    for t, block in enumerate(blocks):
        out = lax.dynamic_update_slice_in_dim(out, block[None], partner(axis, t), axis=0)
    return out


def bias_rows(offsets_row, width):
    rows = jnp.broadcast_to(offsets_row, (8, width))
    rows = pltpu.roll(rows, width - (QBLOCK - 1), 1)
    place = lax.broadcasted_iota(jnp.int32, (8, width), 0)
    for bit in (1, 2, 4):
        rows = jnp.where((place & bit) != 0, pltpu.roll(rows, bit, 1), rows)
    count = 8
    while count < QBLOCK:
        rows = jnp.concatenate([rows, pltpu.roll(rows, count, 1)], axis=0)
        count *= 2
    return rows


def diagonal_row(grid, width):
    count = QBLOCK
    while count > 8:
        count //= 2
        grid = grid[:count] + pltpu.roll(grid[count:], width - count, 1)
    place = lax.broadcasted_iota(jnp.int32, (8, width), 0)
    for bit in (4, 2, 1):
        grid = jnp.where((place & bit) != 0, pltpu.roll(grid, width - bit, 1), grid)
    return pltpu.roll(jnp.sum(grid, axis=0, keepdims=True), QBLOCK - 1, 1)


def attention_forward_kernel(q_ref, k_ref, v_ref, table_ref, onehot_ref, mixed_ref, log_ref, bias_ref):
    total = q_ref.shape[0]
    width = onehot_ref.shape[1]
    heads = q_ref.shape[1] // HEAD_DIM
    blocks = total // QBLOCK
    offsets = mm(table_ref[...], onehot_ref[...])
    for h in range(heads):
        cols = slice(h * HEAD_DIM, (h + 1) * HEAD_DIM)
        bias_ref[...] = bias_rows(offsets[h : h + 1, :], width)
        keys = k_ref[:, cols]
        values = v_ref[:, cols]
        for a in range(blocks):
            rows = slice(a * QBLOCK, (a + 1) * QBLOCK)
            start = total - QBLOCK * (a + 1)
            scores = mm(q_ref[rows, cols], keys, NT) * score_scale
            scores = scores + bias_ref[:, start : start + total]
            peak = jnp.max(scores, axis=-1, keepdims=True)
            raised = jnp.exp(scores - peak)
            norm = jnp.sum(raised, axis=-1, keepdims=True)
            probs_low = (raised * (1.0 / norm)).astype(bf16)
            mixed_ref[rows, cols] = mm(probs_low, values).astype(bf16)
            log_ref[rows, h : h + 1] = peak + jnp.log(norm)


def attention_backward_kernel(
    q_ref, k_ref, v_ref, gm_ref, log_ref, table_ref, onehot_ref,
    gq_ref, gk_ref, gv_ref, gt_ref, bias_ref, sums_ref, diag_ref,
):
    total = q_ref.shape[0]
    width = onehot_ref.shape[1]
    heads = q_ref.shape[1] // HEAD_DIM
    blocks = total // QBLOCK
    offsets = mm(table_ref[...], onehot_ref[...])
    diag_ref[...] = jnp.zeros_like(diag_ref)
    for h in range(heads):
        cols = slice(h * HEAD_DIM, (h + 1) * HEAD_DIM)
        bias_ref[...] = bias_rows(offsets[h : h + 1, :], width)
        sums_ref[...] = jnp.zeros_like(sums_ref)
        keys = k_ref[:, cols]
        values = v_ref[:, cols]
        gk = jnp.zeros((HEAD_DIM, total), f32)
        gv = jnp.zeros((HEAD_DIM, total), f32)
        for a in range(blocks):
            rows = slice(a * QBLOCK, (a + 1) * QBLOCK)
            start = total - QBLOCK * (a + 1)
            queries = q_ref[rows, cols]
            gm = gm_ref[rows, cols]
            scores = mm(queries, keys, NT) * score_scale
            scores = scores + bias_ref[:, start : start + total]
            probs = jnp.exp(scores - log_ref[rows, h : h + 1])
            grad_probs = mm(gm, values, NT)
            dots = jnp.sum(probs * grad_probs, axis=-1, keepdims=True)
            grad_scores_f = probs * (grad_probs - dots)
            grad_scores = grad_scores_f.astype(bf16)
            sums_ref[:, start : start + total] += grad_scores.astype(f32)
            gq_ref[rows, cols] = (mm(grad_scores, keys) * score_scale).astype(bf16)
            gk = gk + mm(queries, grad_scores, TN)
            gv = gv + mm(gm, probs.astype(bf16), TN)
        gk_ref[:, cols] = (gk * score_scale).T.astype(bf16)
        gv_ref[:, cols] = gv.T.astype(bf16)
        diag_ref[h : h + 1, :] = diagonal_row(sums_ref[...], width)
    gt_ref[...] = mm_exact(diag_ref[...], onehot_ref[...].astype(f32), NT)


def vmem_specs(count):
    return [pl.BlockSpec(memory_space=pltpu.VMEM)] * count


def attention_forward(queries, keys, values, table, onehot):
    total, width = queries.shape
    flops = 4 * total * total * width
    return pl.pallas_call(
        attention_forward_kernel,
        out_shape=(
            jax.ShapeDtypeStruct((total, width), bf16),
            jax.ShapeDtypeStruct((total, 8), f32),
        ),
        in_specs=vmem_specs(5),
        out_specs=tuple(vmem_specs(2)),
        scratch_shapes=[pltpu.VMEM((QBLOCK, onehot.shape[1]), f32)],
        compiler_params=pltpu.CompilerParams(vmem_limit_bytes=48 * 2**20),
        cost_estimate=pl.CostEstimate(
            flops=flops, bytes_accessed=8 * total * width, transcendentals=3 * total * total
        ),
        name="attention_forward",
    )(queries, keys, values, table, onehot)


def attention_backward(queries, keys, values, gm, logs, table, onehot):
    total, width = queries.shape
    flops = 10 * total * total * width
    low = jax.ShapeDtypeStruct((total, width), bf16)
    return pl.pallas_call(
        attention_backward_kernel,
        out_shape=(low, low, low, jax.ShapeDtypeStruct((table.shape[0], table.shape[1]), f32)),
        in_specs=vmem_specs(7),
        out_specs=tuple(vmem_specs(4)),
        scratch_shapes=[
            pltpu.VMEM((QBLOCK, onehot.shape[1]), f32),
            pltpu.VMEM((QBLOCK, onehot.shape[1]), f32),
            pltpu.VMEM((8, onehot.shape[1]), f32),
        ],
        compiler_params=pltpu.CompilerParams(vmem_limit_bytes=48 * 2**20),
        cost_estimate=pl.CostEstimate(
            flops=flops, bytes_accessed=14 * total * width, transcendentals=3 * total * total
        ),
        name="attention_backward",
    )(queries, keys, values, gm, logs, table, onehot)


def per_device(
    tokens, gain_attn, pos_table, buckets, w_query, w_key, w_value, w_attn_out, w_router, gain_ffn,
    w_in, w_out, expert_ids, slots, keep, grad_out,
):
    shards = lax.axis_size("shard")
    experts = lax.axis_size("expert")
    me = lax.axis_index("shard")
    block_rows, model_width = tokens.shape[1:]
    total_rows = block_rows * shards
    rows_own = w_query.shape[0]
    local_heads = HEADS // shards
    part_width = local_heads * HEAD_DIM
    expert_count = w_router.shape[1]
    slot_count = expert_count * CAP
    bucket_count = pos_table.shape[0] * shards

    target = jnp.where(keep[0] > 0, expert_ids[0] * CAP + slots[0], -1).astype(jnp.int32)
    small = jnp.concatenate(
        [gain_attn, gain_ffn, pos_table.reshape(-1), w_router.reshape(-1)]
    )
    small_size = small.shape[0]
    small = jnp.pad(small, (0, -small_size % 2048)).reshape(-1, 128)
    small_all = in_order(gather_pairs(small, "shard"), "shard").reshape(shards, -1)
    gain_one = small_all[:, :rows_own].reshape(-1).astype(f32)
    gain_two = small_all[:, rows_own : 2 * rows_own].reshape(-1).astype(f32)
    at = 2 * rows_own
    table_full = small_all[:, at : at + pos_table.size].reshape(bucket_count, HEADS)
    at += pos_table.size
    router_weight = small_all[:, at : at + w_router.size].reshape(model_width, expert_count)

    stacked = jnp.stack([w_query, w_key, w_value], axis=1)
    stacked = stacked.reshape(rows_own, 3, shards, part_width).transpose(2, 0, 1, 3)
    stacked = stacked.reshape(shards, rows_own, 3 * part_width)
    token_blocks = gather_pairs(tokens[0], "shard")
    weight_blocks = [take(stacked, me)]
    for t in range(1, shards):
        weight_blocks.append(swap(take(stacked, partner("shard", t)), "shard", t))
    tokens_all = in_order(token_blocks, "shard").reshape(total_rows, model_width)
    weights = in_order(weight_blocks, "shard").reshape(model_width, 3 * part_width)

    w_attn_out_b, grad_out_b, target_b, _ = lax.optimization_barrier(
        (w_attn_out, grad_out[0], target, weights)
    )
    out_w = gather_pairs(w_attn_out_b, "shard")
    grad_all = in_order(gather_pairs(grad_out_b, "shard"), "shard")
    target_all = in_order(gather_pairs(target_b, "shard"), "shard")

    tokens_all_f = tokens_all.astype(f32)
    normed_all = (tokens_all_f * rms_factor(tokens_all_f) * gain_one).astype(bf16)
    projected = mm(normed_all, weights).astype(bf16)
    queries = projected[:, :part_width]
    keys = projected[:, part_width : 2 * part_width]
    values = projected[:, 2 * part_width :]
    table = lax.dynamic_slice_in_dim(table_full, me * local_heads, local_heads, axis=1)
    table = jnp.pad(table.T, ((0, 8 - local_heads), (0, 0)))
    padded_buckets = jnp.pad(buckets, (0, 2 * total_rows - buckets.shape[0]), constant_values=-1)
    onehot = (padded_buckets[None, :] == jnp.arange(bucket_count)[:, None]).astype(bf16)
    mixed, logs = attention_forward(queries, keys, values, table, onehot)

    mixed_blocks = mixed.reshape(shards, block_rows, part_width)
    mixed_own = [take(mixed_blocks, me)]
    for t in range(1, shards):
        mixed_own.append(swap(take(mixed_blocks, partner("shard", t)), "shard", t))
    tokens_f = tokens[0].astype(f32)
    residual = tokens_f + mm(jnp.concatenate(mixed_own, axis=1), jnp.concatenate(out_w, axis=0))
    normed_two_pre = residual * rms_factor(residual)
    ffn_in = (normed_two_pre * gain_two).astype(bf16)
    router_probs = jax.nn.softmax(mm(ffn_in, router_weight), axis=-1)
    chosen = (expert_ids[0][:, None] == jnp.arange(expert_count)[None, :]).astype(f32)
    gating = jnp.sum(router_probs * chosen, axis=-1, keepdims=True)

    placing = target[None, :] == jnp.arange(slot_count)[:, None]
    placing_low = placing.astype(bf16)
    placing_f = placing.astype(f32)
    grad_y = grad_out[0].astype(f32)
    sent_rows = mm(placing_low, ffn_in).astype(bf16)
    gating_rows = mm_exact(placing_f, gating)
    grad_y_rows = mm(placing_low, grad_out[0])
    sent_grads = (gating_rows * grad_y_rows).astype(bf16)
    sent = jnp.concatenate(
        [
            sent_rows.reshape(expert_count, CAP, model_width),
            sent_grads.reshape(expert_count, CAP, model_width),
        ],
        axis=1,
    )
    sent = jnp.broadcast_to(sent[:, None], (expert_count, shards, 2 * CAP, model_width))
    arrived = lax.all_to_all(
        sent.reshape(expert_count * shards, 2 * CAP, model_width),
        ("expert", "shard"),
        split_axis=0,
        concat_axis=0,
        tiled=True,
    )
    rows_all = arrived[:, :CAP].reshape(-1, model_width)
    grad_rows_all = arrived[:, CAP:].reshape(-1, model_width)
    first_part = w_in[0]
    second_part = w_out[0]
    hidden = mm(rows_all, first_part)
    activation = jax.nn.gelu(hidden).astype(bf16)
    partial_out = mm(activation, second_part).astype(bf16)
    grad_act = mm(grad_rows_all, second_part, NT)
    grad_hidden = gelu_back(hidden, grad_act).astype(bf16)
    grad_partial = mm(grad_hidden, first_part, NT).astype(bf16)
    back = jnp.concatenate(
        [
            partial_out.reshape(-1, CAP, model_width),
            grad_partial.reshape(-1, CAP, model_width),
        ],
        axis=1,
    )
    returned = lax.all_to_all(
        back, ("expert", "shard"), split_axis=0, concat_axis=0, tiled=True
    )
    grad_second = mm(activation, grad_rows_all, TN)
    grad_first = mm(rows_all, grad_hidden, TN)

    kept_all = target_all >= 0
    grad_free = jnp.where(kept_all[..., None], jnp.zeros_like(grad_all), grad_all)
    grad_free = grad_free.reshape(total_rows, model_width)
    mixed_grad_free = mm(grad_free, w_attn_out, NT).astype(bf16)
    placing_all = (
        target_all[:, None, :] == jnp.arange(slot_count)[None, :, None]
    ).astype(bf16)
    mixed_rows = jnp.einsum(
        "bri,bid->brd", placing_all, mixed_blocks, preferred_element_type=f32
    ).astype(bf16)
    residual_rows = mm_exact(placing_f, residual)
    factor_rows = rms_factor(residual_rows)
    normed_rows = residual_rows * factor_rows
    probs_rows = mm_exact(placing_f, router_probs)
    chosen_rows = mm_exact(placing_f, chosen)

    summed = jnp.sum(
        returned.reshape(expert_count, shards, 2 * CAP, model_width).astype(f32), axis=1
    ).astype(bf16)
    out_rows = summed[:, :CAP].reshape(slot_count, model_width)
    grad_back_rows = summed[:, CAP:].reshape(slot_count, model_width).astype(f32)
    output = (residual + gating * mm(placing_low, out_rows, TN)).astype(bf16)
    grad_gate = jnp.sum(grad_y_rows * out_rows.astype(f32), axis=-1, keepdims=True)
    grad_logits = (grad_gate * gating_rows) * (chosen_rows - probs_rows)
    grad_router = mm_exact(sent_rows.astype(f32), grad_logits, TN)
    grad_ffn = grad_back_rows + mm_exact(grad_logits, router_weight.astype(f32), NT)
    grad_gain_two = jnp.sum(grad_ffn * normed_rows, axis=0)
    grad_delta = norm_back(grad_ffn * gain_two, normed_rows, factor_rows)
    att_rows = (grad_y_rows + grad_delta).astype(bf16)
    att_rows_all = in_order(
        [att_rows] + [swap(att_rows, "shard", t) for t in range(1, shards)], "shard"
    )
    mixed_grad_rows = jnp.einsum(
        "brf,cf->brc", att_rows_all, w_attn_out, preferred_element_type=f32
    ).astype(bf16)
    grad_mixed = (
        jnp.einsum("bri,brc->bic", placing_all, mixed_grad_rows, preferred_element_type=f32)
        .astype(bf16)
        .reshape(total_rows, part_width)
        + mixed_grad_free
    )
    grad_out_w = mm(mixed, grad_free, TN) + mm(
        mixed_rows.reshape(-1, part_width), att_rows_all.reshape(-1, model_width), TN
    )

    grad_queries, grad_keys, grad_values, grad_table = attention_backward(
        queries, keys, values, grad_mixed, logs, table, onehot
    )
    grad_projected = jnp.concatenate([grad_queries, grad_keys, grad_values], axis=1)
    grad_weights = mm(normed_all, grad_projected, TN).astype(bf16)

    partial_normed = mm(grad_projected, weights, NT).astype(bf16)
    partial_normed = partial_normed.reshape(shards, block_rows, model_width)
    step = 1
    held = {t: take(partial_normed, partner("shard", t)) for t in range(shards)}
    while len(held) > 1:
        away = [t for t in held if t & step]
        got = swap(jnp.stack([held[t] for t in away]), "shard", step)
        held = {
            t ^ step: (held[t ^ step].astype(f32) + got[i].astype(f32))
            for i, t in enumerate(away)
        }
        if len(held) > 1:
            held = {t: value.astype(bf16) for t, value in held.items()}
        step *= 2
    grad_normed = held[0]
    factor_one = rms_factor(tokens_f)
    grad_residual = grad_y + mm_exact(placing_f, grad_delta, TN)
    grad_tokens = grad_residual + norm_back(grad_normed * gain_one, tokens_f * factor_one, factor_one)

    def total_over_experts(part):
        count, rows, cols = part.shape
        piece = rows // experts
        pieces = part.reshape(count, experts, piece, cols).transpose(1, 0, 2, 3)
        got = lax.all_to_all(
            pieces.reshape(experts, count * piece, cols),
            "expert",
            split_axis=0,
            concat_axis=0,
            tiled=True,
        )
        return jnp.sum(got.astype(f32), axis=0).astype(bf16).reshape(count, piece, cols)

    qkv_sums = total_over_experts(grad_weights.reshape(shards, rows_own, 3 * part_width))
    blocks = [take(qkv_sums, me)]
    for t in range(1, shards):
        blocks.append(swap(take(qkv_sums, partner("shard", t)), "shard", t))
    qkv_mine = in_order(blocks, "shard")
    piece = rows_own // experts
    qkv_mine = (
        qkv_mine.reshape(shards, piece, 3, part_width)
        .transpose(1, 2, 0, 3)
        .reshape(piece, 3 * model_width)
    )
    qkv_total = in_order(gather_pairs(qkv_mine, "expert"), "expert")
    qkv_total = qkv_total.reshape(rows_own, 3, model_width).astype(f32)
    total_query = qkv_total[:, 0]
    total_key = qkv_total[:, 1]
    total_value = qkv_total[:, 2]
    out_sums = total_over_experts(grad_out_w.astype(bf16)[None])
    out_total = in_order(gather_pairs(out_sums[0], "expert"), "expert")
    total_out = out_total.reshape(rows_own, model_width).astype(f32)
    total_one = (
        jnp.sum(
            w_query.astype(f32) * total_query
            + w_key.astype(f32) * total_key
            + w_value.astype(f32) * total_value,
            axis=1,
        )
        / gain_attn.astype(f32)
    )

    router_two = jnp.concatenate([grad_router, grad_gain_two[:, None]], axis=1)
    table_grid = lax.dynamic_update_slice_in_dim(
        jnp.zeros((bucket_count, HEADS), f32),
        grad_table[:local_heads].T,
        me * local_heads,
        axis=1,
    )
    router_two, table_grid = lax.psum((router_two, table_grid), ("expert", "shard"))
    router_two = lax.dynamic_slice_in_dim(router_two, me * rows_own, rows_own, axis=0)
    total_table = lax.dynamic_slice_in_dim(
        table_grid, me * pos_table.shape[0], pos_table.shape[0], axis=0
    )
    return (
        output[None],
        grad_tokens[None],
        total_one,
        total_table,
        total_query,
        total_key,
        total_value,
        total_out,
        router_two[:, :expert_count],
        router_two[:, expert_count],
        grad_first[None],
        grad_second[None],
    )


def solution(mesh):
    in_specs = (
        P("expert", "shard", None),
        P("shard"),
        P("shard", None),
        P(),
        P("shard", None),
        P("shard", None),
        P("shard", None),
        P("shard", None),
        P("shard", None),
        P("shard"),
        P("expert", None, "shard"),
        P("expert", "shard", None),
        P("expert", "shard"),
        P("expert", "shard"),
        P("expert", "shard"),
        P("expert", "shard", None),
    )
    out_specs = (
        P("expert", "shard", None),
        P("expert", "shard", None),
        P("shard"),
        P("shard", None),
        P("shard", None),
        P("shard", None),
        P("shard", None),
        P("shard", None),
        P("shard", None),
        P("shard"),
        P("expert", None, "shard"),
        P("expert", "shard", None),
    )
    return jax.shard_map(
        per_device, mesh=mesh, in_specs=in_specs, out_specs=out_specs, check_vma=False
    )
```

```python
import jax
import jax.numpy as jnp
from jax import lax
from jax.experimental import pallas as pl
from jax.experimental.pallas import tpu as pltpu
from jax.sharding import PartitionSpec as P

HEADS = 12
HEAD_DIM = 64
CAP = 4
PAIR = 2 * CAP
LANES = 128

bf16 = jnp.bfloat16
f32 = jnp.float32
highest = lax.Precision.HIGHEST
epsilon = 1e-06
score_scale = HEAD_DIM ** (-0.5)

NN = (((1,), (0,)), ((), ()))
NT = (((1,), (1,)), ((), ()))
TN = (((0,), (0,)), ((), ()))


def mm(a, b, dims=NN):
    return lax.dot_general(a, b, dims, preferred_element_type=f32)


def mm_exact(a, b, dims=NN):
    return lax.dot_general(a, b, dims, precision=highest, preferred_element_type=f32)


def rms_factor(values):
    return lax.rsqrt(jnp.mean(values * values, axis=-1, keepdims=True) + epsilon)


def norm_back(grad_normed, normed_pre, factor):
    return factor * (
        grad_normed - normed_pre * jnp.mean(grad_normed * normed_pre, axis=-1, keepdims=True)
    )


def gelu_back(hidden, grad_act):
    return jax.vjp(jax.nn.gelu, hidden)[1](grad_act)[0]


def swap(value, axis, bits):
    count = lax.axis_size(axis)
    return lax.ppermute(value, axis, [(i, i ^ bits) for i in range(count)])


def gather_blocks(value, axis):
    held = {0: value}
    step = lax.axis_size(axis) // 2
    while step >= 1:
        for t in list(held):
            held[t ^ step] = swap(held[t], axis, step)
        step //= 2
    return [held[t] for t in range(len(held))]


def exchange(blocks, axis):
    return [blocks[0]] + [swap(blocks[t], axis, t) for t in range(1, len(blocks))]


def stages(count, near_first):
    bits = [b for b in (1 << i for i in range(20)) if b < count][::-1]
    groups = []
    if near_first:
        groups.append([1])
        bits = bits[:-1]
    while bits:
        groups.append(bits[:2])
        bits = bits[2:]
    return groups


def span(bits):
    combos = [0]
    for b in bits[::-1]:
        combos = combos + [c | b for c in combos]
    return combos


def place_of(relative, count, near_first):
    if near_first:
        return (relative & 1) * (count // 2) + (relative >> 1)
    return relative


def sum_pieces(pieces, near_first):
    for group in stages(pieces.shape[0], near_first):
        combos = span(group)
        size = pieces.shape[0] // len(combos)
        kept = pieces[:size]
        got = [
            swap(pieces[j * size : (j + 1) * size].astype(bf16), "expert", m)
            for j, m in enumerate(combos)
            if m
        ]
        for part in got:
            kept = kept + part.astype(f32)
        pieces = kept
    return pieces[0]


def share_piece(piece, near_first):
    count = lax.axis_size("expert")
    if count > 8:
        return [lax.all_gather(piece, "expert", axis=0)]
    held = {0: piece}
    for group in stages(count, near_first)[::-1]:
        combos = span(group)
        for r in list(held):
            for m in combos[1:]:
                held[r ^ m] = swap(held[r], "expert", m)
    return [held[r] for r in range(count)]


VM = pl.BlockSpec(memory_space=pltpu.VMEM)
SM = pl.BlockSpec(memory_space=pltpu.SMEM)


def call(kernel, name, place, args, outs, scratch=(), flops=1e9, transcendentals=0):
    size = sum(a.size * a.dtype.itemsize for a in args)
    size += sum(o.size * o.dtype.itemsize for o in outs)
    return pl.pallas_call(
        kernel,
        out_shape=tuple(outs),
        in_specs=[SM] + [VM] * len(args),
        out_specs=tuple([VM] * len(outs)),
        scratch_shapes=list(scratch),
        compiler_params=pltpu.CompilerParams(vmem_limit_bytes=56 * 2**20),
        cost_estimate=pl.CostEstimate(
            flops=int(flops), bytes_accessed=int(size), transcendentals=int(transcendentals)
        ),
        name=name,
    )(place, *args)


def like(shape, dtype):
    return jax.ShapeDtypeStruct(shape, dtype)


def block_at(index, size):
    return pl.ds(pl.multiple_of(index * size, size), size)


def pack_kernel(place, wq, wk, wv, *outs):
    me = place[0]
    shards = len(outs)
    part = wq.shape[1] // shards
    for t in range(shards):
        for owner in range(shards):

            @pl.when((me ^ t) == owner)
            def _(t=t, owner=owner):
                cols = slice(owner * part, (owner + 1) * part)
                joined = jnp.concatenate(
                    [wq[:, cols].astype(f32), wk[:, cols].astype(f32), wv[:, cols].astype(f32)],
                    axis=1,
                )
                outs[t][...] = joined.astype(bf16)


def bias_rows(offsets_row, count):
    width = offsets_row.shape[1]
    rows = jnp.broadcast_to(offsets_row, (8, width))
    rows = pltpu.roll(rows, width - (count - 1), 1)
    place = lax.broadcasted_iota(jnp.int32, (8, width), 0)
    for bit in (1, 2, 4):
        rows = jnp.where((place & bit) != 0, pltpu.roll(rows, bit, 1), rows)
    while rows.shape[0] < count:
        rows = jnp.concatenate([rows, pltpu.roll(rows, rows.shape[0], 1)], axis=0)
    return rows


def diagonal_row(grid):
    total, width = grid.shape
    count = total
    while count > 8:
        count //= 2
        grid = grid[:count] + pltpu.roll(grid[count:], width - count, 1)
    place = lax.broadcasted_iota(jnp.int32, (8, width), 0)
    for bit in (4, 2, 1):
        grid = jnp.where((place & bit) != 0, pltpu.roll(grid, width - bit, 1), grid)
    return pltpu.roll(jnp.sum(grid, axis=0, keepdims=True), total - 1, 1)


def forward_kernel(shards, experts, local_heads):
    def kernel(place, *refs):
        tok = refs[:shards]
        wts = refs[shards : 2 * shards]
        small = refs[2 * shards : 3 * shards]
        buckets = refs[3 * shards]
        rest = refs[3 * shards + 1 :]
        normed, weights, projected, mixed, logs, gains, router, table, onehot = rest[:9]
        mixes = rest[9 : 9 + shards]
        small_f, heads_f, bias = rest[9 + shards :]
        me = place[0]
        rows_own = wts[0].shape[0]
        block = tok[0].shape[0]
        total = block * shards
        bucket_rows = onehot.shape[0] // shards
        part = local_heads * HEAD_DIM
        for t in range(shards):
            weights[block_at(me ^ t, rows_own), :] = wts[t][...]
            small_f[block_at(me ^ t, rows_own), :] = small[t][:rows_own].astype(f32)
            heads_f[block_at(me ^ t, bucket_rows), :] = small[t][rows_own:].astype(f32)[:bucket_rows]
        router[...] = small_f[...].astype(bf16)
        turned = small_f[...].T
        gains[...] = jnp.concatenate(
            [turned[experts : experts + 2], jnp.zeros((6, turned.shape[1]), f32)], axis=0
        )
        gain = gains[0:1, :]
        for t in range(shards):
            tokens_f = tok[t][...].astype(f32)
            normed[block_at(me ^ t, block), :] = (tokens_f * rms_factor(tokens_f) * gain).astype(bf16)
        projected[...] = mm(normed[...], weights[...]).astype(bf16)
        onehot[...] = (
            lax.broadcasted_iota(jnp.int32, onehot.shape, 0) == buckets[0:1, :]
        ).astype(bf16)
        small_f[:LANES, : onehot.shape[0]] = heads_f[...].T
        table[...] = jnp.zeros_like(table)
        for h in range(local_heads):
            table[h : h + 1, :] = small_f[pl.ds(me * local_heads + h, 1), : onehot.shape[0]]
        offsets = mm(table[...].astype(bf16), onehot[...])
        for h in range(local_heads):
            cols = slice(h * HEAD_DIM, (h + 1) * HEAD_DIM)
            bias[...] = bias_rows(offsets[h : h + 1, :], block)
            keys = projected[:, part + h * HEAD_DIM : part + (h + 1) * HEAD_DIM]
            values = projected[:, 2 * part + h * HEAD_DIM : 2 * part + (h + 1) * HEAD_DIM]
            for t in range(shards):
                rows = block_at(me ^ t, block)
                start = block_at(shards - 1 - (me ^ t), block).start
                scores = mm(projected[rows, cols], keys, NT) * score_scale
                scores = scores + bias[:, pl.ds(pl.multiple_of(start, block), total)]
                peak = jnp.max(scores, axis=-1, keepdims=True)
                raised = jnp.exp(scores - peak)
                norm = jnp.sum(raised, axis=-1, keepdims=True)
                probs_low = (raised * (1.0 / norm)).astype(bf16)
                mix = mm(probs_low, values).astype(bf16)
                mixes[t][:, cols] = mix
                mixed[rows, cols] = mix
                logs[rows, h : h + 1] = peak + jnp.log(norm)

    return kernel


def slot_places(target_row, slot_rows):
    row = lax.broadcasted_iota(jnp.int32, (slot_rows, target_row.shape[1]), 0)
    slot = (row >> 3) * CAP + (row & (CAP - 1))
    return (slot == target_row).astype(f32)


def is_grad_row(shape):
    return (lax.broadcasted_iota(jnp.int32, shape, 0) & CAP) != 0


def route_kernel(shards, experts):
    def kernel(place, *refs):
        mix = refs[:shards]
        outw = refs[shards : 2 * shards]
        tokens, grad_out, gains, router, target, ids = refs[2 * shards : 2 * shards + 6]
        residual, gating, sent, sent_low, grad_y_rows, probs_rows, chosen_rows, residual_rows = refs[
            2 * shards + 6 :
        ]
        value = tokens[...].astype(f32)
        for t in range(shards):
            value = value + mm(mix[t][...], outw[t][...])
        residual[...] = value
        ffn_in = (value * rms_factor(value) * gains[1:2, :]).astype(bf16)
        logits = mm(ffn_in, router[...])
        lane = lax.broadcasted_iota(jnp.int32, logits.shape, 1)
        logits = jnp.where(lane < experts, logits, -1e30)
        raised = jnp.exp(logits - jnp.max(logits, axis=-1, keepdims=True))
        raised = jnp.where(lane < experts, raised, 0.0)
        probs = raised / jnp.sum(raised, axis=-1, keepdims=True)
        chosen = (lane == ids[...]).astype(f32)
        gating[...] = jnp.broadcast_to(
            jnp.sum(probs * chosen, axis=-1, keepdims=True), gating.shape
        )
        slot_rows = experts * PAIR
        places = slot_places(target[...], slot_rows)
        places_low = places.astype(bf16)
        rows = mm(places_low, ffn_in)
        grad_y = mm(places_low, grad_out[...])
        probs_r = mm_exact(places, probs)
        chosen_r = mm(places_low, chosen.astype(bf16))
        gate_r = jnp.sum(probs_r * chosen_r, axis=-1, keepdims=True)
        joined = jnp.where(is_grad_row(rows.shape), gate_r * grad_y, rows)
        for e in range(experts):
            piece = joined[e * PAIR : (e + 1) * PAIR].astype(bf16)
            for t in range(shards):
                sent[e * shards + t] = piece
        sent_low[...] = rows.astype(bf16)
        grad_y_rows[...] = grad_y
        probs_rows[...] = probs_r
        chosen_rows[...] = chosen_r
        residual_rows[...] = mm_exact(places, value)

    return kernel


def expert_kernel(place, arrived, first, second, back, rows_moved, act_moved, grads, grad_hidden):
    blocks = arrived.shape[0]
    width = arrived.shape[2]
    chunk = min(32, blocks)

    def step(c):
        at = pl.ds(c * chunk, chunk)
        flat = pl.ds(pl.multiple_of(c * chunk * PAIR, chunk * PAIR), chunk * PAIR)
        both = arrived[at].astype(f32).reshape(chunk * PAIR, width)
        is_grad = is_grad_row(both.shape)
        both_low = both.astype(bf16)
        hidden = mm(both_low, first[...])
        act = jax.nn.gelu(hidden)
        act_low = act.astype(bf16)
        grad_low = jnp.where(is_grad, both, 0.0).astype(bf16)
        grad_act = mm(grad_low, second[...], NT)
        grad_h = gelu_back(pltpu.roll(hidden, CAP, 0), grad_act)
        grad_h = jnp.where(is_grad, grad_h, 0.0).astype(bf16)
        out = jnp.where(is_grad, mm(grad_h, first[...], NT), mm(act_low, second[...]))
        back[at] = out.reshape(chunk, PAIR, width).astype(bf16)
        rows_moved[flat, :] = pltpu.roll(both, CAP, 0).astype(bf16)
        act_moved[flat, :] = pltpu.roll(act_low.astype(f32), CAP, 0).astype(bf16)
        grads[flat, :] = grad_low
        grad_hidden[flat, :] = grad_h

    if blocks == chunk:
        step(0)
    else:
        pl.loop(0, blocks // chunk)(step)


def expert_grads_kernel(place, rows_moved, act_moved, grads, grad_hidden, grad_first, grad_second):
    grad_first[0] = mm(rows_moved[...], grad_hidden[...], TN)
    grad_second[0] = mm(act_moved[...], grads[...], TN)


def slot_sums(returned, shards, experts):
    width = returned.shape[2]
    value = returned[...].astype(f32).reshape(experts, shards, PAIR, width)
    total = value[:, 0]
    for t in range(1, shards):
        total = total + value[:, t]
    return total.reshape(experts * PAIR, width).astype(bf16)


def slot_back_kernel(shards, experts):
    def kernel(
        place, returned, grad_y_rows, probs_rows, chosen_rows, residual_rows, sent_low, gains, router,
        att_rows, grad_delta, summed, *rest
    ):
        shares, grid = rest[:shards], rest[shards]
        me = place[0]
        total = slot_sums(returned, shards, experts)
        summed[...] = total
        total = total.astype(f32)
        is_grad = is_grad_row(total.shape)
        out_rows = pltpu.roll(total, CAP, 0)
        grad_y = grad_y_rows[...]
        probs = probs_rows[...]
        chosen = chosen_rows[...]
        gate = jnp.sum(probs * chosen, axis=-1, keepdims=True)
        grad_gate = jnp.sum(grad_y * out_rows, axis=-1, keepdims=True)
        grad_logits = grad_gate * gate * (chosen - probs)
        grad_logits = jnp.where(is_grad_row(grad_logits.shape), grad_logits, 0.0)
        grad_ffn = jnp.where(is_grad, total, 0.0) + mm_exact(
            grad_logits, router[...].astype(f32), NT
        )
        values = residual_rows[...]
        factor = rms_factor(values)
        normed = values * factor
        delta = norm_back(grad_ffn * gains[1:2, :], normed, factor)
        delta = jnp.where(is_grad, delta, 0.0)
        grad_delta[...] = delta
        att_rows[...] = jnp.where(is_grad, grad_y + delta, 0.0).astype(bf16)
        lane = lax.broadcasted_iota(jnp.int32, (total.shape[0], LANES), 1)
        one = (lane == experts).astype(f32)
        grid[...] = mm_exact(sent_low[...].astype(f32), grad_logits, TN) + mm_exact(
            grad_ffn * normed, one, TN
        )
        rows = shares[0].shape[0]
        for t in range(shards):
            shares[t][...] = grid[block_at(me ^ t, rows), :]

    return kernel


def token_back_kernel(experts):
    def kernel(
        place, residual, gating, summed, grad_delta, grad_out, target, output, grad_residual
    ):
        places = slot_places(target[...], experts * PAIR)
        is_grad = is_grad_row(places.shape)
        rows = jnp.where(is_grad, 0.0, places).astype(bf16)
        token_out = mm(rows, summed[...], TN)
        output[...] = (residual[...] + gating[:, 0:1] * token_out).astype(bf16)
        grad_residual[...] = grad_out[...].astype(f32) + mm_exact(
            jnp.where(is_grad, places, 0.0), grad_delta[...], TN
        )

    return kernel


def mixed_back_kernel(shards, experts):
    def kernel(place, *refs):
        att = refs[:shards]
        targets = refs[shards : 2 * shards]
        shares = refs[2 * shards : 3 * shards]
        out_w, free, out_free, mixed, grad_mixed, pieces = refs[3 * shards :]
        me, expert = place[0], place[1]
        block = targets[0].shape[1]
        total_out = out_free[...]
        for t in range(shards):
            rows = block_at(me ^ t, block)
            places = slot_places(targets[t][...], experts * PAIR).astype(bf16)
            rows_mixed = mm(att[t][...], out_w[...], NT).astype(bf16)
            placed = mm(places, rows_mixed, TN)
            grad_mixed[rows, :] = (free[rows, :].astype(f32) + placed).astype(bf16)
            mixed_rows = mm(places, mixed[rows, :]).astype(bf16)
            total_out = total_out + mm(mixed_rows, att[t][...], TN)
        router = shares[0][...]
        for t in range(1, shards):
            router = router + shares[t][...]
        count, piece, _ = pieces.shape
        width = total_out.shape[1]
        for p in range(count):
            at = place_of(expert ^ p, count, True)
            rows = slice(p * piece, (p + 1) * piece)
            pieces[at, :, :width] = total_out[rows]
            pieces[at, :, width:] = router[rows]

    return kernel


def backward_kernel(local_heads):
    def kernel(
        place, normed, projected, gm_ref, logs, table, onehot,
        grad_projected, grad_table, near, far, bias, sums, diagonals, grid,
    ):
        me, expert = place[0], place[1]
        total = normed.shape[0]
        block = bias.shape[0]
        blocks = total // block
        part = local_heads * HEAD_DIM
        offsets = mm(table[...].astype(bf16), onehot[...])
        diagonals[...] = jnp.zeros_like(diagonals)
        for h in range(local_heads):
            cols = slice(h * HEAD_DIM, (h + 1) * HEAD_DIM)
            key_cols = slice(part + h * HEAD_DIM, part + (h + 1) * HEAD_DIM)
            value_cols = slice(2 * part + h * HEAD_DIM, 2 * part + (h + 1) * HEAD_DIM)
            bias[...] = bias_rows(offsets[h : h + 1, :], block)
            sums[...] = jnp.zeros_like(sums)
            keys = projected[:, key_cols]
            values = projected[:, value_cols]
            gk = jnp.zeros((HEAD_DIM, total), f32)
            gv = jnp.zeros((HEAD_DIM, total), f32)
            for a in range(blocks):
                rows = slice(a * block, (a + 1) * block)
                start = total - block * (a + 1)
                queries = projected[rows, cols]
                gm = gm_ref[rows, cols]
                scores = mm(queries, keys, NT) * score_scale
                scores = scores + bias[:, start : start + total]
                probs = jnp.exp(scores - logs[rows, h : h + 1])
                grad_probs = mm(gm, values, NT)
                dots = jnp.sum(probs * grad_probs, axis=-1, keepdims=True)
                grad_scores = (probs * (grad_probs - dots)).astype(bf16)
                sums[:, start : start + total] += grad_scores.astype(f32)
                grad_projected[rows, cols] = (mm(grad_scores, keys) * score_scale).astype(bf16)
                gk = gk + mm(queries, grad_scores, TN)
                gv = gv + mm(gm, probs.astype(bf16), TN)
            grad_projected[:, key_cols] = (gk * score_scale).T.astype(bf16)
            grad_projected[:, value_cols] = gv.T.astype(bf16)
            diagonals[h : h + 1, :] = diagonal_row(sums[...])
        grad_table[...] = mm_exact(diagonals[...], onehot[...].astype(f32), NT)
        grid[...] = mm(normed[...], grad_projected[...], TN)
        count, shards, piece, split = near.shape
        for p in range(count):
            at_near = place_of(expert ^ p, count, True)
            at_far = place_of(expert ^ p, count, False)
            for t in range(shards):
                first = (t * count + p) * piece
                near[at_near, me ^ t] = grid[first : first + piece, :split]
                far[at_far, me ^ t] = grid[first : first + piece, split:]

    return kernel


def normed_back_kernel(place, grad_projected, weights, *outs):
    me = place[0]
    block = outs[0].shape[0]
    for t in range(len(outs)):
        outs[t][...] = mm(grad_projected[block_at(me ^ t, block), :], weights[...], NT).astype(bf16)


def finish_kernel(shards, experts, blocks):
    def kernel(place, *refs):
        near = refs[:blocks]
        far = refs[blocks : 2 * blocks]
        outs = refs[2 * blocks : 3 * blocks]
        wq, wk, wv, gain, gq, gk, gv, gout, grouter, ggain = refs[3 * blocks :]
        me, expert = place[0], place[1]
        rows, width = gq.shape
        part = width // shards

        def put(at, near_block, far_block, out_block):
            for t in range(shards):
                cols = slice(t * part, (t + 1) * part)
                first = near_block[me ^ t].astype(f32)
                gq[at, cols] = first[:, :part]
                gk[at, cols] = first[:, part:]
                gv[at, cols] = far_block[me ^ t].astype(f32)
            last = out_block.astype(f32)
            gout[at, :] = last[:, :width]
            grouter[at, :] = last[:, width:]

        if blocks > 1:
            piece = rows // blocks
            for r in range(blocks):
                put(block_at(expert ^ r, piece), near[r], far[r], outs[r][...])
        else:
            count = near[0].shape[0]
            piece = rows // count
            for p in range(count):
                at = slice(p * piece, (p + 1) * piece)
                put(at, near[0].at[p], far[0].at[p], outs[0][p])
        dots = (
            wq[...].astype(f32) * gq[...]
            + wk[...].astype(f32) * gk[...]
            + wv[...].astype(f32) * gv[...]
        )
        ggain[...] = jnp.sum(dots, axis=1, keepdims=True) / gain[...].astype(f32)

    return kernel


def per_device(
    tokens, gain_attn, pos_table, buckets, w_query, w_key, w_value, w_attn_out, w_router, gain_ffn,
    w_in, w_out, expert_ids, slots, keep, grad_out,
):
    shards = lax.axis_size("shard")
    devices = lax.axis_size("expert")
    me = lax.axis_index("shard")
    place = jnp.stack([me, lax.axis_index("expert")]).astype(jnp.int32)
    block, width = tokens.shape[1:]
    total = block * shards
    rows_own = w_query.shape[0]
    local_heads = HEADS // shards
    part = local_heads * HEAD_DIM
    experts = w_router.shape[1]
    slot_rows = experts * PAIR
    bucket_rows = pos_table.shape[0]
    bucket_count = bucket_rows * shards
    piece = rows_own // devices
    own_tokens = tokens[0]
    own_grad = grad_out[0]

    tok = gather_blocks(own_tokens, "shard")
    small = jnp.concatenate([w_router, gain_attn[:, None], gain_ffn[:, None]], axis=1)
    small = jnp.pad(small, ((0, 0), (0, LANES - experts - 2)))
    heads = jnp.pad(pos_table, ((0, 16 - bucket_rows), (0, LANES - HEADS)))
    small = gather_blocks(jnp.concatenate([small, heads], axis=0), "shard")
    wts = call(
        pack_kernel, "pack_columns", place, [w_query, w_key, w_value],
        [like((rows_own, 3 * part), bf16)] * shards, flops=1e6,
    )
    wts = exchange(wts, "shard")

    target = jnp.where(keep > 0, expert_ids * CAP + slots, -1).astype(jnp.int32)
    outw_own, grad_own, target_own, _ = lax.optimization_barrier(
        (w_attn_out, own_grad, target, wts[shards - 1])
    )
    outw = gather_blocks(outw_own, "shard")
    grad_blocks = gather_blocks(grad_own, "shard")
    targets = gather_blocks(target_own, "shard")

    bucket_row = jnp.pad(
        buckets, (0, 2 * total - buckets.shape[0]), constant_values=-1
    ).reshape(1, -1)
    (
        normed, weights, projected, mixed, logs, gains, router, table, onehot, *mixes
    ) = call(
        forward_kernel(shards, experts, local_heads), "attention_forward", place,
        [*tok, *wts, *small, bucket_row],
        [
            like((total, width), bf16),
            like((width, 3 * part), bf16),
            like((total, 3 * part), bf16),
            like((total, part), bf16),
            like((total, 8), f32),
            like((8, width), f32),
            like((width, LANES), bf16),
            like((8, bucket_count), f32),
            like((bucket_count, 2 * total), bf16),
        ]
        + [like((block, part), bf16)] * shards,
        [
            pltpu.VMEM((width, LANES), f32),
            pltpu.VMEM((bucket_count, LANES), f32),
            pltpu.VMEM((block, 2 * total), f32),
        ],
        flops=4 * total * total * part + 6 * total * width * part,
        transcendentals=3 * total * total,
    )

    mixes = exchange(mixes, "shard")
    (
        residual, gating, sent, sent_low, grad_y_rows, probs_rows, chosen_rows, residual_rows
    ) = call(
        route_kernel(shards, experts), "route", place,
        [*mixes, *outw, own_tokens, own_grad, gains, router, target, expert_ids.reshape(block, 1)],
        [
            like((block, width), f32),
            like((block, LANES), f32),
            like((experts * shards, PAIR, width), bf16),
            like((slot_rows, width), bf16),
            like((slot_rows, width), f32),
            like((slot_rows, LANES), f32),
            like((slot_rows, LANES), f32),
            like((slot_rows, width), f32),
        ],
        flops=4 * block * width * width,
    )
    arrived = lax.all_to_all(
        sent, ("expert", "shard"), split_axis=0, concat_axis=0, tiled=True
    )

    kept = jnp.stack(targets) >= 0
    free = jnp.where(kept.reshape(shards, block, 1), jnp.zeros((), bf16), jnp.stack(grad_blocks))
    order = jnp.bitwise_xor(jnp.arange(shards), me)
    free = jnp.stack([lax.dynamic_index_in_dim(free, order[t], 0, False) for t in range(shards)])
    free = free.reshape(total, width)
    mixed_free = mm(free, w_attn_out, NT).astype(bf16)
    out_free = mm(mixed, free, TN)

    all_rows = arrived.shape[0] * PAIR
    hidden_own = w_in.shape[2]
    back, rows_moved, act_moved, grads, grad_hidden = call(
        expert_kernel, "experts", place, [arrived, w_in[0], w_out[0]],
        [
            like(arrived.shape, bf16),
            like((all_rows, width), bf16),
            like((all_rows, hidden_own), bf16),
            like((all_rows, width), bf16),
            like((all_rows, hidden_own), bf16),
        ],
        flops=8 * all_rows * width * hidden_own,
    )
    returned = lax.all_to_all(
        back, ("expert", "shard"), split_axis=0, concat_axis=0, tiled=True
    )
    grad_first, grad_second = call(
        expert_grads_kernel, "expert_weight_grads", place,
        [rows_moved, act_moved, grads, grad_hidden],
        [like((1, width, hidden_own), f32), like((1, hidden_own, width), f32)],
        flops=4 * all_rows * width * hidden_own,
    )

    att_rows, grad_delta, summed, *shares = call(
        slot_back_kernel(shards, experts), "slot_back", place,
        [
            returned, grad_y_rows, probs_rows, chosen_rows, residual_rows, sent_low, gains, router
        ],
        [
            like((slot_rows, width), bf16),
            like((slot_rows, width), f32),
            like((slot_rows, width), bf16),
        ]
        + [like((rows_own, LANES), f32)] * shards,
        [pltpu.VMEM((width, LANES), f32)],
        flops=1e9,
    )
    att = [att_rows] + [swap(att_rows, "shard", t) for t in range(1, shards)]
    shares = exchange(shares, "shard")
    output, grad_residual = call(
        token_back_kernel(experts), "token_back", place,
        [residual, gating, summed, grad_delta, own_grad, target],
        [like((block, width), bf16), like((block, width), f32)],
        flops=1e8,
    )
    grad_mixed, out_pieces = call(
        mixed_back_kernel(shards, experts), "mixed_back", place,
        [*att, *targets, *shares, w_attn_out, mixed_free, out_free, mixed],
        [like((total, part), bf16), like((devices, piece, width + LANES), f32)],
        flops=1e9,
    )
    out_own = sum_pieces(out_pieces, True).astype(bf16)
    out_blocks = share_piece(out_own, True)

    grad_projected, grad_table, near, far = call(
        backward_kernel(local_heads), "attention_backward", place,
        [normed, projected, grad_mixed, logs, table, onehot],
        [
            like((total, 3 * part), bf16),
            like((8, bucket_count), f32),
            like((devices, shards, piece, 2 * part), f32),
            like((devices, shards, piece, part), f32),
        ],
        [
            pltpu.VMEM((block, 2 * total), f32),
            pltpu.VMEM((block, 2 * total), f32),
            pltpu.VMEM((8, 2 * total), f32),
            pltpu.VMEM((width, 3 * part), f32),
        ],
        flops=10 * total * total * part + 6 * total * width * part,
        transcendentals=3 * total * total,
    )

    near = sum_pieces(near, True).astype(bf16)
    far = sum_pieces(far, False).astype(bf16)
    near = jnp.stack(exchange([near[t] for t in range(shards)], "shard"))
    far = jnp.stack(exchange([far[t] for t in range(shards)], "shard"))
    near_blocks = share_piece(near, True)
    far_blocks = share_piece(far, False)

    held = dict(enumerate(call(
        normed_back_kernel, "normed_back", place, [grad_projected, weights],
        [like((block, width), bf16)] * shards, flops=6 * total * width * part,
    )))
    step = 1
    while len(held) > 1:
        held = {
            t: held[t].astype(f32) + swap(held[t ^ step].astype(bf16), "shard", step).astype(f32)
            for t in held
            if not t & step
        }
        step *= 2
    tokens_f = own_tokens.astype(f32)
    factor_one = rms_factor(tokens_f)
    grad_tokens = grad_residual + norm_back(
        held[0] * gains[0:1], tokens_f * factor_one, factor_one
    )

    bit = 1
    while bit < devices:
        grad_table = grad_table + swap(grad_table, "expert", bit)
        bit *= 2
    tables = jnp.stack([grad_table] + [swap(grad_table, "shard", t) for t in range(1, shards)])
    tables = jnp.stack([lax.dynamic_index_in_dim(tables, order[t], 0, False) for t in range(shards)])
    tables = tables[:, :local_heads].reshape(HEADS, bucket_count)
    total_table = lax.dynamic_slice_in_dim(tables, me * bucket_rows, bucket_rows, axis=1).T

    total_query, total_key, total_value, total_out, total_router, total_one = call(
        finish_kernel(shards, experts, len(near_blocks)), "finish", place,
        [
            *near_blocks, *far_blocks, *out_blocks, w_query, w_key, w_value,
            gain_attn.reshape(rows_own, 1),
        ],
        [like((rows_own, width), f32)] * 4
        + [like((rows_own, LANES), f32), like((rows_own, 1), f32)],
        flops=1e7,
    )
    return (
        output[None],
        grad_tokens[None],
        total_one[:, 0],
        total_table,
        total_query,
        total_key,
        total_value,
        total_out,
        total_router[:, :experts],
        total_router[:, experts],
        grad_first,
        grad_second,
    )


def solution(mesh):
    in_specs = (
        P("expert", "shard", None),
        P("shard"),
        P("shard", None),
        P(),
        P("shard", None),
        P("shard", None),
        P("shard", None),
        P("shard", None),
        P("shard", None),
        P("shard"),
        P("expert", None, "shard"),
        P("expert", "shard", None),
        P("expert", "shard"),
        P("expert", "shard"),
        P("expert", "shard"),
        P("expert", "shard", None),
    )
    out_specs = (
        P("expert", "shard", None),
        P("expert", "shard", None),
        P("shard"),
        P("shard", None),
        P("shard", None),
        P("shard", None),
        P("shard", None),
        P("shard", None),
        P("shard", None),
        P("shard"),
        P("expert", None, "shard"),
        P("expert", "shard", None),
    )
    return jax.shard_map(
        per_device, mesh=mesh, in_specs=in_specs, out_specs=out_specs, check_vma=False
    )
```

```python
import jax
import jax.numpy as jnp
from jax import lax
from jax.experimental import pallas as pl
from jax.experimental.pallas import tpu as pltpu
from jax.sharding import PartitionSpec as P

HEADS = 12
HEAD_DIM = 64
CAP = 4
PAIR = 2 * CAP
LANES = 128

bf16 = jnp.bfloat16
f32 = jnp.float32
epsilon = 1e-06
score_scale = HEAD_DIM ** (-0.5)

NN = (((1,), (0,)), ((), ()))
NT = (((1,), (1,)), ((), ()))
TN = (((0,), (0,)), ((), ()))


def mm(a, b, dims=NN):
    return lax.dot_general(a, b, dims, preferred_element_type=f32)


def split(value):
    high = value.astype(bf16)
    rest = value - high.astype(f32)
    middle = rest.astype(bf16)
    return high, middle, (rest - middle.astype(f32)).astype(bf16)


def mm_left(a, b, dims=NN):
    return sum(mm(part, b, dims) for part in split(a))


def mm_right(a, b, dims=NN):
    return sum(mm(a, part, dims) for part in split(b))


def rms_factor(values):
    return lax.rsqrt(jnp.mean(values * values, axis=-1, keepdims=True) + epsilon)


def norm_back(grad_normed, normed_pre, factor):
    return factor * (
        grad_normed - normed_pre * jnp.mean(grad_normed * normed_pre, axis=-1, keepdims=True)
    )


def gelu_back(hidden, grad_act):
    return jax.vjp(jax.nn.gelu, hidden)[1](grad_act)[0]


def swap(value, axis, bits):
    count = lax.axis_size(axis)
    return lax.ppermute(value, axis, [(i, i ^ bits) for i in range(count)])


def gather_blocks(value, axis):
    held = {0: value}
    step = lax.axis_size(axis) // 2
    while step >= 1:
        for t in list(held):
            held[t ^ step] = swap(held[t], axis, step)
        step //= 2
    return [held[t] for t in range(len(held))]


def exchange(blocks, axis):
    return [blocks[0]] + [swap(blocks[t], axis, t) for t in range(1, len(blocks))]


VM = pl.BlockSpec(memory_space=pltpu.VMEM)
SM = pl.BlockSpec(memory_space=pltpu.SMEM)


def call(kernel, name, place, args, outs, scratch=(), flops=1e9, transcendentals=0):
    size = sum(a.size * a.dtype.itemsize for a in args)
    size += sum(o.size * o.dtype.itemsize for o in outs)
    return pl.pallas_call(
        kernel,
        out_shape=tuple(outs),
        in_specs=[SM] + [VM] * len(args),
        out_specs=tuple([VM] * len(outs)),
        scratch_shapes=list(scratch),
        compiler_params=pltpu.CompilerParams(vmem_limit_bytes=56 * 2**20),
        cost_estimate=pl.CostEstimate(
            flops=int(flops), bytes_accessed=int(size), transcendentals=int(transcendentals)
        ),
        name=name,
    )(place, *args)


def like(shape, dtype):
    return jax.ShapeDtypeStruct(shape, dtype)


def block_at(index, size):
    return pl.ds(pl.multiple_of(index * size, size), size)


def pack_kernel(place, wq, wk, wv, small, last, *outs):
    me = place[0]
    shards = len(outs)
    rows, width = wq.shape
    part = width // shards
    for t in range(shards):
        for owner in range(shards):

            @pl.when((me ^ t) == owner)
            def _(t=t, owner=owner):
                cols = slice(owner * part, (owner + 1) * part)
                joined = jnp.concatenate(
                    [wq[:, cols], wk[:, cols], wv[:, cols], small[...]], axis=1
                )
                outs[t][:rows, :] = joined

        outs[t][rows:, :] = last[...]


def bias_rows(offsets_row, count):
    width = offsets_row.shape[1]
    rows = jnp.broadcast_to(offsets_row, (8, width))
    rows = pltpu.roll(rows, width - (count - 1), 1)
    place = lax.broadcasted_iota(jnp.int32, (8, width), 0)
    for bit in (1, 2, 4):
        rows = jnp.where((place & bit) != 0, pltpu.roll(rows, bit, 1), rows)
    while rows.shape[0] < count:
        rows = jnp.concatenate([rows, pltpu.roll(rows, rows.shape[0], 1)], axis=0)
    return rows


def diagonal_row(grid):
    total, width = grid.shape
    count = total
    while count > 8:
        count //= 2
        grid = grid[:count] + pltpu.roll(grid[count:], width - count, 1)
    place = lax.broadcasted_iota(jnp.int32, (8, width), 0)
    for bit in (4, 2, 1):
        grid = jnp.where((place & bit) != 0, pltpu.roll(grid, width - bit, 1), grid)
    return pltpu.roll(jnp.sum(grid, axis=0, keepdims=True), total - 1, 1)


def forward_kernel(shards, experts, local_heads):
    def kernel(place, *refs):
        tok = refs[:shards]
        wts = refs[shards : 2 * shards]
        buckets = refs[2 * shards]
        rest = refs[2 * shards + 1 :]
        (
            normed, weights, projected, mixed, logs, gains, router, table, onehot, targets
        ) = rest[:10]
        mixes = rest[10 : 10 + shards]
        small_f, heads_f, bias = rest[10 + shards :]
        me = place[0]
        block = tok[0].shape[0]
        total = block * shards
        part = local_heads * HEAD_DIM
        rows_own = weights.shape[0] // shards
        used = min(wts[0].shape[1] - 3 * part, LANES)
        bucket_rows = onehot.shape[0] // shards
        small_f[...] = jnp.zeros_like(small_f)
        targets[...] = jnp.zeros_like(targets)
        for t in range(shards):
            weights[block_at(me ^ t, rows_own), :] = wts[t][:rows_own, : 3 * part]
            small_f[block_at(me ^ t, rows_own), :used] = wts[t][
                :rows_own, 3 * part : 3 * part + used
            ].astype(f32)
            last = wts[t][rows_own:, :block].astype(f32)
            heads_f[block_at(me ^ t, bucket_rows), :] = last[:bucket_rows, :LANES]
            targets[t : t + 1, :] = last[bucket_rows : bucket_rows + 1]
        router[...] = small_f[...].astype(bf16)
        turned = small_f[...].T
        gains[...] = jnp.concatenate(
            [turned[experts : experts + 2], jnp.zeros((6, turned.shape[1]), f32)], axis=0
        )
        gain = gains[0:1, :]
        for t in range(shards):
            tokens_f = tok[t][...].astype(f32)
            normed[block_at(me ^ t, block), :] = (tokens_f * rms_factor(tokens_f) * gain).astype(bf16)
        projected[...] = mm(normed[...], weights[...]).astype(bf16)
        onehot[...] = (
            lax.broadcasted_iota(jnp.int32, onehot.shape, 0) == buckets[0:1, :]
        ).astype(bf16)
        small_f[:LANES, : onehot.shape[0]] = heads_f[...].T
        table[...] = jnp.zeros_like(table)
        for h in range(local_heads):
            table[h : h + 1, :] = small_f[pl.ds(me * local_heads + h, 1), : onehot.shape[0]]
        offsets = mm(table[...].astype(bf16), onehot[...])
        for h in range(local_heads):
            cols = slice(h * HEAD_DIM, (h + 1) * HEAD_DIM)
            bias[...] = bias_rows(offsets[h : h + 1, :], block)
            keys = projected[:, part + h * HEAD_DIM : part + (h + 1) * HEAD_DIM]
            values = projected[:, 2 * part + h * HEAD_DIM : 2 * part + (h + 1) * HEAD_DIM]
            for t in range(shards):
                rows = block_at(me ^ t, block)
                start = block_at(shards - 1 - (me ^ t), block).start
                scores = mm(projected[rows, cols], keys, NT) * score_scale
                scores = scores + bias[:, pl.ds(pl.multiple_of(start, block), total)]
                peak = jnp.max(scores, axis=-1, keepdims=True)
                raised = jnp.exp(scores - peak)
                norm = jnp.sum(raised, axis=-1, keepdims=True)
                probs_low = (raised * (1.0 / norm)).astype(bf16)
                mix = mm(probs_low, values).astype(bf16)
                mixes[t][:, cols] = mix
                mixed[rows, cols] = mix
                logs[rows, h : h + 1] = peak + jnp.log(norm)

    return kernel


def slot_places(target_row, slot_rows):
    row = lax.broadcasted_iota(jnp.int32, (slot_rows, target_row.shape[1]), 0)
    slot = (row >> 3) * CAP + (row & (CAP - 1))
    return (slot.astype(f32) == target_row).astype(f32)


def is_grad_row(shape):
    return (lax.broadcasted_iota(jnp.int32, shape, 0) & CAP) != 0


def route_kernel(shards, experts):
    def kernel(place, *refs):
        mix = refs[:shards]
        outw = refs[shards : 2 * shards]
        tokens, grad_out, gains, router, target, ids = refs[2 * shards : 2 * shards + 6]
        residual, gating, sent, sent_low, grad_y_rows, probs_rows, chosen_rows, residual_rows = refs[
            2 * shards + 6 :
        ]
        value = tokens[...].astype(f32)
        for t in range(shards):
            value = value + mm(mix[t][...], outw[t][: mix[t].shape[1], :])
        residual[...] = value
        ffn_in = (value * rms_factor(value) * gains[1:2, :]).astype(bf16)
        logits = mm(ffn_in, router[...])
        lane = lax.broadcasted_iota(jnp.int32, logits.shape, 1)
        logits = jnp.where(lane < experts, logits, -1e30)
        raised = jnp.exp(logits - jnp.max(logits, axis=-1, keepdims=True))
        raised = jnp.where(lane < experts, raised, 0.0)
        probs = raised / jnp.sum(raised, axis=-1, keepdims=True)
        expert = lax.broadcasted_iota(jnp.int32, (LANES, ids.shape[1]), 0)
        chosen = (expert == ids[...]).astype(f32).T
        gating[...] = jnp.broadcast_to(
            jnp.sum(probs * chosen, axis=-1, keepdims=True), gating.shape
        )
        slot_rows = experts * PAIR
        places = slot_places(target[...], slot_rows)
        places_low = places.astype(bf16)
        rows = mm(places_low, ffn_in)
        grad_y = mm(places_low, grad_out[...])
        probs_r = mm_right(places_low, probs)
        chosen_r = mm(places_low, chosen.astype(bf16))
        gate_r = jnp.sum(probs_r * chosen_r, axis=-1, keepdims=True)
        joined = jnp.where(is_grad_row(rows.shape), gate_r * grad_y, rows)
        for e in range(experts):
            piece = joined[e * PAIR : (e + 1) * PAIR].astype(bf16)
            for t in range(shards):
                sent[e * shards + t] = piece
        sent_low[...] = rows.astype(bf16)
        grad_y_rows[...] = grad_y
        probs_rows[...] = probs_r
        chosen_rows[...] = chosen_r
        residual_rows[...] = mm_right(places_low, value)

    return kernel


def expert_kernel(place, arrived, first, second, back, rows_moved, act_moved, grads, grad_hidden):
    blocks = arrived.shape[0]
    width = arrived.shape[2]
    chunk = min(32, blocks)

    def step(c):
        at = pl.ds(c * chunk, chunk)
        flat = pl.ds(pl.multiple_of(c * chunk * PAIR, chunk * PAIR), chunk * PAIR)
        both = arrived[at].astype(f32).reshape(chunk * PAIR, width)
        is_grad = is_grad_row(both.shape)
        both_low = both.astype(bf16)
        hidden = mm(both_low, first[...])
        act = jax.nn.gelu(hidden)
        act_low = act.astype(bf16)
        grad_low = jnp.where(is_grad, both, 0.0).astype(bf16)
        grad_act = mm(grad_low, second[...], NT)
        grad_h = gelu_back(pltpu.roll(hidden, CAP, 0), grad_act)
        grad_h = jnp.where(is_grad, grad_h, 0.0).astype(bf16)
        out = jnp.where(is_grad, mm(grad_h, first[...], NT), mm(act_low, second[...]))
        back[at] = out.reshape(chunk, PAIR, width).astype(bf16)
        rows_moved[flat, :] = pltpu.roll(both, CAP, 0).astype(bf16)
        act_moved[flat, :] = pltpu.roll(act_low.astype(f32), CAP, 0).astype(bf16)
        grads[flat, :] = grad_low
        grad_hidden[flat, :] = grad_h

    if blocks == chunk:
        step(0)
    else:
        pl.loop(0, blocks // chunk)(step)


def expert_grads_kernel(place, rows_moved, act_moved, grads, grad_hidden, grad_first, grad_second):
    grad_first[0] = mm(rows_moved[...], grad_hidden[...], TN)
    grad_second[0] = mm(act_moved[...], grads[...], TN)


def slot_sums(returned, shards, experts):
    width = returned.shape[2]
    value = returned[...].astype(f32).reshape(experts, shards, PAIR, width)
    total = value[:, 0]
    for t in range(1, shards):
        total = total + value[:, t]
    return total.reshape(experts * PAIR, width).astype(bf16)


def slot_back_kernel(shards, experts):
    def kernel(
        place, returned, grad_y_rows, probs_rows, chosen_rows, residual_rows, sent_low, gains, router,
        att_rows, grad_delta, summed, grid
    ):
        total = slot_sums(returned, shards, experts)
        summed[...] = total
        total = total.astype(f32)
        is_grad = is_grad_row(total.shape)
        out_rows = pltpu.roll(total, CAP, 0)
        grad_y = grad_y_rows[...]
        probs = probs_rows[...]
        chosen = chosen_rows[...]
        gate = jnp.sum(probs * chosen, axis=-1, keepdims=True)
        grad_gate = jnp.sum(grad_y * out_rows, axis=-1, keepdims=True)
        grad_logits = grad_gate * gate * (chosen - probs)
        grad_logits = jnp.where(is_grad_row(grad_logits.shape), grad_logits, 0.0)
        grad_ffn = jnp.where(is_grad, total, 0.0) + mm_left(
            grad_logits, router[...], NT
        )
        values = residual_rows[...]
        factor = rms_factor(values)
        normed = values * factor
        delta = norm_back(grad_ffn * gains[1:2, :], normed, factor)
        delta = jnp.where(is_grad, delta, 0.0)
        grad_delta[...] = delta
        att_rows[...] = jnp.where(is_grad, grad_y + delta, 0.0).astype(bf16)
        lane = lax.broadcasted_iota(jnp.int32, (total.shape[0], LANES), 1)
        one = (lane == experts).astype(bf16)
        grid[...] = mm_right(sent_low[...], grad_logits, TN) + mm_left(grad_ffn * normed, one, TN)

    return kernel


def token_back_kernel(experts):
    def kernel(
        place, residual, gating, summed, grad_delta, grad_out, target, output, grad_residual
    ):
        places = slot_places(target[...], experts * PAIR)
        is_grad = is_grad_row(places.shape)
        rows = jnp.where(is_grad, 0.0, places).astype(bf16)
        token_out = mm(rows, summed[...], TN)
        output[...] = (residual[...] + gating[:, 0:1] * token_out).astype(bf16)
        grad_residual[...] = grad_out[...].astype(f32) + mm_right(
            jnp.where(is_grad, places, 0.0).astype(bf16), grad_delta[...], TN
        )

    return kernel


def free_kernel(shards):
    def kernel(place, *refs):
        blocks = refs[:shards]
        targets, out_w, mixed, free, out_free = refs[shards:]
        me = place[0]
        block = targets.shape[1]
        taken = targets[...].T
        total_out = jnp.zeros(out_free.shape, f32)
        for t in range(shards):
            rows = block_at(me ^ t, block)
            grads = blocks[t][out_w.shape[0] :, :]
            grads = jnp.where(taken[:, t : t + 1] >= 0, 0.0, grads.astype(f32)).astype(bf16)
            free[rows, :] = mm(grads, out_w[...], NT).astype(bf16)
            total_out = total_out + mm(mixed[rows, :], grads, TN)
        out_free[...] = total_out

    return kernel


def mixed_back_kernel(shards, experts):
    def kernel(place, *refs):
        att = refs[:shards]
        targets, out_w, free, out_free, mixed, grad_mixed, grad_out_w = refs[shards:]
        me = place[0]
        block = targets.shape[1]
        total_out = out_free[...]
        for t in range(shards):
            rows = block_at(me ^ t, block)
            places = slot_places(targets[t : t + 1, :], experts * PAIR).astype(bf16)
            rows_mixed = mm(att[t][...], out_w[...], NT).astype(bf16)
            placed = mm(places, rows_mixed, TN)
            grad_mixed[rows, :] = (free[rows, :].astype(f32) + placed).astype(bf16)
            mixed_rows = mm(places, mixed[rows, :]).astype(bf16)
            total_out = total_out + mm(mixed_rows, att[t][...], TN)
        grad_out_w[...] = total_out

    return kernel


def backward_kernel(shards, experts, local_heads):
    def kernel(
        place, normed, projected, gm_ref, logs, table, onehot, router_grid,
        grad_projected, pieces, bias, sums, diagonals, grid,
    ):
        total = normed.shape[0]
        block = bias.shape[0]
        blocks = total // block
        part = local_heads * HEAD_DIM
        offsets = mm(table[...].astype(bf16), onehot[...])
        diagonals[...] = jnp.zeros_like(diagonals)
        for h in range(local_heads):
            cols = slice(h * HEAD_DIM, (h + 1) * HEAD_DIM)
            key_cols = slice(part + h * HEAD_DIM, part + (h + 1) * HEAD_DIM)
            value_cols = slice(2 * part + h * HEAD_DIM, 2 * part + (h + 1) * HEAD_DIM)
            bias[...] = bias_rows(offsets[h : h + 1, :], block)
            sums[...] = jnp.zeros_like(sums)
            keys = projected[:, key_cols]
            values = projected[:, value_cols]
            gk = jnp.zeros((HEAD_DIM, total), f32)
            gv = jnp.zeros((HEAD_DIM, total), f32)
            for a in range(blocks):
                rows = slice(a * block, (a + 1) * block)
                start = total - block * (a + 1)
                queries = projected[rows, cols]
                gm = gm_ref[rows, cols]
                scores = mm(queries, keys, NT) * score_scale
                scores = scores + bias[:, start : start + total]
                probs = jnp.exp(scores - logs[rows, h : h + 1])
                grad_probs = mm(gm, values, NT)
                dots = jnp.sum(probs * grad_probs, axis=-1, keepdims=True)
                grad_scores = (probs * (grad_probs - dots)).astype(bf16)
                sums[:, start : start + total] += grad_scores.astype(f32)
                grad_projected[rows, cols] = (mm(grad_scores, keys) * score_scale).astype(bf16)
                gk = gk + mm(queries, grad_scores, TN)
                gv = gv + mm(gm, probs.astype(bf16), TN)
            grad_projected[:, key_cols] = (gk * score_scale).T.astype(bf16)
            grad_projected[:, value_cols] = gv.T.astype(bf16)
            diagonals[h : h + 1, :] = diagonal_row(sums[...])
        low_onehot = onehot[...]
        grad_table = mm_left(diagonals[...], low_onehot, NT)
        width = 3 * part
        bucket_rows = low_onehot.shape[0] // shards
        used = local_heads * bucket_rows
        rows_own = grid.shape[0] // shards
        count, piece, _ = pieces.shape
        count = count // shards
        grid[:, :width] = mm(normed[...], grad_projected[...], TN)
        grid[:, width:] = jnp.zeros((grid.shape[0], grid.shape[1] - width), f32)
        grid[:, width + used : width + used + experts + 1] = router_grid[:, : experts + 1]
        for t in range(shards):
            row = jnp.concatenate(
                [
                    grad_table[h : h + 1, t * bucket_rows : (t + 1) * bucket_rows]
                    for h in range(local_heads)
                ],
                axis=1,
            )
            for p in range(count):
                at = t * rows_own + p * piece
                grid[at : at + 1, width : width + used] = row
        for p in range(count):
            for t in range(shards):
                at = t * rows_own + p * piece
                pieces[p * shards + t] = grid[at : at + piece, :].astype(bf16)

    return kernel


def normed_back_kernel(place, grad_projected, weights, *outs):
    me = place[0]
    block = outs[0].shape[0]
    for t in range(len(outs)):
        outs[t][...] = mm(grad_projected[block_at(me ^ t, block), :], weights[...], NT).astype(bf16)


def sums_kernel(shards, experts, part, used):
    def kernel(place, got, total, tables):
        count = got.shape[0] // shards
        width = 3 * part
        tables[...] = jnp.zeros_like(tables)
        router = None
        for t in range(shards):
            value = got[t].astype(f32)
            for p in range(1, count):
                value = value + got[p * shards + t].astype(f32)
            total[:, t * width : (t + 1) * width] = value[:, :width].astype(bf16)
            tables[t : t + 1, :used] = value[0:1, width : width + used]
            share = value[:, width + used : width + used + experts + 1]
            router = share if router is None else router + share
        total[:, shards * width :] = jnp.zeros((total.shape[0], LANES), bf16)
        total[:, shards * width : shards * width + experts + 1] = router.astype(bf16)

    return kernel


def finish_kernel(shards, experts):
    def kernel(place, total, wq, wk, wv, gain, gq, gk, gv, grouter, gtwo, gone):
        part = wq.shape[1] // shards
        for t in range(shards):
            cols = slice(t * part, (t + 1) * part)
            at = 3 * part * t
            gq[:, cols] = total[:, at : at + part].astype(f32)
            gk[:, cols] = total[:, at + part : at + 2 * part].astype(f32)
            gv[:, cols] = total[:, at + 2 * part : at + 3 * part].astype(f32)
        turned = total[:, 3 * part * shards :].astype(f32).T
        grouter[...] = turned[:experts]
        gtwo[...] = turned[experts : experts + 1]
        dots = (
            wq[...].astype(f32) * gq[...]
            + wk[...].astype(f32) * gk[...]
            + wv[...].astype(f32) * gv[...]
        )
        ones = jnp.ones((8, dots.shape[1]), bf16)
        gone[...] = mm_right(ones, dots, NT)[0:1] / gain[...].astype(f32)

    return kernel


def per_device(
    tokens, gain_attn, pos_table, buckets, w_query, w_key, w_value, w_attn_out, w_router, gain_ffn,
    w_in, w_out, expert_ids, slots, keep, grad_out,
):
    shards = lax.axis_size("shard")
    devices = lax.axis_size("expert")
    me = lax.axis_index("shard")
    place = jnp.stack([me, lax.axis_index("expert")]).astype(jnp.int32)
    block, width = tokens.shape[1:]
    total = block * shards
    rows_own = w_query.shape[0]
    local_heads = HEADS // shards
    part = local_heads * HEAD_DIM
    experts = w_router.shape[1]
    slot_rows = experts * PAIR
    bucket_rows = pos_table.shape[0]
    bucket_count = bucket_rows * shards
    piece = rows_own // devices
    own_tokens = tokens[0]
    own_grad = grad_out[0]

    tok = gather_blocks(own_tokens, "shard")
    target = jnp.where(keep > 0, expert_ids * CAP + slots, -1).astype(f32)
    extra = experts + 2
    extra += -(3 * part + extra) % LANES
    packed_width = 3 * part + extra
    small = jnp.concatenate([w_router, gain_attn[:, None], gain_ffn[:, None]], axis=1)
    small = jnp.pad(small, ((0, 0), (0, extra - experts - 2)))
    last = jnp.concatenate(
        [
            jnp.pad(pos_table, ((0, 0), (0, packed_width - HEADS))),
            jnp.pad(target.astype(bf16), ((0, 15 - bucket_rows), (0, packed_width - block))),
        ],
        axis=0,
    )
    wts = call(
        pack_kernel, "pack_columns", place, [w_query, w_key, w_value, small, last],
        [like((rows_own + 16, packed_width), bf16)] * shards, flops=1e6,
    )
    wts = exchange(wts, "shard")

    later = jnp.concatenate([w_attn_out, own_grad], axis=0)
    later, _ = lax.optimization_barrier((later, wts[shards - 1]))
    later = gather_blocks(later, "shard")

    bucket_row = jnp.pad(
        buckets, (0, 2 * total - buckets.shape[0]), constant_values=-1
    ).reshape(1, -1)
    (
        normed, weights, projected, mixed, logs, gains, router, table, onehot, targets, *mixes
    ) = call(
        forward_kernel(shards, experts, local_heads), "attention_forward", place,
        [*tok, *wts, bucket_row],
        [
            like((total, width), bf16),
            like((width, 3 * part), bf16),
            like((total, 3 * part), bf16),
            like((total, part), bf16),
            like((total, 8), f32),
            like((8, width), f32),
            like((width, LANES), bf16),
            like((8, bucket_count), f32),
            like((bucket_count, 2 * total), bf16),
            like((8, block), f32),
        ]
        + [like((block, part), bf16)] * shards,
        [
            pltpu.VMEM((width, LANES), f32),
            pltpu.VMEM((bucket_count, LANES), f32),
            pltpu.VMEM((block, 2 * total), f32),
        ],
        flops=4 * total * total * part + 6 * total * width * part,
        transcendentals=3 * total * total,
    )

    mixes = exchange(mixes, "shard")
    (
        residual, gating, sent, sent_low, grad_y_rows, probs_rows, chosen_rows, residual_rows
    ) = call(
        route_kernel(shards, experts), "route", place,
        [*mixes, *later, own_tokens, own_grad, gains, router, target, expert_ids],
        [
            like((block, width), f32),
            like((block, LANES), f32),
            like((experts * shards, PAIR, width), bf16),
            like((slot_rows, width), bf16),
            like((slot_rows, width), f32),
            like((slot_rows, LANES), f32),
            like((slot_rows, LANES), f32),
            like((slot_rows, width), f32),
        ],
        flops=4 * block * width * width,
    )
    arrived = lax.all_to_all(
        sent, ("expert", "shard"), split_axis=0, concat_axis=0, tiled=True
    )

    mixed_free, out_free = call(
        free_kernel(shards), "free_tokens", place, [*later, targets, w_attn_out, mixed],
        [like((total, part), bf16), like((part, width), f32)],
        flops=4 * total * width * part,
    )

    all_rows = arrived.shape[0] * PAIR
    hidden_own = w_in.shape[2]
    back, rows_moved, act_moved, grads, grad_hidden = call(
        expert_kernel, "experts", place, [arrived, w_in[0], w_out[0]],
        [
            like(arrived.shape, bf16),
            like((all_rows, width), bf16),
            like((all_rows, hidden_own), bf16),
            like((all_rows, width), bf16),
            like((all_rows, hidden_own), bf16),
        ],
        flops=8 * all_rows * width * hidden_own,
    )
    returned = lax.all_to_all(
        back, ("expert", "shard"), split_axis=0, concat_axis=0, tiled=True
    )
    grad_first, grad_second = call(
        expert_grads_kernel, "expert_weight_grads", place,
        [rows_moved, act_moved, grads, grad_hidden],
        [like((1, width, hidden_own), f32), like((1, hidden_own, width), f32)],
        flops=4 * all_rows * width * hidden_own,
    )

    att_rows, grad_delta, summed, router_grid = call(
        slot_back_kernel(shards, experts), "slot_back", place,
        [
            returned, grad_y_rows, probs_rows, chosen_rows, residual_rows, sent_low, gains, router
        ],
        [
            like((slot_rows, width), bf16),
            like((slot_rows, width), f32),
            like((slot_rows, width), bf16),
            like((width, LANES), f32),
        ],
        flops=1e9,
    )
    att = [att_rows] + [swap(att_rows, "shard", t) for t in range(1, shards)]
    output, grad_residual = call(
        token_back_kernel(experts), "token_back", place,
        [residual, gating, summed, grad_delta, own_grad, target],
        [like((block, width), bf16), like((block, width), f32)],
        flops=1e8,
    )
    grad_mixed, grad_out_w = call(
        mixed_back_kernel(shards, experts), "mixed_back", place,
        [*att, targets, w_attn_out, mixed_free, out_free, mixed],
        [like((total, part), bf16), like((part, width), f32)],
        flops=1e9,
    )
    out_own = lax.psum_scatter(grad_out_w, "expert", scatter_dimension=0, tiled=True)
    total_out = lax.all_gather(out_own.astype(bf16), "expert", axis=0, tiled=True).astype(f32)

    used = local_heads * bucket_rows
    piece_width = 3 * part + used + experts + 1
    piece_width += -piece_width % LANES
    grad_projected, pieces = call(
        backward_kernel(shards, experts, local_heads), "attention_backward", place,
        [normed, projected, grad_mixed, logs, table, onehot, router_grid],
        [
            like((total, 3 * part), bf16),
            like((devices * shards, piece, piece_width), bf16),
        ],
        [
            pltpu.VMEM((block, 2 * total), f32),
            pltpu.VMEM((block, 2 * total), f32),
            pltpu.VMEM((8, 2 * total), f32),
            pltpu.VMEM((width, piece_width), f32),
        ],
        flops=10 * total * total * part + 6 * total * width * part,
        transcendentals=3 * total * total,
    )

    got = lax.all_to_all(
        pieces, ("expert", "shard"), split_axis=0, concat_axis=0, tiled=True
    )
    piece_total, tables = call(
        sums_kernel(shards, experts, part, used), "sums", place, [got],
        [
            like((piece, 3 * width + LANES), bf16),
            like((8, LANES), f32),
        ],
        flops=1e7,
    )
    all_total = lax.all_gather(piece_total, "expert", axis=0, tiled=True)

    held = dict(enumerate(call(
        normed_back_kernel, "normed_back", place, [grad_projected, weights],
        [like((block, width), bf16)] * shards, flops=6 * total * width * part,
    )))
    step = 1
    while len(held) > 1:
        held = {
            t: held[t].astype(f32) + swap(held[t ^ step].astype(bf16), "shard", step).astype(f32)
            for t in held
            if not t & step
        }
        step *= 2
    tokens_f = own_tokens.astype(f32)
    factor_one = rms_factor(tokens_f)
    grad_tokens = grad_residual + norm_back(
        held[0] * gains[0:1], tokens_f * factor_one, factor_one
    )

    total_table = tables[:shards, :used].reshape(shards, local_heads, bucket_rows)
    total_table = total_table.transpose(2, 0, 1).reshape(bucket_rows, HEADS)
    total_query, total_key, total_value, total_router, total_two, total_one = call(
        finish_kernel(shards, experts), "finish", place,
        [all_total, w_query, w_key, w_value, gain_attn.reshape(1, rows_own)],
        [like((rows_own, width), f32)] * 3
        + [like((experts, rows_own), f32)]
        + [like((1, rows_own), f32)] * 2,
        flops=1e7,
    )
    return (
        output[None],
        grad_tokens[None],
        total_one[0],
        total_table,
        total_query,
        total_key,
        total_value,
        total_out,
        total_router.T,
        total_two[0],
        grad_first,
        grad_second,
    )


def solution(mesh):
    in_specs = (
        P("expert", "shard", None),
        P("shard"),
        P("shard", None),
        P(),
        P("shard", None),
        P("shard", None),
        P("shard", None),
        P("shard", None),
        P("shard", None),
        P("shard"),
        P("expert", None, "shard"),
        P("expert", "shard", None),
        P("expert", "shard"),
        P("expert", "shard"),
        P("expert", "shard"),
        P("expert", "shard", None),
    )
    out_specs = (
        P("expert", "shard", None),
        P("expert", "shard", None),
        P("shard"),
        P("shard", None),
        P("shard", None),
        P("shard", None),
        P("shard", None),
        P("shard", None),
        P("shard", None),
        P("shard"),
        P("expert", None, "shard"),
        P("expert", "shard", None),
    )
    return jax.shard_map(
        per_device, mesh=mesh, in_specs=in_specs, out_specs=out_specs, check_vma=False
    )
```

```python
import jax
import jax.numpy as jnp
from jax import lax
from jax.experimental import pallas as pl
from jax.experimental.pallas import tpu as pltpu
from jax.sharding import PartitionSpec as P

HEADS = 12
HEAD_DIM = 64
CAP = 4
PAIR = 2 * CAP
LANES = 128

bf16 = jnp.bfloat16
f32 = jnp.float32
epsilon = 1e-06
score_scale = HEAD_DIM ** (-0.5)

NN = (((1,), (0,)), ((), ()))
NT = (((1,), (1,)), ((), ()))
TN = (((0,), (0,)), ((), ()))


def mm(a, b, dims=NN):
    return lax.dot_general(a, b, dims, preferred_element_type=f32)


def split(value):
    high = value.astype(bf16)
    rest = value - high.astype(f32)
    middle = rest.astype(bf16)
    return high, middle, (rest - middle.astype(f32)).astype(bf16)


def mm_left(a, b, dims=NN):
    return sum(mm(part, b, dims) for part in split(a))


def mm_right(a, b, dims=NN):
    return sum(mm(a, part, dims) for part in split(b))


def rms_factor(values):
    return lax.rsqrt(jnp.mean(values * values, axis=-1, keepdims=True) + epsilon)


def norm_back(grad_normed, normed_pre, factor):
    return factor * (
        grad_normed - normed_pre * jnp.mean(grad_normed * normed_pre, axis=-1, keepdims=True)
    )


def gelu_back(hidden, grad_act):
    return jax.vjp(jax.nn.gelu, hidden)[1](grad_act)[0]


def swap(value, axis, bits):
    count = lax.axis_size(axis)
    return lax.ppermute(value, axis, [(i, i ^ bits) for i in range(count)])


def gather_blocks(value, axis):
    held = {0: value}
    step = lax.axis_size(axis) // 2
    while step >= 1:
        for t in list(held):
            held[t ^ step] = swap(held[t], axis, step)
        step //= 2
    return [held[t] for t in range(len(held))]


def exchange(blocks, axis):
    return [blocks[0]] + [swap(blocks[t], axis, t) for t in range(1, len(blocks))]


def share_piece(piece):
    count = lax.axis_size("expert")
    if count != 8:
        return [lax.all_gather(piece, "expert", axis=0)]
    held = {0: piece}
    for t in (4, 2, 6):
        held[t] = swap(piece, "expert", t)
    for t in (0, 4, 2, 6):
        held[t ^ 1] = swap(held[t], "expert", 1)
    return [held[t] for t in range(count)]


VM = pl.BlockSpec(memory_space=pltpu.VMEM)
SM = pl.BlockSpec(memory_space=pltpu.SMEM)


def call(kernel, name, place, args, outs, scratch=(), flops=1e9, transcendentals=0):
    size = sum(a.size * a.dtype.itemsize for a in args)
    size += sum(o.size * o.dtype.itemsize for o in outs)
    return pl.pallas_call(
        kernel,
        out_shape=tuple(outs),
        in_specs=[SM] + [VM] * len(args),
        out_specs=tuple([VM] * len(outs)),
        scratch_shapes=list(scratch),
        compiler_params=pltpu.CompilerParams(vmem_limit_bytes=56 * 2**20),
        cost_estimate=pl.CostEstimate(
            flops=int(flops), bytes_accessed=int(size), transcendentals=int(transcendentals)
        ),
        name=name,
    )(place, *args)


def like(shape, dtype):
    return jax.ShapeDtypeStruct(shape, dtype)


def block_at(index, size):
    return pl.ds(pl.multiple_of(index * size, size), size)


def pack_kernel(place, wq, wk, wv, small, last, *outs):
    me = place[0]
    shards = len(outs)
    rows, width = wq.shape
    part = width // shards
    for t in range(shards):
        for owner in range(shards):

            @pl.when((me ^ t) == owner)
            def _(t=t, owner=owner):
                cols = slice(owner * part, (owner + 1) * part)
                joined = jnp.concatenate(
                    [wq[:, cols], wk[:, cols], wv[:, cols], small[...]], axis=1
                )
                outs[t][:rows, :] = joined

        outs[t][rows:, :] = last[...]


def bias_rows(offsets_row, count):
    width = offsets_row.shape[1]
    rows = jnp.broadcast_to(offsets_row, (8, width))
    rows = pltpu.roll(rows, width - (count - 1), 1)
    place = lax.broadcasted_iota(jnp.int32, (8, width), 0)
    for bit in (1, 2, 4):
        rows = jnp.where((place & bit) != 0, pltpu.roll(rows, bit, 1), rows)
    while rows.shape[0] < count:
        rows = jnp.concatenate([rows, pltpu.roll(rows, rows.shape[0], 1)], axis=0)
    return rows


def diagonal_row(grid):
    total, width = grid.shape
    count = total
    while count > 8:
        count //= 2
        grid = grid[:count] + pltpu.roll(grid[count:], width - count, 1)
    place = lax.broadcasted_iota(jnp.int32, (8, width), 0)
    for bit in (4, 2, 1):
        grid = jnp.where((place & bit) != 0, pltpu.roll(grid, width - bit, 1), grid)
    return pltpu.roll(jnp.sum(grid, axis=0, keepdims=True), total - 1, 1)


def forward_kernel(shards, experts, local_heads):
    def kernel(place, *refs):
        tok = refs[:shards]
        wts = refs[shards : 2 * shards]
        buckets = refs[2 * shards]
        rest = refs[2 * shards + 1 :]
        (
            normed, weights, projected, mixed, logs, gains, router, table, onehot, targets
        ) = rest[:10]
        mixes = rest[10 : 10 + shards]
        small_f, heads_f, bias = rest[10 + shards :]
        me = place[0]
        block = tok[0].shape[0]
        total = block * shards
        part = local_heads * HEAD_DIM
        rows_own = weights.shape[0] // shards
        used = min(wts[0].shape[1] - 3 * part, LANES)
        bucket_rows = onehot.shape[0] // shards
        small_f[...] = jnp.zeros_like(small_f)
        targets[...] = jnp.zeros_like(targets)
        for t in range(shards):
            weights[block_at(me ^ t, rows_own), :] = wts[t][:rows_own, : 3 * part]
            small_f[block_at(me ^ t, rows_own), :used] = wts[t][
                :rows_own, 3 * part : 3 * part + used
            ].astype(f32)
            last = wts[t][rows_own:, :block].astype(f32)
            heads_f[block_at(me ^ t, bucket_rows), :] = last[:bucket_rows, :LANES]
            targets[t : t + 1, :] = last[bucket_rows : bucket_rows + 1]
        router[...] = small_f[...].astype(bf16)
        turned = small_f[...].T
        gains[...] = jnp.concatenate(
            [turned[experts : experts + 2], jnp.zeros((6, turned.shape[1]), f32)], axis=0
        )
        gain = gains[0:1, :]
        for t in range(shards):
            tokens_f = tok[t][...].astype(f32)
            normed[block_at(me ^ t, block), :] = (tokens_f * rms_factor(tokens_f) * gain).astype(bf16)
        projected[...] = mm(normed[...], weights[...]).astype(bf16)
        onehot[...] = (
            lax.broadcasted_iota(jnp.int32, onehot.shape, 0) == buckets[0:1, :]
        ).astype(bf16)
        small_f[:LANES, : onehot.shape[0]] = heads_f[...].T
        table[...] = jnp.zeros_like(table)
        for h in range(local_heads):
            table[h : h + 1, :] = small_f[pl.ds(me * local_heads + h, 1), : onehot.shape[0]]
        offsets = mm(table[...].astype(bf16), onehot[...])
        for h in range(local_heads):
            cols = slice(h * HEAD_DIM, (h + 1) * HEAD_DIM)
            bias[...] = bias_rows(offsets[h : h + 1, :], block)
            keys = projected[:, part + h * HEAD_DIM : part + (h + 1) * HEAD_DIM]
            values = projected[:, 2 * part + h * HEAD_DIM : 2 * part + (h + 1) * HEAD_DIM]

            def step(a, carry, cols=cols, keys=keys, values=values, h=h):
                rows = block_at(a, block)
                scores = mm(projected[rows, cols], keys, NT) * score_scale
                scores = scores + bias[:, pl.ds(pl.multiple_of((shards - 1 - a) * block, block), total)]
                peak = jnp.max(scores, axis=-1, keepdims=True)
                raised = jnp.exp(scores - peak)
                norm = jnp.sum(raised, axis=-1, keepdims=True)
                probs_low = (raised * (1.0 / norm)).astype(bf16)
                mixed[rows, cols] = mm(probs_low, values).astype(bf16)
                logs[rows, h : h + 1] = peak + jnp.log(norm)
                return carry

            lax.fori_loop(0, shards, step, 0)
        for t in range(shards):
            mixes[t][...] = mixed[block_at(me ^ t, block), :]

    return kernel


def slot_places(target_row, slot_rows):
    row = lax.broadcasted_iota(jnp.int32, (slot_rows, target_row.shape[1]), 0)
    slot = (row >> 3) * CAP + (row & (CAP - 1))
    return (slot.astype(f32) == target_row).astype(f32)


def kept_places(target_row, slots):
    row = lax.broadcasted_iota(jnp.int32, (slots, target_row.shape[1]), 0)
    return (row.astype(f32) == target_row).astype(bf16)


def is_grad_row(shape):
    return (lax.broadcasted_iota(jnp.int32, shape, 0) & CAP) != 0


def route_kernel(shards, experts):
    def kernel(place, *refs):
        mix = refs[:shards]
        outw = refs[shards : 2 * shards]
        tokens, grad_out, gains, router, target, ids = refs[2 * shards : 2 * shards + 6]
        residual, gating, sent, sent_low, grad_y_rows, probs_rows, chosen_rows, residual_rows = refs[
            2 * shards + 6 :
        ]
        value = tokens[...].astype(f32)
        for t in range(shards):
            value = value + mm(mix[t][...], outw[t][: mix[t].shape[1], :])
        residual[...] = value
        ffn_in = (value * rms_factor(value) * gains[1:2, :]).astype(bf16)
        logits = mm(ffn_in, router[...])
        lane = lax.broadcasted_iota(jnp.int32, logits.shape, 1)
        logits = jnp.where(lane < experts, logits, -1e30)
        raised = jnp.exp(logits - jnp.max(logits, axis=-1, keepdims=True))
        raised = jnp.where(lane < experts, raised, 0.0)
        probs = raised / jnp.sum(raised, axis=-1, keepdims=True)
        expert = lax.broadcasted_iota(jnp.int32, (LANES, ids.shape[1]), 0)
        chosen = (expert == ids[...]).astype(f32).T
        gating[...] = jnp.broadcast_to(
            jnp.sum(probs * chosen, axis=-1, keepdims=True), gating.shape
        )
        slot_rows = experts * PAIR
        places = slot_places(target[...], slot_rows)
        places_low = places.astype(bf16)
        rows = mm(places_low, ffn_in)
        grad_y = mm(places_low, grad_out[...])
        probs_r = mm_right(places_low, probs)
        chosen_r = mm(places_low, chosen.astype(bf16))
        gate_r = jnp.sum(probs_r * chosen_r, axis=-1, keepdims=True)
        joined = jnp.where(is_grad_row(rows.shape), gate_r * grad_y, rows)
        for e in range(experts):
            piece = joined[e * PAIR : (e + 1) * PAIR].astype(bf16)
            for t in range(shards):
                sent[e * shards + t] = piece
        sent_low[...] = rows.astype(bf16)
        grad_y_rows[...] = grad_y
        probs_rows[...] = probs_r
        chosen_rows[...] = chosen_r
        residual_rows[...] = mm_right(places_low, value)

    return kernel


def expert_kernel(place, arrived, first, second, back, rows_moved, act_moved, grads, grad_hidden):
    blocks = arrived.shape[0]
    width = arrived.shape[2]
    chunk = min(32, blocks)

    def step(c):
        at = pl.ds(c * chunk, chunk)
        flat = pl.ds(pl.multiple_of(c * chunk * PAIR, chunk * PAIR), chunk * PAIR)
        both = arrived[at].astype(f32).reshape(chunk * PAIR, width)
        is_grad = is_grad_row(both.shape)
        both_low = both.astype(bf16)
        hidden = mm(both_low, first[...])
        act = jax.nn.gelu(hidden)
        act_low = act.astype(bf16)
        grad_low = jnp.where(is_grad, both, 0.0).astype(bf16)
        grad_act = mm(grad_low, second[...], NT)
        grad_h = gelu_back(pltpu.roll(hidden, CAP, 0), grad_act)
        grad_h = jnp.where(is_grad, grad_h, 0.0).astype(bf16)
        out = jnp.where(is_grad, mm(grad_h, first[...], NT), mm(act_low, second[...]))
        back[at] = out.reshape(chunk, PAIR, width).astype(bf16)
        rows_moved[flat, :] = pltpu.roll(both, CAP, 0).astype(bf16)
        act_moved[flat, :] = pltpu.roll(act_low.astype(f32), CAP, 0).astype(bf16)
        grads[flat, :] = grad_low
        grad_hidden[flat, :] = grad_h

    if blocks == chunk:
        step(0)
    else:
        pl.loop(0, blocks // chunk)(step)


def expert_grads_kernel(place, rows_moved, act_moved, grads, grad_hidden, grad_first, grad_second):
    grad_first[0] = mm(rows_moved[...], grad_hidden[...], TN)
    grad_second[0] = mm(act_moved[...], grads[...], TN)


def slot_sums(returned, shards, experts):
    width = returned.shape[2]
    value = returned[...].astype(f32).reshape(experts, shards, PAIR, width)
    total = value[:, 0]
    for t in range(1, shards):
        total = total + value[:, t]
    return total.reshape(experts * PAIR, width).astype(bf16)


def slot_back_kernel(shards, experts):
    def kernel(
        place, returned, grad_y_rows, probs_rows, chosen_rows, residual_rows, sent_low, gains, router,
        att_rows, grad_delta, summed, grid
    ):
        total = slot_sums(returned, shards, experts)
        summed[...] = total
        total = total.astype(f32)
        is_grad = is_grad_row(total.shape)
        out_rows = pltpu.roll(total, CAP, 0)
        grad_y = grad_y_rows[...]
        probs = probs_rows[...]
        chosen = chosen_rows[...]
        gate = jnp.sum(probs * chosen, axis=-1, keepdims=True)
        grad_gate = jnp.sum(grad_y * out_rows, axis=-1, keepdims=True)
        grad_logits = grad_gate * gate * (chosen - probs)
        grad_logits = jnp.where(is_grad_row(grad_logits.shape), grad_logits, 0.0)
        grad_ffn = jnp.where(is_grad, total, 0.0) + mm_left(
            grad_logits, router[...], NT
        )
        values = residual_rows[...]
        factor = rms_factor(values)
        normed = values * factor
        delta = norm_back(grad_ffn * gains[1:2, :], normed, factor)
        delta = jnp.where(is_grad, delta, 0.0)
        grad_delta[...] = delta
        att = jnp.where(is_grad, grad_y + delta, 0.0).astype(bf16)
        slot = lax.broadcasted_iota(jnp.int32, (att_rows.shape[0], total.shape[0]), 0)
        row = lax.broadcasted_iota(jnp.int32, (att_rows.shape[0], total.shape[0]), 1)
        pick = row == ((slot >> 2) * PAIR + CAP + (slot & (CAP - 1)))
        att_rows[...] = mm(pick.astype(f32).astype(bf16), att).astype(bf16)
        lane = lax.broadcasted_iota(jnp.int32, (total.shape[0], LANES), 1)
        one = (lane == experts).astype(bf16)
        grid[...] = mm_right(sent_low[...], grad_logits, TN) + mm_left(grad_ffn * normed, one, TN)

    return kernel


def token_back_kernel(experts):
    def kernel(
        place, residual, gating, summed, grad_delta, grad_out, target, output, grad_residual
    ):
        places = slot_places(target[...], experts * PAIR)
        is_grad = is_grad_row(places.shape)
        rows = jnp.where(is_grad, 0.0, places).astype(bf16)
        token_out = mm(rows, summed[...], TN)
        output[...] = (residual[...] + gating[:, 0:1] * token_out).astype(bf16)
        grad_residual[...] = grad_out[...].astype(f32) + mm_right(
            jnp.where(is_grad, places, 0.0).astype(bf16), grad_delta[...], TN
        )

    return kernel


def free_kernel(shards, slots):
    def kernel(place, *refs):
        blocks = refs[:shards]
        targets, out_w, mixed, projected, free, out_free, kept_queries, kept_mixed = refs[shards:]
        me = place[0]
        block = targets.shape[1]
        part = mixed.shape[1]
        taken = targets[...].T
        total_out = jnp.zeros(out_free.shape, f32)
        for t in range(shards):
            rows = block_at(me ^ t, block)
            grads = blocks[t][part:, :]
            grads = jnp.where(taken[:, t : t + 1] >= 0, 0.0, grads.astype(f32)).astype(bf16)
            free[rows, :] = mm(grads, out_w[...], NT).astype(bf16)
            total_out = total_out + mm(mixed[rows, :], grads, TN)
            places = kept_places(targets[t : t + 1, :], slots)
            at = slice(t * slots, (t + 1) * slots)
            kept_queries[at, :] = mm(places, projected[rows, :part]).astype(bf16)
            kept_mixed[at, :] = mm(places, mixed[rows, :]).astype(bf16)
        out_free[...] = total_out

    return kernel


def early_kernel(shards, slots, local_heads, first_head):
    def kernel(
        place, projected, free, logs, table, onehot, targets,
        gq, gk, gv, diagonals, kept_probs, bias, sums,
    ):
        me = place[0]
        total = projected.shape[0]
        block = total // shards
        part = local_heads * HEAD_DIM
        offsets = mm(table[...].astype(bf16), onehot[...])
        diagonals[...] = jnp.zeros_like(diagonals)
        gk[...] = jnp.zeros_like(gk)
        gv[...] = jnp.zeros_like(gv)
        for n in range(kept_probs.shape[0]):
            h = first_head + n
            cols = slice(h * HEAD_DIM, (h + 1) * HEAD_DIM)
            own = slice(n * HEAD_DIM, (n + 1) * HEAD_DIM)
            bias[...] = bias_rows(offsets[h : h + 1, :], block)
            sums[...] = jnp.zeros_like(sums)
            keys = projected[:, part + h * HEAD_DIM : part + (h + 1) * HEAD_DIM]
            values = projected[:, 2 * part + h * HEAD_DIM : 2 * part + (h + 1) * HEAD_DIM]

            def step(a, carry, n=n, h=h, cols=cols, own=own, keys=keys, values=values):
                rows = block_at(a, block)
                lanes = pl.ds(pl.multiple_of((shards - 1 - a) * block, block), total)
                queries = projected[rows, cols]
                gm = free[rows, cols]
                scores = mm(queries, keys, NT) * score_scale + bias[:, lanes]
                probs = jnp.exp(scores - logs[rows, h : h + 1])
                grad_probs = mm(gm, values, NT)
                dots = jnp.sum(probs * grad_probs, axis=-1, keepdims=True)
                grad_scores = (probs * (grad_probs - dots)).astype(bf16)
                sums[:, lanes] += grad_scores.astype(f32)
                gq[rows, own] = mm(grad_scores, keys) * score_scale
                gk[own, :] += mm(queries, grad_scores, TN)
                probs_low = probs.astype(bf16)
                gv[own, :] += mm(gm, probs_low, TN)
                rest = probs - probs_low.astype(f32)
                rest_low = rest.astype(bf16)
                last = (rest - rest_low.astype(f32)).astype(bf16)
                places = kept_places(targets[pl.ds(a ^ me, 1), :], slots)
                kept_probs[n, block_at(a ^ me, slots), :] = (
                    mm(places, probs_low) + mm(places, rest_low) + mm(places, last)
                )
                return carry

            lax.fori_loop(0, shards, step, 0)
            diagonals[h : h + 1, :] = diagonal_row(sums[...])

    return kernel


def late_kernel(shards, slots, experts, local_heads, calls):
    def kernel(place, *refs):
        att = refs[:shards]
        refs = refs[shards:]
        early = [refs[5 * c : 5 * c + 5] for c in range(len(calls))]
        (
            normed, projected, targets, onehot, out_w, out_free, kept_queries, kept_mixed,
            router_grid, grad_projected, pieces, out_pieces,
            att_all, gm_all, gq_all, scores_all, gk, gv, sums, diagonals, grid,
        ) = refs[5 * len(calls) :]
        me = place[0]
        total = normed.shape[0]
        block = total // shards
        part = local_heads * HEAD_DIM
        for t in range(shards):
            att_all[t * slots : (t + 1) * slots, :] = att[t][...]
        gm_all[...] = mm(att_all[...], out_w[...], NT).astype(bf16)
        grad_out_w = out_free[...] + mm(kept_mixed[...], att_all[...], TN)
        count, out_piece, _ = out_pieces.shape
        for p in range(count):
            out_pieces[p] = grad_out_w[p * out_piece : (p + 1) * out_piece].astype(bf16)
        diagonals[...] = jnp.zeros_like(diagonals)
        all_rows = shards * slots
        chunk = min(all_rows, 2 * LANES)
        for c, (first_head, head_count) in enumerate(calls):
            gq_free, gk_free, gv_free, diagonals_free, kept_probs = early[c]
            gk[: head_count * HEAD_DIM, :] = gk_free[...]
            gv[: head_count * HEAD_DIM, :] = gv_free[...]
            for n in range(head_count):
                h = first_head + n
                cols = slice(h * HEAD_DIM, (h + 1) * HEAD_DIM)
                own = slice(n * HEAD_DIM, (n + 1) * HEAD_DIM)
                key_cols = slice(part + h * HEAD_DIM, part + (h + 1) * HEAD_DIM)
                value_cols = slice(2 * part + h * HEAD_DIM, 2 * part + (h + 1) * HEAD_DIM)
                keys = projected[:, key_cols]
                values = projected[:, value_cols]

                def step(i, carry, n=n, cols=cols, own=own, keys=keys, values=values):
                    rows = block_at(i, chunk)
                    gm = gm_all[rows, cols]
                    probs = kept_probs[n, rows, :]
                    grad_probs = mm(gm, values, NT)
                    dots = jnp.sum(probs * grad_probs, axis=-1, keepdims=True)
                    grad_scores = (probs * (grad_probs - dots)).astype(bf16)
                    gq_all[rows, cols] = (mm(grad_scores, keys) * score_scale).astype(bf16)
                    gk[own, :] += mm(kept_queries[rows, cols], grad_scores, TN)
                    gv[own, :] += mm(gm, probs.astype(bf16), TN)
                    scores_all[rows, :] = grad_scores
                    return carry

                if chunk == all_rows:
                    step(0, 0)
                else:
                    lax.fori_loop(0, all_rows // chunk, step, 0)
                sums[...] = jnp.zeros_like(sums)
                for t in range(shards):
                    lanes = pl.ds(pl.multiple_of((shards - 1 - (me ^ t)) * block, block), total)
                    places = kept_places(targets[t : t + 1, :], slots)
                    sums[:, lanes] += mm(places, scores_all[t * slots : (t + 1) * slots, :], TN)
                diagonals[h : h + 1, :] = diagonals_free[h : h + 1, :] + diagonal_row(sums[...])
                grad_projected[:, key_cols] = (gk[own, :] * score_scale).T.astype(bf16)
                grad_projected[:, value_cols] = gv[own, :].T.astype(bf16)
            for t in range(shards):
                rows = block_at(me ^ t, block)
                places = kept_places(targets[t : t + 1, :], slots)
                cols = slice(first_head * HEAD_DIM, (first_head + head_count) * HEAD_DIM)
                placed = mm(places, gq_all[t * slots : (t + 1) * slots, cols], TN)
                grad_projected[rows, cols] = (gq_free[rows, :] + placed).astype(bf16)
        low_onehot = onehot[...]
        grad_table = mm_left(diagonals[...], low_onehot, NT)
        width = 3 * part
        bucket_rows = low_onehot.shape[0] // shards
        used = local_heads * bucket_rows
        rows_own = grid.shape[0] // shards
        count, piece, _ = pieces.shape
        count = count // shards
        grid[:, :width] = mm(normed[...], grad_projected[...], TN)
        grid[:, width:] = jnp.zeros((grid.shape[0], grid.shape[1] - width), f32)
        grid[:, width + used : width + used + experts + 1] = router_grid[:, : experts + 1]
        for t in range(shards):
            row = jnp.concatenate(
                [
                    grad_table[h : h + 1, t * bucket_rows : (t + 1) * bucket_rows]
                    for h in range(local_heads)
                ],
                axis=1,
            )
            for p in range(count):
                at = t * rows_own + p * piece
                grid[at : at + 1, width : width + used] = row
        for p in range(count):
            for t in range(shards):
                at = t * rows_own + p * piece
                pieces[p * shards + t] = grid[at : at + piece, :].astype(bf16)

    return kernel


def normed_back_kernel(place, grad_projected, weights, *outs):
    me = place[0]
    block = outs[0].shape[0]
    for t in range(len(outs)):
        outs[t][...] = mm(grad_projected[block_at(me ^ t, block), :], weights[...], NT).astype(bf16)


def sums_kernel(shards, experts, part, used):
    def kernel(place, got, out_got, total, tables):
        count = got.shape[0] // shards
        width = 3 * part
        model_width = out_got.shape[2]
        tables[...] = jnp.zeros_like(tables)
        router = None
        for t in range(shards):
            value = got[t].astype(f32)
            for p in range(1, count):
                value = value + got[p * shards + t].astype(f32)
            total[:, t * width : (t + 1) * width] = value[:, :width].astype(bf16)
            tables[t : t + 1, :used] = value[0:1, width : width + used]
            share = value[:, width + used : width + used + experts + 1]
            router = share if router is None else router + share
        value = out_got[0].astype(f32)
        for p in range(1, count):
            value = value + out_got[p].astype(f32)
        at = shards * width
        total[:, at : at + model_width] = value.astype(bf16)
        at += model_width
        total[:, at:] = jnp.zeros((total.shape[0], LANES), bf16)
        total[:, at : at + experts + 1] = router.astype(bf16)

    return kernel


def finish_kernel(shards, experts, blocks):
    def kernel(place, *refs):
        totals = refs[:blocks]
        wq, wk, wv, gain, gq, gk, gv, gout, grouter, gtwo, gone, grid = refs[blocks:]
        rows, width = gq.shape
        part = width // shards

        def put(at, value):
            for t in range(shards):
                cols = slice(t * part, (t + 1) * part)
                first = 3 * part * t
                gq[at, cols] = value[:, first : first + part]
                gk[at, cols] = value[:, first + part : first + 2 * part]
                gv[at, cols] = value[:, first + 2 * part : first + 3 * part]
            gout[at, :] = value[:, 3 * width : 4 * width]
            grid[at, :] = value[:, 4 * width :]

        if blocks > 1:
            piece = rows // blocks
            for r in range(blocks):
                put(block_at(place[1] ^ r, piece), totals[r][...].astype(f32))
        else:
            count, piece, _ = totals[0].shape
            for p in range(count):
                put(slice(p * piece, (p + 1) * piece), totals[0][p].astype(f32))
        turned = grid[...].T
        grouter[...] = turned[:experts]
        gtwo[...] = turned[experts : experts + 1]
        dots = (
            wq[...].astype(f32) * gq[...]
            + wk[...].astype(f32) * gk[...]
            + wv[...].astype(f32) * gv[...]
        )
        ones = jnp.ones((8, dots.shape[1]), bf16)
        gone[...] = mm_right(ones, dots, NT)[0:1] / gain[...].astype(f32)

    return kernel


def per_device(
    tokens, gain_attn, pos_table, buckets, w_query, w_key, w_value, w_attn_out, w_router, gain_ffn,
    w_in, w_out, expert_ids, slots, keep, grad_out,
):
    shards = lax.axis_size("shard")
    devices = lax.axis_size("expert")
    me = lax.axis_index("shard")
    place = jnp.stack([me, lax.axis_index("expert")]).astype(jnp.int32)
    block, width = tokens.shape[1:]
    total = block * shards
    rows_own = w_query.shape[0]
    local_heads = HEADS // shards
    part = local_heads * HEAD_DIM
    experts = w_router.shape[1]
    slot_rows = experts * PAIR
    kept_rows = experts * CAP
    bucket_rows = pos_table.shape[0]
    bucket_count = bucket_rows * shards
    piece = rows_own // devices
    own_tokens = tokens[0]
    own_grad = grad_out[0]

    tok = gather_blocks(own_tokens, "shard")
    target = jnp.where(keep > 0, expert_ids * CAP + slots, -1).astype(f32)
    extra = experts + 2
    extra += -(3 * part + extra) % LANES
    packed_width = 3 * part + extra
    small = jnp.concatenate([w_router, gain_attn[:, None], gain_ffn[:, None]], axis=1)
    small = jnp.pad(small, ((0, 0), (0, extra - experts - 2)))
    last = jnp.concatenate(
        [
            jnp.pad(pos_table, ((0, 0), (0, packed_width - HEADS))),
            jnp.pad(target.astype(bf16), ((0, 15 - bucket_rows), (0, packed_width - block))),
        ],
        axis=0,
    )
    wts = call(
        pack_kernel, "pack_columns", place, [w_query, w_key, w_value, small, last],
        [like((rows_own + 16, packed_width), bf16)] * shards, flops=1e6,
    )
    wts = exchange(wts, "shard")

    later = jnp.concatenate([w_attn_out, own_grad], axis=0)
    later, _, _ = lax.optimization_barrier((later, wts, tok))
    later = gather_blocks(later, "shard")

    bucket_row = jnp.pad(
        buckets, (0, 2 * total - buckets.shape[0]), constant_values=-1
    ).reshape(1, -1)
    (
        normed, weights, projected, mixed, logs, gains, router, table, onehot, targets, *mixes
    ) = call(
        forward_kernel(shards, experts, local_heads), "attention_forward", place,
        [*tok, *wts, bucket_row],
        [
            like((total, width), bf16),
            like((width, 3 * part), bf16),
            like((total, 3 * part), bf16),
            like((total, part), bf16),
            like((total, 8), f32),
            like((8, width), f32),
            like((width, LANES), bf16),
            like((8, bucket_count), f32),
            like((bucket_count, 2 * total), bf16),
            like((8, block), f32),
        ]
        + [like((block, part), bf16)] * shards,
        [
            pltpu.VMEM((width, LANES), f32),
            pltpu.VMEM((bucket_count, LANES), f32),
            pltpu.VMEM((block, 2 * total), f32),
        ],
        flops=4 * total * total * part + 6 * total * width * part,
        transcendentals=3 * total * total,
    )

    mixes = exchange(mixes, "shard")
    (
        residual, gating, sent, sent_low, grad_y_rows, probs_rows, chosen_rows, residual_rows
    ) = call(
        route_kernel(shards, experts), "route", place,
        [*mixes, *later, own_tokens, own_grad, gains, router, target, expert_ids],
        [
            like((block, width), f32),
            like((block, LANES), f32),
            like((experts * shards, PAIR, width), bf16),
            like((slot_rows, width), bf16),
            like((slot_rows, width), f32),
            like((slot_rows, LANES), f32),
            like((slot_rows, LANES), f32),
            like((slot_rows, width), f32),
        ],
        flops=4 * block * width * width,
    )
    arrived = lax.all_to_all(
        sent, ("expert", "shard"), split_axis=0, concat_axis=0, tiled=True
    )

    later, targets, mixed, projected, logs, table, onehot, _ = lax.optimization_barrier(
        (later, targets, mixed, projected, logs, table, onehot, sent)
    )
    free, out_free, kept_queries, kept_mixed = call(
        free_kernel(shards, kept_rows), "free_tokens", place,
        [*later, targets, w_attn_out, mixed, projected],
        [
            like((total, part), bf16),
            like((part, width), f32),
            like((shards * kept_rows, part), bf16),
            like((shards * kept_rows, part), bf16),
        ],
        flops=4 * total * width * part,
    )

    def early(first_head, head_count, after):
        free_in, after = lax.optimization_barrier((free, after))
        size = head_count * HEAD_DIM
        return call(
            early_kernel(shards, kept_rows, local_heads, first_head),
            "attention_backward_free", place,
            [projected, free_in, logs, table, onehot, targets],
            [
                like((total, size), f32),
                like((size, total), f32),
                like((size, total), f32),
                like((8, 2 * total), f32),
                like((head_count, shards * kept_rows, total), f32),
            ],
            [pltpu.VMEM((block, 2 * total), f32)] * 2,
            flops=40 * total * total * size,
            transcendentals=head_count * total * total,
        )

    calls = [(0, local_heads - 1), (local_heads - 1, 1)]
    early_first = early(*calls[0], sent)
    arrived, early_first, free, out_free, kept_queries, kept_mixed = lax.optimization_barrier(
        (arrived, early_first, free, out_free, kept_queries, kept_mixed)
    )

    all_rows = arrived.shape[0] * PAIR
    hidden_own = w_in.shape[2]
    back, rows_moved, act_moved, grads, grad_hidden = call(
        expert_kernel, "experts", place, [arrived, w_in[0], w_out[0]],
        [
            like(arrived.shape, bf16),
            like((all_rows, width), bf16),
            like((all_rows, hidden_own), bf16),
            like((all_rows, width), bf16),
            like((all_rows, hidden_own), bf16),
        ],
        flops=8 * all_rows * width * hidden_own,
    )
    returned = lax.all_to_all(
        back, ("expert", "shard"), split_axis=0, concat_axis=0, tiled=True
    )
    early_second = early(*calls[1], back)
    grad_first, grad_second = call(
        expert_grads_kernel, "expert_weight_grads", place,
        [rows_moved, act_moved, grads, grad_hidden],
        [like((1, width, hidden_own), f32), like((1, hidden_own, width), f32)],
        flops=4 * all_rows * width * hidden_own,
    )

    returned, early_second, grad_first, grad_second = lax.optimization_barrier(
        (returned, early_second, grad_first, grad_second)
    )

    att_rows, grad_delta, summed, router_grid = call(
        slot_back_kernel(shards, experts), "slot_back", place,
        [
            returned, grad_y_rows, probs_rows, chosen_rows, residual_rows, sent_low, gains, router
        ],
        [
            like((kept_rows, width), bf16),
            like((slot_rows, width), f32),
            like((slot_rows, width), bf16),
            like((width, LANES), f32),
        ],
        flops=1e9,
    )
    att = [att_rows] + [swap(att_rows, "shard", t) for t in range(1, shards)]
    output, grad_residual = call(
        token_back_kernel(experts), "token_back", place,
        [residual, gating, summed, grad_delta, own_grad, target],
        [like((block, width), bf16), like((block, width), f32)],
        flops=1e8,
    )

    used = local_heads * bucket_rows
    piece_width = 3 * part + used + experts + 1
    piece_width += -piece_width % LANES
    all_kept = shards * kept_rows
    grad_projected, pieces, out_pieces = call(
        late_kernel(shards, kept_rows, experts, local_heads, calls), "attention_backward_kept", place,
        [
            *att, *early_first, *early_second, normed, projected, targets, onehot, w_attn_out,
            out_free, kept_queries, kept_mixed, router_grid,
        ],
        [
            like((total, 3 * part), bf16),
            like((devices * shards, piece, piece_width), bf16),
            like((devices, piece, width), bf16),
        ],
        [
            pltpu.VMEM((all_kept, width), bf16),
            pltpu.VMEM((all_kept, part), bf16),
            pltpu.VMEM((all_kept, part), bf16),
            pltpu.VMEM((all_kept, total), bf16),
            pltpu.VMEM((part, total), f32),
            pltpu.VMEM((part, total), f32),
            pltpu.VMEM((block, 2 * total), f32),
            pltpu.VMEM((8, 2 * total), f32),
            pltpu.VMEM((width, piece_width), f32),
        ],
        flops=10 * all_kept * total * part + 6 * total * width * part,
    )

    got = lax.all_to_all(
        pieces, ("expert", "shard"), split_axis=0, concat_axis=0, tiled=True
    )
    out_got = lax.all_to_all(out_pieces, "expert", split_axis=0, concat_axis=0, tiled=True)
    piece_total, tables = call(
        sums_kernel(shards, experts, part, used), "sums", place, [got, out_got],
        [
            like((piece, 4 * width + LANES), bf16),
            like((8, LANES), f32),
        ],
        flops=1e7,
    )
    all_total = share_piece(piece_total)

    held = dict(enumerate(call(
        normed_back_kernel, "normed_back", place, [grad_projected, weights],
        [like((block, width), bf16)] * shards, flops=6 * total * width * part,
    )))
    step = 1
    while len(held) > 1:
        held = {
            t: held[t].astype(f32) + swap(held[t ^ step].astype(bf16), "shard", step).astype(f32)
            for t in held
            if not t & step
        }
        step *= 2
    tokens_f = own_tokens.astype(f32)
    factor_one = rms_factor(tokens_f)
    grad_tokens = grad_residual + norm_back(
        held[0] * gains[0:1], tokens_f * factor_one, factor_one
    )

    total_table = tables[:shards, :used].reshape(shards, local_heads, bucket_rows)
    total_table = total_table.transpose(2, 0, 1).reshape(bucket_rows, HEADS)
    total_query, total_key, total_value, total_out, total_router, total_two, total_one = call(
        finish_kernel(shards, experts, len(all_total)), "finish", place,
        [*all_total, w_query, w_key, w_value, gain_attn.reshape(1, rows_own)],
        [like((rows_own, width), f32)] * 4
        + [like((experts, rows_own), f32)]
        + [like((1, rows_own), f32)] * 2,
        [pltpu.VMEM((rows_own, LANES), f32)],
        flops=1e7,
    )
    return (
        output[None],
        grad_tokens[None],
        total_one[0],
        total_table,
        total_query,
        total_key,
        total_value,
        total_out,
        total_router.T,
        total_two[0],
        grad_first,
        grad_second,
    )


def solution(mesh):
    in_specs = (
        P("expert", "shard", None),
        P("shard"),
        P("shard", None),
        P(),
        P("shard", None),
        P("shard", None),
        P("shard", None),
        P("shard", None),
        P("shard", None),
        P("shard"),
        P("expert", None, "shard"),
        P("expert", "shard", None),
        P("expert", "shard"),
        P("expert", "shard"),
        P("expert", "shard"),
        P("expert", "shard", None),
    )
    out_specs = (
        P("expert", "shard", None),
        P("expert", "shard", None),
        P("shard"),
        P("shard", None),
        P("shard", None),
        P("shard", None),
        P("shard", None),
        P("shard", None),
        P("shard", None),
        P("shard"),
        P("expert", None, "shard"),
        P("expert", "shard", None),
    )
    return jax.shard_map(
        per_device, mesh=mesh, in_specs=in_specs, out_specs=out_specs, check_vma=False
    )
```

```python
import math

import jax
import jax.numpy as jnp
from jax import lax
from jax.experimental import pallas as pl
from jax.experimental.pallas import tpu as pltpu
from jax.sharding import PartitionSpec as P

HEADS = 12
HEAD_DIM = 64
CAP = 4
PAIR = 2 * CAP
LANES = 128

bf16 = jnp.bfloat16
f32 = jnp.float32
epsilon = 1e-06
score_scale = HEAD_DIM ** (-0.5)

NN = (((1,), (0,)), ((), ()))
NT = (((1,), (1,)), ((), ()))
TN = (((0,), (0,)), ((), ()))


def mm(a, b, dims=NN):
    return lax.dot_general(a, b, dims, preferred_element_type=f32)


def split(value):
    high = value.astype(bf16)
    rest = value - high.astype(f32)
    middle = rest.astype(bf16)
    return high, middle, (rest - middle.astype(f32)).astype(bf16)


def mm_left(a, b, dims=NN):
    return sum(mm(part, b, dims) for part in split(a))


def mm_right(a, b, dims=NN):
    return sum(mm(a, part, dims) for part in split(b))


def rms_factor(values):
    return lax.rsqrt(jnp.mean(values * values, axis=-1, keepdims=True) + epsilon)


def norm_back(grad_normed, normed_pre, factor):
    return factor * (
        grad_normed - normed_pre * jnp.mean(grad_normed * normed_pre, axis=-1, keepdims=True)
    )


def gelu_back(hidden, grad_act):
    return jax.vjp(jax.nn.gelu, hidden)[1](grad_act)[0]


def swap(value, axis, bits):
    count = lax.axis_size(axis)
    return lax.ppermute(value, axis, [(i, i ^ bits) for i in range(count)])


def gather_blocks(value, axis):
    held = {0: value}
    step = lax.axis_size(axis) // 2
    while step >= 1:
        for t in list(held):
            held[t ^ step] = swap(held[t], axis, step)
        step //= 2
    return [held[t] for t in range(len(held))]


def exchange(blocks, axis):
    return [blocks[0]] + [swap(blocks[t], axis, t) for t in range(1, len(blocks))]


def share_piece(piece):
    count = lax.axis_size("expert")
    if count != 8:
        return [lax.all_gather(piece, "expert", axis=0)]
    held = {0: piece}
    for t in (4, 2, 6):
        held[t] = swap(piece, "expert", t)
    for t in (0, 4, 2, 6):
        held[t ^ 1] = swap(held[t], "expert", 1)
    return [held[t] for t in range(count)]


VM = pl.BlockSpec(memory_space=pltpu.VMEM)
SM = pl.BlockSpec(memory_space=pltpu.SMEM)


def call(kernel, name, place, args, outs, scratch=(), flops=1e9, transcendentals=0):
    size = sum(a.size * a.dtype.itemsize for a in args)
    size += sum(o.size * o.dtype.itemsize for o in outs)
    held = size + sum(r.dtype.itemsize * math.prod(r.shape) for r in scratch)
    limit = min(56, 14 + held // 2**20)
    return pl.pallas_call(
        kernel,
        out_shape=tuple(outs),
        in_specs=[SM] + [VM] * len(args),
        out_specs=tuple([VM] * len(outs)),
        scratch_shapes=list(scratch),
        compiler_params=pltpu.CompilerParams(vmem_limit_bytes=limit * 2**20),
        cost_estimate=pl.CostEstimate(
            flops=int(flops), bytes_accessed=int(size), transcendentals=int(transcendentals)
        ),
        name=name,
    )(place, *args)


def like(shape, dtype):
    return jax.ShapeDtypeStruct(shape, dtype)


def block_at(index, size):
    if isinstance(index, int):
        return slice(index * size, (index + 1) * size)
    return pl.ds(pl.multiple_of(index * size, size), size)


def lanes_at(index, size, count):
    if isinstance(index, int):
        return slice(index * size, index * size + count)
    return pl.ds(pl.multiple_of(index * size, size), count)


def steps(count, unroll, step):
    if unroll:
        for a in range(count):
            step(a, 0)
    else:
        lax.fori_loop(0, count, step, 0)


def pack_kernel(
    place, wq, wk, wv, router, gain_one, gain_two, heads, ids, slots, keep, *rest
):
    outs, target, tall, flat = rest[:-3], rest[-3], rest[-2], rest[-1]
    me = place[0]
    shards = len(outs)
    rows, width = wq.shape
    part = width // shards
    experts = router.shape[0]
    extra = outs[0].shape[1] - 3 * part
    tall[...] = jnp.zeros_like(tall)
    tall[:experts, :] = router[...].astype(f32)
    tall[experts : experts + 1, :] = gain_one[...].astype(f32)
    tall[experts + 1 : experts + 2, :] = gain_two[...].astype(f32)
    small = tall[...].T[:, :extra].astype(bf16)
    slot = ids[...] * CAP + slots[...]
    target[...] = jnp.where(keep[...] > 0, slot, -1).astype(f32)
    flat[...] = jnp.zeros_like(flat)
    flat[: heads.shape[0], : heads.shape[1]] = heads[...].astype(f32)
    flat[heads.shape[0] : heads.shape[0] + 1, : target.shape[1]] = target[...]
    last = flat[...].astype(bf16)
    for t in range(shards):
        for owner in range(shards):

            @pl.when((me ^ t) == owner)
            def _(t=t, owner=owner):
                cols = slice(owner * part, (owner + 1) * part)
                joined = jnp.concatenate(
                    [wq[:, cols], wk[:, cols], wv[:, cols], small], axis=1
                )
                outs[t][:rows, :] = joined

        outs[t][rows:, :] = last


def bias_rows(offsets_row, count):
    width = offsets_row.shape[1]
    rows = jnp.broadcast_to(offsets_row, (8, width))
    rows = pltpu.roll(rows, width - (count - 1), 1)
    place = lax.broadcasted_iota(jnp.int32, (8, width), 0)
    for bit in (1, 2, 4):
        rows = jnp.where((place & bit) != 0, pltpu.roll(rows, bit, 1), rows)
    while rows.shape[0] < count:
        rows = jnp.concatenate([rows, pltpu.roll(rows, rows.shape[0], 1)], axis=0)
    return rows


def diagonal_row(grid):
    total, width = grid.shape
    count = total
    while count > 8:
        count //= 2
        grid = grid[:count] + pltpu.roll(grid[count:], width - count, 1)
    place = lax.broadcasted_iota(jnp.int32, (8, width), 0)
    for bit in (4, 2, 1):
        grid = jnp.where((place & bit) != 0, pltpu.roll(grid, width - bit, 1), grid)
    return pltpu.roll(jnp.sum(grid, axis=0, keepdims=True), total - 1, 1)


def forward_kernel(shards, experts, local_heads):
    def kernel(place, *refs):
        tok = refs[:shards]
        wts = refs[shards : 2 * shards]
        buckets = refs[2 * shards]
        rest = refs[2 * shards + 1 :]
        (
            normed, weights, projected, mixed, logs, gains, router, table, onehot, targets
        ) = rest[:10]
        mixes = rest[10 : 10 + shards]
        small_f, heads_f, bias = rest[10 + shards :]
        me = place[0]
        block = tok[0].shape[0]
        total = block * shards
        part = local_heads * HEAD_DIM
        rows_own = weights.shape[0] // shards
        used = min(wts[0].shape[1] - 3 * part, LANES)
        bucket_rows = onehot.shape[0] // shards
        small_f[...] = jnp.zeros_like(small_f)
        targets[...] = jnp.zeros_like(targets)
        for t in range(shards):
            weights[block_at(me ^ t, rows_own), :] = wts[t][:rows_own, : 3 * part]
            small_f[block_at(me ^ t, rows_own), :used] = wts[t][
                :rows_own, 3 * part : 3 * part + used
            ].astype(f32)
            last = wts[t][rows_own:, :block].astype(f32)
            heads_f[block_at(me ^ t, bucket_rows), :] = last[:bucket_rows, :LANES]
            targets[t : t + 1, :] = last[bucket_rows : bucket_rows + 1]
        router[...] = small_f[...].astype(bf16)
        turned = small_f[...].T
        gains[...] = jnp.concatenate(
            [turned[experts : experts + 2], jnp.zeros((6, turned.shape[1]), f32)], axis=0
        )
        gain = gains[0:1, :]
        for t in range(shards):
            tokens_f = tok[t][...].astype(f32)
            normed[block_at(me ^ t, block), :] = (tokens_f * rms_factor(tokens_f) * gain).astype(bf16)
        projected[...] = mm(normed[...], weights[...]).astype(bf16)
        onehot[...] = (
            lax.broadcasted_iota(jnp.int32, onehot.shape, 0) == buckets[0:1, :]
        ).astype(bf16)
        small_f[:LANES, : onehot.shape[0]] = heads_f[...].T
        table[...] = jnp.zeros_like(table)
        for h in range(local_heads):
            table[h : h + 1, :] = small_f[pl.ds(me * local_heads + h, 1), : onehot.shape[0]]
        offsets = mm(table[...].astype(bf16), onehot[...])
        for h in range(local_heads):
            cols = slice(h * HEAD_DIM, (h + 1) * HEAD_DIM)
            bias[...] = bias_rows(offsets[h : h + 1, :], block)
            keys = projected[:, part + h * HEAD_DIM : part + (h + 1) * HEAD_DIM]
            values = projected[:, 2 * part + h * HEAD_DIM : 2 * part + (h + 1) * HEAD_DIM]

            def step(a, carry, cols=cols, keys=keys, values=values, h=h):
                rows = block_at(a, block)
                scores = mm(projected[rows, cols], keys, NT) * score_scale
                scores = scores + bias[:, lanes_at(shards - 1 - a, block, total)]
                peak = jnp.max(scores, axis=-1, keepdims=True)
                raised = jnp.exp(scores - peak)
                norm = jnp.sum(raised, axis=-1, keepdims=True)
                probs_low = (raised * (1.0 / norm)).astype(bf16)
                mixed[rows, cols] = mm(probs_low, values).astype(bf16)
                logs[rows, h : h + 1] = peak + jnp.log(norm)
                return carry

            steps(shards, True, step)
        for t in range(shards):
            mixes[t][...] = mixed[block_at(me ^ t, block), :]

    return kernel


def slot_places(target_row, slot_rows):
    row = lax.broadcasted_iota(jnp.int32, (slot_rows, target_row.shape[1]), 0)
    slot = (row >> 3) * CAP + (row & (CAP - 1))
    return (slot.astype(f32) == target_row).astype(f32)


def kept_places(target_row, slots):
    row = lax.broadcasted_iota(jnp.int32, (slots, target_row.shape[1]), 0)
    return (row.astype(f32) == target_row).astype(bf16)


def is_grad_row(shape):
    return (lax.broadcasted_iota(jnp.int32, shape, 0) & CAP) != 0


def route_kernel(shards, experts):
    def kernel(place, *refs):
        mix = refs[:shards]
        outw = refs[shards : 2 * shards]
        tokens, grad_out, gains, router, target, ids = refs[2 * shards : 2 * shards + 6]
        residual, gating, sent, sent_low, grad_y_rows, probs_rows, chosen_rows, residual_rows = refs[
            2 * shards + 6 :
        ]
        value = tokens[...].astype(f32)
        for t in range(shards):
            value = value + mm(mix[t][...], outw[t][: mix[t].shape[1], :])
        residual[...] = value
        ffn_in = (value * rms_factor(value) * gains[1:2, :]).astype(bf16)
        logits = mm(ffn_in, router[...])
        lane = lax.broadcasted_iota(jnp.int32, logits.shape, 1)
        logits = jnp.where(lane < experts, logits, -1e30)
        raised = jnp.exp(logits - jnp.max(logits, axis=-1, keepdims=True))
        raised = jnp.where(lane < experts, raised, 0.0)
        probs = raised / jnp.sum(raised, axis=-1, keepdims=True)
        expert = lax.broadcasted_iota(jnp.int32, (LANES, ids.shape[1]), 0)
        chosen = (expert == ids[...]).astype(f32).T
        gating[...] = jnp.broadcast_to(
            jnp.sum(probs * chosen, axis=-1, keepdims=True), gating.shape
        )
        slot_rows = experts * PAIR
        places = slot_places(target[...], slot_rows)
        places_low = places.astype(bf16)
        rows = mm(places_low, ffn_in)
        grad_y = mm(places_low, grad_out[...])
        probs_r = mm_right(places_low, probs)
        chosen_r = mm(places_low, chosen.astype(bf16))
        gate_r = jnp.sum(probs_r * chosen_r, axis=-1, keepdims=True)
        joined = jnp.where(is_grad_row(rows.shape), gate_r * grad_y, rows)
        for e in range(experts):
            piece = joined[e * PAIR : (e + 1) * PAIR].astype(bf16)
            for t in range(shards):
                sent[e * shards + t] = piece
        sent_low[...] = rows.astype(bf16)
        grad_y_rows[...] = grad_y
        probs_rows[...] = probs_r
        chosen_rows[...] = chosen_r
        residual_rows[...] = mm_right(places_low, value)

    return kernel


def expert_kernel(place, arrived, first, second, back, rows_moved, act_moved, grads, grad_hidden):
    blocks = arrived.shape[0]
    width = arrived.shape[2]
    chunk = min(32, blocks)

    def step(c):
        at = pl.ds(c * chunk, chunk)
        flat = pl.ds(pl.multiple_of(c * chunk * PAIR, chunk * PAIR), chunk * PAIR)
        both = arrived[at].astype(f32).reshape(chunk * PAIR, width)
        is_grad = is_grad_row(both.shape)
        both_low = both.astype(bf16)
        hidden = mm(both_low, first[...])
        act = jax.nn.gelu(hidden)
        act_low = act.astype(bf16)
        grad_low = jnp.where(is_grad, both, 0.0).astype(bf16)
        grad_act = mm(grad_low, second[...], NT)
        grad_h = gelu_back(pltpu.roll(hidden, CAP, 0), grad_act)
        grad_h = jnp.where(is_grad, grad_h, 0.0).astype(bf16)
        out = jnp.where(is_grad, mm(grad_h, first[...], NT), mm(act_low, second[...]))
        back[at] = out.reshape(chunk, PAIR, width).astype(bf16)
        rows_moved[flat, :] = pltpu.roll(both, CAP, 0).astype(bf16)
        act_moved[flat, :] = pltpu.roll(act_low.astype(f32), CAP, 0).astype(bf16)
        grads[flat, :] = grad_low
        grad_hidden[flat, :] = grad_h

    if blocks == chunk:
        step(0)
    else:
        pl.loop(0, blocks // chunk)(step)


def expert_grads_kernel(place, rows_moved, act_moved, grads, grad_hidden, grad_first, grad_second):
    grad_first[0] = mm(rows_moved[...], grad_hidden[...], TN)
    grad_second[0] = mm(act_moved[...], grads[...], TN)


def slot_sums(returned, shards, experts):
    width = returned.shape[2]
    value = returned[...].astype(f32).reshape(experts, shards, PAIR, width)
    total = value[:, 0]
    for t in range(1, shards):
        total = total + value[:, t]
    return total.reshape(experts * PAIR, width).astype(bf16)


def slot_back_kernel(shards, experts):
    def kernel(
        place, returned, grad_y_rows, probs_rows, chosen_rows, residual_rows, sent_low, gains, router,
        att_rows, grad_delta, summed, grid
    ):
        total = slot_sums(returned, shards, experts)
        summed[...] = total
        total = total.astype(f32)
        is_grad = is_grad_row(total.shape)
        out_rows = pltpu.roll(total, CAP, 0)
        grad_y = grad_y_rows[...]
        probs = probs_rows[...]
        chosen = chosen_rows[...]
        gate = jnp.sum(probs * chosen, axis=-1, keepdims=True)
        grad_gate = jnp.sum(grad_y * out_rows, axis=-1, keepdims=True)
        grad_logits = grad_gate * gate * (chosen - probs)
        grad_logits = jnp.where(is_grad_row(grad_logits.shape), grad_logits, 0.0)
        grad_ffn = jnp.where(is_grad, total, 0.0) + mm_left(
            grad_logits, router[...], NT
        )
        values = residual_rows[...]
        factor = rms_factor(values)
        normed = values * factor
        delta = norm_back(grad_ffn * gains[1:2, :], normed, factor)
        delta = jnp.where(is_grad, delta, 0.0)
        grad_delta[...] = delta
        att = jnp.where(is_grad, grad_y + delta, 0.0).astype(bf16)
        slot = lax.broadcasted_iota(jnp.int32, (att_rows.shape[0], total.shape[0]), 0)
        row = lax.broadcasted_iota(jnp.int32, (att_rows.shape[0], total.shape[0]), 1)
        pick = row == ((slot >> 2) * PAIR + CAP + (slot & (CAP - 1)))
        att_rows[...] = mm(pick.astype(f32).astype(bf16), att).astype(bf16)
        lane = lax.broadcasted_iota(jnp.int32, (total.shape[0], LANES), 1)
        one = (lane == experts).astype(bf16)
        grid[...] = mm_right(sent_low[...], grad_logits, TN) + mm_left(grad_ffn * normed, one, TN)

    return kernel


def token_back_kernel(experts):
    def kernel(
        place, residual, gating, summed, grad_delta, grad_out, target, output, grad_residual
    ):
        places = slot_places(target[...], experts * PAIR)
        is_grad = is_grad_row(places.shape)
        rows = jnp.where(is_grad, 0.0, places).astype(bf16)
        token_out = mm(rows, summed[...], TN)
        output[...] = (residual[...] + gating[:, 0:1] * token_out).astype(bf16)
        grad_residual[...] = grad_out[...].astype(f32) + mm_right(
            jnp.where(is_grad, places, 0.0).astype(bf16), grad_delta[...], TN
        )

    return kernel


def free_kernel(shards, slots):
    def kernel(place, *refs):
        blocks = refs[:shards]
        targets, out_w, mixed, projected, free, out_free, kept_queries, kept_mixed = refs[shards:]
        me = place[0]
        block = targets.shape[1]
        part = mixed.shape[1]
        taken = targets[...].T
        total_out = jnp.zeros(out_free.shape, f32)
        for t in range(shards):
            rows = block_at(me ^ t, block)
            grads = blocks[t][part:, :]
            grads = jnp.where(taken[:, t : t + 1] >= 0, 0.0, grads.astype(f32)).astype(bf16)
            free[rows, :] = mm(grads, out_w[...], NT).astype(bf16)
            total_out = total_out + mm(mixed[rows, :], grads, TN)
            places = kept_places(targets[t : t + 1, :], slots)
            at = slice(t * slots, (t + 1) * slots)
            kept_queries[at, :] = mm(places, projected[rows, :part]).astype(bf16)
            kept_mixed[at, :] = mm(places, mixed[rows, :]).astype(bf16)
        out_free[...] = total_out

    return kernel


def early_kernel(shards, slots, local_heads, first_head):
    def kernel(
        place, projected, free, logs, table, onehot, targets,
        gq, gk, gv, diagonals, kept_probs, bias, sums,
    ):
        me = place[0]
        total = projected.shape[0]
        block = total // shards
        part = local_heads * HEAD_DIM
        offsets = mm(table[...].astype(bf16), onehot[...])
        diagonals[...] = jnp.zeros_like(diagonals)
        gk[...] = jnp.zeros_like(gk)
        gv[...] = jnp.zeros_like(gv)
        for n in range(kept_probs.shape[0]):
            h = first_head + n
            cols = slice(h * HEAD_DIM, (h + 1) * HEAD_DIM)
            own = slice(n * HEAD_DIM, (n + 1) * HEAD_DIM)
            bias[...] = bias_rows(offsets[h : h + 1, :], block)
            sums[...] = jnp.zeros_like(sums)
            keys = projected[:, part + h * HEAD_DIM : part + (h + 1) * HEAD_DIM]
            values = projected[:, 2 * part + h * HEAD_DIM : 2 * part + (h + 1) * HEAD_DIM]

            def step(a, carry, n=n, h=h, cols=cols, own=own, keys=keys, values=values):
                rows = block_at(a, block)
                lanes = lanes_at(shards - 1 - a, block, total)
                queries = projected[rows, cols]
                gm = free[rows, cols]
                scores = mm(queries, keys, NT) * score_scale + bias[:, lanes]
                probs = jnp.exp(scores - logs[rows, h : h + 1])
                grad_probs = mm(gm, values, NT)
                dots = jnp.sum(probs * grad_probs, axis=-1, keepdims=True)
                grad_scores = (probs * (grad_probs - dots)).astype(bf16)
                sums[:, lanes] += grad_scores.astype(f32)
                gq[rows, own] = mm(grad_scores, keys) * score_scale
                gk[own, :] += mm(queries, grad_scores, TN)
                probs_low = probs.astype(bf16)
                gv[own, :] += mm(gm, probs_low, TN)
                rest = probs - probs_low.astype(f32)
                rest_low = rest.astype(bf16)
                last = (rest - rest_low.astype(f32)).astype(bf16)
                places = kept_places(targets[pl.ds(a ^ me, 1), :], slots)
                kept_probs[n, block_at(a ^ me, slots), :] = (
                    mm(places, probs_low) + mm(places, rest_low) + mm(places, last)
                )
                return carry

            steps(shards, slots <= 64, step)
            diagonals[h : h + 1, :] = diagonal_row(sums[...])

    return kernel


def out_grad_kernel(shards):
    def kernel(place, *refs):
        att = refs[:shards]
        out_w, out_free, kept_mixed, gm_all, *outs, att_all = refs[shards:]
        slots = att[0].shape[0]
        for t in range(shards):
            att_all[t * slots : (t + 1) * slots, :] = att[t][...]
        gm_all[...] = mm(att_all[...], out_w[...], NT).astype(bf16)
        total = out_free[...] + mm(kept_mixed[...], att_all[...], TN)
        if len(outs) == 1:
            outs[0][...] = total
            return
        keep, send, grid = outs
        grid[...] = total
        count, piece, _ = keep.shape
        for j in range(count):
            keep[j] = grid[block_at(place[1] ^ (2 * j), piece), :]
            send[j] = grid[block_at(place[1] ^ (2 * j + 1), piece), :].astype(bf16)

    return kernel


def late_kernel(shards, slots, experts, local_heads, calls):
    def kernel(place, *refs):
        early = [refs[5 * c : 5 * c + 5] for c in range(len(calls))]
        (
            gm_all, normed, projected, targets, onehot, kept_queries, router_grid,
            grad_projected, pieces,
            gq_all, scores_all, gk, gv, sums, diagonals, grid,
        ) = refs[5 * len(calls) :]
        me = place[0]
        total = normed.shape[0]
        block = total // shards
        part = local_heads * HEAD_DIM
        diagonals[...] = jnp.zeros_like(diagonals)
        all_rows = shards * slots
        chunk = min(all_rows, 2 * LANES)
        for c, (first_head, head_count) in enumerate(calls):
            gq_free, gk_free, gv_free, diagonals_free, kept_probs = early[c]
            gk[: head_count * HEAD_DIM, :] = gk_free[...]
            gv[: head_count * HEAD_DIM, :] = gv_free[...]
            for n in range(head_count):
                h = first_head + n
                cols = slice(h * HEAD_DIM, (h + 1) * HEAD_DIM)
                own = slice(n * HEAD_DIM, (n + 1) * HEAD_DIM)
                key_cols = slice(part + h * HEAD_DIM, part + (h + 1) * HEAD_DIM)
                value_cols = slice(2 * part + h * HEAD_DIM, 2 * part + (h + 1) * HEAD_DIM)
                keys = projected[:, key_cols]
                values = projected[:, value_cols]

                def step(i, carry, n=n, cols=cols, own=own, keys=keys, values=values):
                    rows = block_at(i, chunk)
                    gm = gm_all[rows, cols]
                    probs = kept_probs[n, rows, :]
                    grad_probs = mm(gm, values, NT)
                    dots = jnp.sum(probs * grad_probs, axis=-1, keepdims=True)
                    grad_scores = (probs * (grad_probs - dots)).astype(bf16)
                    gq_all[rows, cols] = (mm(grad_scores, keys) * score_scale).astype(bf16)
                    gk[own, :] += mm(kept_queries[rows, cols], grad_scores, TN)
                    gv[own, :] += mm(gm, probs.astype(bf16), TN)
                    scores_all[rows, :] = grad_scores
                    return carry

                if chunk == all_rows:
                    step(0, 0)
                else:
                    lax.fori_loop(0, all_rows // chunk, step, 0)
                sums[...] = jnp.zeros_like(sums)
                for t in range(shards):
                    lanes = pl.ds(pl.multiple_of((shards - 1 - (me ^ t)) * block, block), total)
                    places = kept_places(targets[t : t + 1, :], slots)
                    sums[:, lanes] += mm(places, scores_all[t * slots : (t + 1) * slots, :], TN)
                diagonals[h : h + 1, :] = diagonals_free[h : h + 1, :] + diagonal_row(sums[...])
                grad_projected[:, key_cols] = (gk[own, :] * score_scale).T.astype(bf16)
                grad_projected[:, value_cols] = gv[own, :].T.astype(bf16)
            for t in range(shards):
                rows = block_at(me ^ t, block)
                places = kept_places(targets[t : t + 1, :], slots)
                cols = slice(first_head * HEAD_DIM, (first_head + head_count) * HEAD_DIM)
                placed = mm(places, gq_all[t * slots : (t + 1) * slots, cols], TN)
                grad_projected[rows, cols] = (gq_free[rows, :] + placed).astype(bf16)
        low_onehot = onehot[...]
        grad_table = mm_left(diagonals[...], low_onehot, NT)
        width = 3 * part
        bucket_rows = low_onehot.shape[0] // shards
        used = local_heads * bucket_rows
        rows_own = grid.shape[0] // shards
        count, piece, _ = pieces.shape
        count = count // shards
        grid[:, :width] = mm(normed[...], grad_projected[...], TN)
        grid[:, width:] = jnp.zeros((grid.shape[0], grid.shape[1] - width), f32)
        grid[:, width + used : width + used + experts + 1] = router_grid[:, : experts + 1]
        for t in range(shards):
            row = jnp.concatenate(
                [
                    grad_table[h : h + 1, t * bucket_rows : (t + 1) * bucket_rows]
                    for h in range(local_heads)
                ],
                axis=1,
            )
            for p in range(count):
                at = t * rows_own + p * piece
                grid[at : at + 1, width : width + used] = row
        for p in range(count):
            for t in range(shards):
                at = t * rows_own + p * piece
                pieces[p * shards + t] = grid[at : at + piece, :].astype(bf16)

    return kernel


def normed_back_kernel(place, grad_projected, weights, *outs):
    me = place[0]
    block = outs[0].shape[0]
    for t in range(len(outs)):
        outs[t][...] = mm(grad_projected[block_at(me ^ t, block), :], weights[...], NT).astype(bf16)


def sums_kernel(shards, experts, part, used):
    def kernel(place, got, total, tables):
        count = got.shape[0] // shards
        width = 3 * part
        tables[...] = jnp.zeros_like(tables)
        router = None
        for t in range(shards):
            value = got[t].astype(f32)
            for p in range(1, count):
                value = value + got[p * shards + t].astype(f32)
            total[:, t * width : (t + 1) * width] = value[:, :width].astype(bf16)
            tables[t : t + 1, :used] = value[0:1, width : width + used]
            share = value[:, width + used : width + used + experts + 1]
            router = share if router is None else router + share
        at = shards * width
        total[:, at:] = jnp.zeros((total.shape[0], LANES), bf16)
        total[:, at : at + experts + 1] = router.astype(bf16)

    return kernel


def finish_kernel(shards, experts, blocks):
    def kernel(place, *refs):
        totals = refs[:blocks]
        out_totals = refs[blocks : 2 * blocks]
        wq, wk, wv, gain, gq, gk, gv, gout, grouter, gtwo, gone, grid = refs[2 * blocks :]
        rows, width = gq.shape
        part = width // shards

        def put(at, value, out_value):
            for t in range(shards):
                cols = slice(t * part, (t + 1) * part)
                first = 3 * part * t
                gq[at, cols] = value[:, first : first + part]
                gk[at, cols] = value[:, first + part : first + 2 * part]
                gv[at, cols] = value[:, first + 2 * part : first + 3 * part]
            gout[at, :] = out_value
            grid[at, :] = value[:, 3 * width :]

        if blocks > 1:
            piece = rows // blocks
            for r in range(blocks):
                at = block_at(place[1] ^ r, piece)
                put(at, totals[r][...].astype(f32), out_totals[r][...].astype(f32))
        else:
            count, piece, _ = totals[0].shape
            for p in range(count):
                at = slice(p * piece, (p + 1) * piece)
                put(at, totals[0][p].astype(f32), out_totals[0][p].astype(f32))
        turned = grid[...].T
        grouter[...] = turned[:experts]
        gtwo[...] = turned[experts : experts + 1]
        dots = (
            wq[...].astype(f32) * gq[...]
            + wk[...].astype(f32) * gk[...]
            + wv[...].astype(f32) * gv[...]
        )
        ones = jnp.ones((8, dots.shape[1]), bf16)
        gone[...] = mm_right(ones, dots, NT)[0:1] / gain[...].astype(f32)

    return kernel


def per_device(
    tokens, gain_attn, pos_table, buckets, w_query, w_key, w_value, w_attn_out, w_router, gain_ffn,
    w_in, w_out, expert_ids, slots, keep, grad_out,
):
    shards = lax.axis_size("shard")
    devices = lax.axis_size("expert")
    me = lax.axis_index("shard")
    place = jnp.stack([me, lax.axis_index("expert")]).astype(jnp.int32)
    block, width = tokens.shape[1:]
    total = block * shards
    rows_own = w_query.shape[0]
    local_heads = HEADS // shards
    part = local_heads * HEAD_DIM
    experts = w_router.shape[1]
    slot_rows = experts * PAIR
    kept_rows = experts * CAP
    bucket_rows = pos_table.shape[0]
    bucket_count = bucket_rows * shards
    piece = rows_own // devices
    own_tokens = tokens[0]
    own_grad = grad_out[0]

    extra = experts + 2
    extra += -(3 * part + extra) % LANES
    packed_width = 3 * part + extra
    *wts, target = call(
        pack_kernel, "pack_columns", place,
        [
            w_query, w_key, w_value, w_router.T, gain_attn.reshape(1, rows_own),
            gain_ffn.reshape(1, rows_own), pos_table, expert_ids, slots, keep,
        ],
        [like((rows_own + 16, packed_width), bf16)] * shards + [like((1, block), f32)],
        [pltpu.VMEM((extra + -extra % LANES, rows_own), f32), pltpu.VMEM((16, packed_width), f32)],
        flops=1e6,
    )
    held = {0: own_tokens}
    step = shards // 2
    held[step] = swap(own_tokens, "shard", step)
    held[step], *wts = lax.optimization_barrier((held[step], *wts))
    wts = exchange(wts, "shard")
    while step > 1:
        step //= 2
        for t in list(held):
            held[t ^ step] = swap(held[t], "shard", step)
    tok = [held[t] for t in range(shards)]

    later = jnp.concatenate([w_attn_out, own_grad], axis=0)
    later, _, _ = lax.optimization_barrier((later, wts, tok))
    later = {0: later}
    step = shards // 2
    while step >= 1:
        later[step] = swap(later[0], "shard", step)
        step //= 2

    bucket_row = jnp.pad(
        buckets, (0, 2 * total - buckets.shape[0]), constant_values=-1
    ).reshape(1, -1)
    (
        normed, weights, projected, mixed, logs, gains, router, table, onehot, targets, *mixes
    ) = call(
        forward_kernel(shards, experts, local_heads), "attention_forward", place,
        [*tok, *wts, bucket_row],
        [
            like((total, width), bf16),
            like((width, 3 * part), bf16),
            like((total, 3 * part), bf16),
            like((total, part), bf16),
            like((total, 8), f32),
            like((8, width), f32),
            like((width, LANES), bf16),
            like((8, bucket_count), f32),
            like((bucket_count, 2 * total), bf16),
            like((8, block), f32),
        ]
        + [like((block, part), bf16)] * shards,
        [
            pltpu.VMEM((width, LANES), f32),
            pltpu.VMEM((bucket_count, LANES), f32),
            pltpu.VMEM((block, 2 * total), f32),
        ],
        flops=4 * total * total * part + 6 * total * width * part,
        transcendentals=3 * total * total,
    )

    for t in range(shards):
        if t not in later:
            near = t & -t
            passed, _ = lax.optimization_barrier((later[t ^ near], mixes))
            later[t] = swap(passed, "shard", near)
    later = [later[t] for t in range(shards)]
    mixes = exchange(mixes, "shard")
    (
        residual, gating, sent, sent_low, grad_y_rows, probs_rows, chosen_rows, residual_rows
    ) = call(
        route_kernel(shards, experts), "route", place,
        [*mixes, *later, own_tokens, own_grad, gains, router, target, expert_ids],
        [
            like((block, width), f32),
            like((block, LANES), f32),
            like((experts * shards, PAIR, width), bf16),
            like((slot_rows, width), bf16),
            like((slot_rows, width), f32),
            like((slot_rows, LANES), f32),
            like((slot_rows, LANES), f32),
            like((slot_rows, width), f32),
        ],
        flops=4 * block * width * width,
    )
    arrived = lax.all_to_all(
        sent, ("expert", "shard"), split_axis=0, concat_axis=0, tiled=True
    )

    later, targets, mixed, projected, logs, table, onehot, _ = lax.optimization_barrier(
        (later, targets, mixed, projected, logs, table, onehot, sent)
    )
    free, out_free, kept_queries, kept_mixed = call(
        free_kernel(shards, kept_rows), "free_tokens", place,
        [*later, targets, w_attn_out, mixed, projected],
        [
            like((total, part), bf16),
            like((part, width), f32),
            like((shards * kept_rows, part), bf16),
            like((shards * kept_rows, part), bf16),
        ],
        flops=4 * total * width * part,
    )

    def early(first_head, head_count, after):
        free_in, after = lax.optimization_barrier((free, after))
        size = head_count * HEAD_DIM
        return call(
            early_kernel(shards, kept_rows, local_heads, first_head),
            "attention_backward_free", place,
            [projected, free_in, logs, table, onehot, targets],
            [
                like((total, size), f32),
                like((size, total), f32),
                like((size, total), f32),
                like((8, 2 * total), f32),
                like((head_count, shards * kept_rows, total), f32),
            ],
            [pltpu.VMEM((block, 2 * total), f32)] * 2,
            flops=40 * total * total * size,
            transcendentals=head_count * total * total,
        )

    calls = [(0, local_heads - 1), (local_heads - 1, 1)]
    early_first = early(*calls[0], sent)
    arrived, early_first, free, out_free, kept_queries, kept_mixed = lax.optimization_barrier(
        (arrived, early_first, free, out_free, kept_queries, kept_mixed)
    )

    all_rows = arrived.shape[0] * PAIR
    hidden_own = w_in.shape[2]
    back, rows_moved, act_moved, grads, grad_hidden = call(
        expert_kernel, "experts", place, [arrived, w_in[0], w_out[0]],
        [
            like(arrived.shape, bf16),
            like((all_rows, width), bf16),
            like((all_rows, hidden_own), bf16),
            like((all_rows, width), bf16),
            like((all_rows, hidden_own), bf16),
        ],
        flops=8 * all_rows * width * hidden_own,
    )
    returned = lax.all_to_all(
        back, ("expert", "shard"), split_axis=0, concat_axis=0, tiled=True
    )
    early_second = early(*calls[1], back)
    grad_first, grad_second = call(
        expert_grads_kernel, "expert_weight_grads", place,
        [rows_moved, act_moved, grads, grad_hidden],
        [like((1, width, hidden_own), f32), like((1, hidden_own, width), f32)],
        flops=4 * all_rows * width * hidden_own,
    )

    returned, early_second, grad_first, grad_second = lax.optimization_barrier(
        (returned, early_second, grad_first, grad_second)
    )

    att_rows, grad_delta, summed, router_grid = call(
        slot_back_kernel(shards, experts), "slot_back", place,
        [
            returned, grad_y_rows, probs_rows, chosen_rows, residual_rows, sent_low, gains, router
        ],
        [
            like((kept_rows, width), bf16),
            like((slot_rows, width), f32),
            like((slot_rows, width), bf16),
            like((width, LANES), f32),
        ],
        flops=1e9,
    )
    att = [att_rows] + [swap(att_rows, "shard", t) for t in range(1, shards)]
    output, grad_residual = call(
        token_back_kernel(experts), "token_back", place,
        [residual, gating, summed, grad_delta, own_grad, target],
        [like((block, width), bf16), like((block, width), f32)],
        flops=1e8,
    )

    all_kept = shards * kept_rows
    paired = devices == 8
    half = like((devices // 2, piece, width), f32)
    gm_all, *out_parts = call(
        out_grad_kernel(shards), "mixer_out_grad", place,
        [*att, w_attn_out, out_free, kept_mixed],
        [like((all_kept, part), bf16)]
        + ([half, like(half.shape, bf16)] if paired else [like((part, width), f32)]),
        ([pltpu.VMEM((part, width), f32)] if paired else [])
        + [pltpu.VMEM((all_kept, width), bf16)],
        flops=1e8,
    )
    if paired:
        summed_pair = out_parts[0] + swap(out_parts[1], "expert", 1).astype(f32)

    used = local_heads * bucket_rows
    piece_width = 3 * part + used + experts + 1
    piece_width += -piece_width % LANES
    grad_projected, pieces = call(
        late_kernel(shards, kept_rows, experts, local_heads, calls), "attention_backward_kept", place,
        [
            *early_first, *early_second, gm_all, normed, projected, targets, onehot, kept_queries,
            router_grid,
        ],
        [
            like((total, 3 * part), bf16),
            like((devices * shards, piece, piece_width), bf16),
        ],
        [
            pltpu.VMEM((all_kept, part), bf16),
            pltpu.VMEM((all_kept, total), bf16),
            pltpu.VMEM((part, total), f32),
            pltpu.VMEM((part, total), f32),
            pltpu.VMEM((block, 2 * total), f32),
            pltpu.VMEM((8, 2 * total), f32),
            pltpu.VMEM((width, piece_width), f32),
        ],
        flops=10 * all_kept * total * part + 6 * total * width * part,
    )

    got = lax.all_to_all(
        pieces, ("expert", "shard"), split_axis=0, concat_axis=0, tiled=True
    )
    normed_parts = call(
        normed_back_kernel, "normed_back", place, [grad_projected, weights],
        [like((block, width), bf16)] * shards, flops=6 * total * width * part,
    )
    if paired:
        summed_pair, *normed_parts = lax.optimization_barrier((summed_pair, *normed_parts))
        out_own = summed_pair[0]
        for j in range(1, devices // 2):
            out_own = out_own + swap(summed_pair[j].astype(bf16), "expert", 2 * j).astype(f32)
    else:
        out_own = lax.psum_scatter(out_parts[0], "expert", scatter_dimension=0, tiled=True)
    out_total = share_piece(out_own.astype(bf16))
    got, *out_total = lax.optimization_barrier((got, *out_total))
    piece_total, tables = call(
        sums_kernel(shards, experts, part, used), "sums", place, [got],
        [
            like((piece, 3 * width + LANES), bf16),
            like((8, LANES), f32),
        ],
        flops=1e7,
    )
    all_total = share_piece(piece_total)

    held = dict(enumerate(normed_parts))
    step = 1
    while len(held) > 1:
        held = {
            t: held[t].astype(f32) + swap(held[t ^ step].astype(bf16), "shard", step).astype(f32)
            for t in held
            if not t & step
        }
        step *= 2
    tokens_f = own_tokens.astype(f32)
    factor_one = rms_factor(tokens_f)
    grad_tokens = grad_residual + norm_back(
        held[0] * gains[0:1], tokens_f * factor_one, factor_one
    )

    total_table = tables[:shards, :used].reshape(shards, local_heads, bucket_rows)
    total_table = total_table.transpose(2, 0, 1).reshape(bucket_rows, HEADS)
    total_query, total_key, total_value, total_out, total_router, total_two, total_one = call(
        finish_kernel(shards, experts, len(all_total)), "finish", place,
        [*all_total, *out_total, w_query, w_key, w_value, gain_attn.reshape(1, rows_own)],
        [like((rows_own, width), f32)] * 4
        + [like((experts, rows_own), f32)]
        + [like((1, rows_own), f32)] * 2,
        [pltpu.VMEM((rows_own, LANES), f32)],
        flops=1e7,
    )
    return (
        output[None],
        grad_tokens[None],
        total_one[0],
        total_table,
        total_query,
        total_key,
        total_value,
        total_out,
        total_router.T,
        total_two[0],
        grad_first,
        grad_second,
    )


def solution(mesh):
    in_specs = (
        P("expert", "shard", None),
        P("shard"),
        P("shard", None),
        P(),
        P("shard", None),
        P("shard", None),
        P("shard", None),
        P("shard", None),
        P("shard", None),
        P("shard"),
        P("expert", None, "shard"),
        P("expert", "shard", None),
        P("expert", "shard"),
        P("expert", "shard"),
        P("expert", "shard"),
        P("expert", "shard", None),
    )
    out_specs = (
        P("expert", "shard", None),
        P("expert", "shard", None),
        P("shard"),
        P("shard", None),
        P("shard", None),
        P("shard", None),
        P("shard", None),
        P("shard", None),
        P("shard", None),
        P("shard"),
        P("expert", None, "shard"),
        P("expert", "shard", None),
    )
    return jax.shard_map(
        per_device, mesh=mesh, in_specs=in_specs, out_specs=out_specs, check_vma=False
    )
```

```python
import jax
import jax.numpy as jnp
from jax import lax
from jax.experimental import pallas as pl
from jax.experimental.pallas import tpu as pltpu
from jax.sharding import PartitionSpec as P

HEADS = 12
HEAD_DIM = 64
CAP = 4
PAIR = 2 * CAP
LANES = 128

bf16 = jnp.bfloat16
f32 = jnp.float32
epsilon = 1e-06
score_scale = HEAD_DIM ** (-0.5)

NN = (((1,), (0,)), ((), ()))
NT = (((1,), (1,)), ((), ()))
TN = (((0,), (0,)), ((), ()))


def mm(a, b, dims=NN):
    return lax.dot_general(a, b, dims, preferred_element_type=f32)


def split(value):
    high = value.astype(bf16)
    rest = value - high.astype(f32)
    middle = rest.astype(bf16)
    return high, middle, (rest - middle.astype(f32)).astype(bf16)


def mm_left(a, b, dims=NN):
    return sum(mm(part, b, dims) for part in split(a))


def mm_right(a, b, dims=NN):
    return sum(mm(a, part, dims) for part in split(b))


def rms_factor(values):
    return lax.rsqrt(jnp.mean(values * values, axis=-1, keepdims=True) + epsilon)


def norm_back(grad_normed, normed_pre, factor):
    return factor * (
        grad_normed - normed_pre * jnp.mean(grad_normed * normed_pre, axis=-1, keepdims=True)
    )


def gelu_back(hidden, grad_act):
    return jax.vjp(jax.nn.gelu, hidden)[1](grad_act)[0]


def swap(value, axis, bits):
    count = lax.axis_size(axis)
    return lax.ppermute(value, axis, [(i, i ^ bits) for i in range(count)])


def gather_blocks(value, axis):
    held = {0: value}
    step = lax.axis_size(axis) // 2
    while step >= 1:
        for t in list(held):
            held[t ^ step] = swap(held[t], axis, step)
        step //= 2
    return [held[t] for t in range(len(held))]


def exchange(blocks, axis):
    return [blocks[0]] + [swap(blocks[t], axis, t) for t in range(1, len(blocks))]


def share_piece(piece):
    count = lax.axis_size("expert")
    if count != 8:
        return [lax.all_gather(piece, "expert", axis=0)]
    held = {0: piece}
    for t in (4, 2, 6):
        held[t] = swap(piece, "expert", t)
    for t in (0, 4, 2, 6):
        held[t ^ 1] = swap(held[t], "expert", 1)
    return [held[t] for t in range(count)]


VM = pl.BlockSpec(memory_space=pltpu.VMEM)
SM = pl.BlockSpec(memory_space=pltpu.SMEM)


def call(kernel, name, place, args, outs, scratch=(), flops=1e9, transcendentals=0):
    size = sum(a.size * a.dtype.itemsize for a in args)
    size += sum(o.size * o.dtype.itemsize for o in outs)
    return pl.pallas_call(
        kernel,
        out_shape=tuple(outs),
        in_specs=[SM] + [VM] * len(args),
        out_specs=tuple([VM] * len(outs)),
        scratch_shapes=list(scratch),
        compiler_params=pltpu.CompilerParams(vmem_limit_bytes=56 * 2**20),
        cost_estimate=pl.CostEstimate(
            flops=int(flops), bytes_accessed=int(size), transcendentals=int(transcendentals)
        ),
        name=name,
    )(place, *args)


def like(shape, dtype):
    return jax.ShapeDtypeStruct(shape, dtype)


def block_at(index, size):
    if isinstance(index, int):
        return slice(index * size, (index + 1) * size)
    return pl.ds(pl.multiple_of(index * size, size), size)


def lanes_at(index, size, count):
    if isinstance(index, int):
        return slice(index * size, index * size + count)
    return pl.ds(pl.multiple_of(index * size, size), count)


def steps(count, unroll, step):
    if unroll:
        for a in range(count):
            step(a, 0)
    else:
        lax.fori_loop(0, count, step, 0)


def pack_kernel(
    place, wq, wk, wv, router, gain_one, gain_two, heads, ids, slots, keep, *rest
):
    outs, target, tall, flat = rest[:-3], rest[-3], rest[-2], rest[-1]
    me = place[0]
    shards = len(outs)
    rows, width = wq.shape
    part = width // shards
    experts = router.shape[0]
    extra = outs[0].shape[1] - 3 * part
    tall[...] = jnp.zeros_like(tall)
    tall[:experts, :] = router[...].astype(f32)
    tall[experts : experts + 1, :] = gain_one[...].astype(f32)
    tall[experts + 1 : experts + 2, :] = gain_two[...].astype(f32)
    small = tall[...].T[:, :extra].astype(bf16)
    slot = ids[...] * CAP + slots[...]
    target[...] = jnp.where(keep[...] > 0, slot, -1).astype(f32)
    flat[...] = jnp.zeros_like(flat)
    flat[: heads.shape[0], : heads.shape[1]] = heads[...].astype(f32)
    flat[heads.shape[0] : heads.shape[0] + 1, : target.shape[1]] = target[...]
    last = flat[...].astype(bf16)
    for t in range(shards):
        for owner in range(shards):

            @pl.when((me ^ t) == owner)
            def _(t=t, owner=owner):
                cols = slice(owner * part, (owner + 1) * part)
                joined = jnp.concatenate(
                    [wq[:, cols], wk[:, cols], wv[:, cols], small], axis=1
                )
                outs[t][:rows, :] = joined

        outs[t][rows:, :] = last


def bias_rows(offsets_row, count):
    width = offsets_row.shape[1]
    rows = jnp.broadcast_to(offsets_row, (8, width))
    rows = pltpu.roll(rows, width - (count - 1), 1)
    place = lax.broadcasted_iota(jnp.int32, (8, width), 0)
    for bit in (1, 2, 4):
        rows = jnp.where((place & bit) != 0, pltpu.roll(rows, bit, 1), rows)
    while rows.shape[0] < count:
        rows = jnp.concatenate([rows, pltpu.roll(rows, rows.shape[0], 1)], axis=0)
    return rows


def diagonal_row(grid):
    total, width = grid.shape
    count = total
    while count > 8:
        count //= 2
        grid = grid[:count] + pltpu.roll(grid[count:], width - count, 1)
    place = lax.broadcasted_iota(jnp.int32, (8, width), 0)
    for bit in (4, 2, 1):
        grid = jnp.where((place & bit) != 0, pltpu.roll(grid, width - bit, 1), grid)
    return pltpu.roll(jnp.sum(grid, axis=0, keepdims=True), total - 1, 1)


def forward_kernel(shards, experts, local_heads):
    def kernel(place, *refs):
        tok = refs[:shards]
        wts = refs[shards : 2 * shards]
        buckets = refs[2 * shards]
        rest = refs[2 * shards + 1 :]
        (
            normed, weights, projected, mixed, logs, gains, router, table, onehot, targets
        ) = rest[:10]
        mixes = rest[10 : 10 + shards]
        small_f, heads_f, bias = rest[10 + shards :]
        me = place[0]
        block = tok[0].shape[0]
        total = block * shards
        part = local_heads * HEAD_DIM
        rows_own = weights.shape[0] // shards
        used = min(wts[0].shape[1] - 3 * part, LANES)
        bucket_rows = onehot.shape[0] // shards
        small_f[...] = jnp.zeros_like(small_f)
        targets[...] = jnp.zeros_like(targets)
        for t in range(shards):
            weights[block_at(me ^ t, rows_own), :] = wts[t][:rows_own, : 3 * part]
            small_f[block_at(me ^ t, rows_own), :used] = wts[t][
                :rows_own, 3 * part : 3 * part + used
            ].astype(f32)
            last = wts[t][rows_own:, :block].astype(f32)
            heads_f[block_at(me ^ t, bucket_rows), :] = last[:bucket_rows, :LANES]
            targets[t : t + 1, :] = last[bucket_rows : bucket_rows + 1]
        router[...] = small_f[...].astype(bf16)
        turned = small_f[...].T
        gains[...] = jnp.concatenate(
            [turned[experts : experts + 2], jnp.zeros((6, turned.shape[1]), f32)], axis=0
        )
        gain = gains[0:1, :]
        for t in range(shards):
            tokens_f = tok[t][...].astype(f32)
            normed[block_at(me ^ t, block), :] = (tokens_f * rms_factor(tokens_f) * gain).astype(bf16)
        projected[...] = mm(normed[...], weights[...]).astype(bf16)
        onehot[...] = (
            lax.broadcasted_iota(jnp.int32, onehot.shape, 0) == buckets[0:1, :]
        ).astype(bf16)
        small_f[:LANES, : onehot.shape[0]] = heads_f[...].T
        table[...] = jnp.zeros_like(table)
        for h in range(local_heads):
            table[h : h + 1, :] = small_f[pl.ds(me * local_heads + h, 1), : onehot.shape[0]]
        offsets = mm(table[...].astype(bf16), onehot[...])
        for h in range(local_heads):
            cols = slice(h * HEAD_DIM, (h + 1) * HEAD_DIM)
            bias[...] = bias_rows(offsets[h : h + 1, :], block)
            keys = projected[:, part + h * HEAD_DIM : part + (h + 1) * HEAD_DIM]
            values = projected[:, 2 * part + h * HEAD_DIM : 2 * part + (h + 1) * HEAD_DIM]

            def step(a, carry, cols=cols, keys=keys, values=values, h=h):
                rows = block_at(a, block)
                scores = mm(projected[rows, cols], keys, NT) * score_scale
                scores = scores + bias[:, lanes_at(shards - 1 - a, block, total)]
                peak = jnp.max(scores, axis=-1, keepdims=True)
                raised = jnp.exp(scores - peak)
                norm = jnp.sum(raised, axis=-1, keepdims=True)
                probs_low = (raised * (1.0 / norm)).astype(bf16)
                mixed[rows, cols] = mm(probs_low, values).astype(bf16)
                logs[rows, h : h + 1] = peak + jnp.log(norm)
                return carry

            steps(shards, True, step)
        for t in range(shards):
            mixes[t][...] = mixed[block_at(me ^ t, block), :]

    return kernel


def slot_places(target_row, slot_rows):
    row = lax.broadcasted_iota(jnp.int32, (slot_rows, target_row.shape[1]), 0)
    slot = (row >> 3) * CAP + (row & (CAP - 1))
    return (slot.astype(f32) == target_row).astype(f32)


def kept_places(target_row, slots):
    row = lax.broadcasted_iota(jnp.int32, (slots, target_row.shape[1]), 0)
    return (row.astype(f32) == target_row).astype(bf16)


def is_grad_row(shape):
    return (lax.broadcasted_iota(jnp.int32, shape, 0) & CAP) != 0


def route_kernel(shards, experts):
    def kernel(place, *refs):
        mix = refs[:shards]
        outw = refs[shards : 2 * shards]
        tokens, grad_out, gains, router, target, ids = refs[2 * shards : 2 * shards + 6]
        residual, gating, sent, sent_low, grad_y_rows, probs_rows, chosen_rows, residual_rows = refs[
            2 * shards + 6 :
        ]
        value = tokens[...].astype(f32)
        for t in range(shards):
            value = value + mm(mix[t][...], outw[t][: mix[t].shape[1], :])
        residual[...] = value
        ffn_in = (value * rms_factor(value) * gains[1:2, :]).astype(bf16)
        logits = mm(ffn_in, router[...])
        lane = lax.broadcasted_iota(jnp.int32, logits.shape, 1)
        logits = jnp.where(lane < experts, logits, -1e30)
        raised = jnp.exp(logits - jnp.max(logits, axis=-1, keepdims=True))
        raised = jnp.where(lane < experts, raised, 0.0)
        probs = raised / jnp.sum(raised, axis=-1, keepdims=True)
        expert = lax.broadcasted_iota(jnp.int32, (LANES, ids.shape[1]), 0)
        chosen = (expert == ids[...]).astype(f32).T
        gating[...] = jnp.broadcast_to(
            jnp.sum(probs * chosen, axis=-1, keepdims=True), gating.shape
        )
        slot_rows = experts * PAIR
        places = slot_places(target[...], slot_rows)
        places_low = places.astype(bf16)
        rows = mm(places_low, ffn_in)
        grad_y = mm(places_low, grad_out[...])
        probs_r = mm_right(places_low, probs)
        chosen_r = mm(places_low, chosen.astype(bf16))
        gate_r = jnp.sum(probs_r * chosen_r, axis=-1, keepdims=True)
        joined = jnp.where(is_grad_row(rows.shape), gate_r * grad_y, rows)
        for e in range(experts):
            piece = joined[e * PAIR : (e + 1) * PAIR].astype(bf16)
            for t in range(shards):
                sent[e * shards + t] = piece
        sent_low[...] = rows.astype(bf16)
        grad_y_rows[...] = grad_y
        probs_rows[...] = probs_r
        chosen_rows[...] = chosen_r
        residual_rows[...] = mm_right(places_low, value)

    return kernel


def expert_kernel(place, arrived, first, second, back, rows_moved, act_moved, grads, grad_hidden):
    blocks = arrived.shape[0]
    width = arrived.shape[2]
    chunk = min(32, blocks)

    def step(c):
        at = pl.ds(c * chunk, chunk)
        flat = pl.ds(pl.multiple_of(c * chunk * PAIR, chunk * PAIR), chunk * PAIR)
        both = arrived[at].astype(f32).reshape(chunk * PAIR, width)
        is_grad = is_grad_row(both.shape)
        both_low = both.astype(bf16)
        hidden = mm(both_low, first[...])
        act = jax.nn.gelu(hidden)
        act_low = act.astype(bf16)
        grad_low = jnp.where(is_grad, both, 0.0).astype(bf16)
        grad_act = mm(grad_low, second[...], NT)
        grad_h = gelu_back(pltpu.roll(hidden, CAP, 0), grad_act)
        grad_h = jnp.where(is_grad, grad_h, 0.0).astype(bf16)
        out = jnp.where(is_grad, mm(grad_h, first[...], NT), mm(act_low, second[...]))
        back[at] = out.reshape(chunk, PAIR, width).astype(bf16)
        rows_moved[flat, :] = pltpu.roll(both, CAP, 0).astype(bf16)
        act_moved[flat, :] = pltpu.roll(act_low.astype(f32), CAP, 0).astype(bf16)
        grads[flat, :] = grad_low
        grad_hidden[flat, :] = grad_h

    if blocks == chunk:
        step(0)
    else:
        pl.loop(0, blocks // chunk)(step)


def expert_grads_kernel(place, rows_moved, act_moved, grads, grad_hidden, grad_first, grad_second):
    grad_first[0] = mm(rows_moved[...], grad_hidden[...], TN)
    grad_second[0] = mm(act_moved[...], grads[...], TN)


def slot_sums(returned, shards, experts):
    width = returned.shape[2]
    value = returned[...].astype(f32).reshape(experts, shards, PAIR, width)
    total = value[:, 0]
    for t in range(1, shards):
        total = total + value[:, t]
    return total.reshape(experts * PAIR, width).astype(bf16)


def slot_back_kernel(shards, experts):
    def kernel(
        place, returned, grad_y_rows, probs_rows, chosen_rows, residual_rows, sent_low, gains, router,
        att_rows, grad_delta, summed, grid
    ):
        total = slot_sums(returned, shards, experts)
        summed[...] = total
        total = total.astype(f32)
        is_grad = is_grad_row(total.shape)
        out_rows = pltpu.roll(total, CAP, 0)
        grad_y = grad_y_rows[...]
        probs = probs_rows[...]
        chosen = chosen_rows[...]
        gate = jnp.sum(probs * chosen, axis=-1, keepdims=True)
        grad_gate = jnp.sum(grad_y * out_rows, axis=-1, keepdims=True)
        grad_logits = grad_gate * gate * (chosen - probs)
        grad_logits = jnp.where(is_grad_row(grad_logits.shape), grad_logits, 0.0)
        grad_ffn = jnp.where(is_grad, total, 0.0) + mm_left(
            grad_logits, router[...], NT
        )
        values = residual_rows[...]
        factor = rms_factor(values)
        normed = values * factor
        delta = norm_back(grad_ffn * gains[1:2, :], normed, factor)
        delta = jnp.where(is_grad, delta, 0.0)
        grad_delta[...] = delta
        att = jnp.where(is_grad, grad_y + delta, 0.0).astype(bf16)
        slot = lax.broadcasted_iota(jnp.int32, (att_rows.shape[0], total.shape[0]), 0)
        row = lax.broadcasted_iota(jnp.int32, (att_rows.shape[0], total.shape[0]), 1)
        pick = row == ((slot >> 2) * PAIR + CAP + (slot & (CAP - 1)))
        att_rows[...] = mm(pick.astype(f32).astype(bf16), att).astype(bf16)
        lane = lax.broadcasted_iota(jnp.int32, (total.shape[0], LANES), 1)
        one = (lane == experts).astype(bf16)
        grid[...] = mm_right(sent_low[...], grad_logits, TN) + mm_left(grad_ffn * normed, one, TN)

    return kernel


def token_back_kernel(experts):
    def kernel(
        place, residual, gating, summed, grad_delta, grad_out, target, output, grad_residual
    ):
        places = slot_places(target[...], experts * PAIR)
        is_grad = is_grad_row(places.shape)
        rows = jnp.where(is_grad, 0.0, places).astype(bf16)
        token_out = mm(rows, summed[...], TN)
        output[...] = (residual[...] + gating[:, 0:1] * token_out).astype(bf16)
        grad_residual[...] = grad_out[...].astype(f32) + mm_right(
            jnp.where(is_grad, places, 0.0).astype(bf16), grad_delta[...], TN
        )

    return kernel


def free_kernel(shards, slots):
    def kernel(place, *refs):
        blocks = refs[:shards]
        targets, out_w, mixed, projected, free, out_free, kept_queries, kept_mixed = refs[shards:]
        me = place[0]
        block = targets.shape[1]
        part = mixed.shape[1]
        taken = targets[...].T
        total_out = jnp.zeros(out_free.shape, f32)
        for t in range(shards):
            rows = block_at(me ^ t, block)
            grads = blocks[t][part:, :]
            grads = jnp.where(taken[:, t : t + 1] >= 0, 0.0, grads.astype(f32)).astype(bf16)
            free[rows, :] = mm(grads, out_w[...], NT).astype(bf16)
            total_out = total_out + mm(mixed[rows, :], grads, TN)
            places = kept_places(targets[t : t + 1, :], slots)
            at = slice(t * slots, (t + 1) * slots)
            kept_queries[at, :] = mm(places, projected[rows, :part]).astype(bf16)
            kept_mixed[at, :] = mm(places, mixed[rows, :]).astype(bf16)
        out_free[...] = total_out

    return kernel


def early_kernel(shards, slots, local_heads, first_head):
    def kernel(
        place, projected, free, logs, table, onehot, targets,
        gq, gk, gv, diagonals, kept_probs, bias, sums,
    ):
        me = place[0]
        total = projected.shape[0]
        block = total // shards
        part = local_heads * HEAD_DIM
        offsets = mm(table[...].astype(bf16), onehot[...])
        diagonals[...] = jnp.zeros_like(diagonals)
        gk[...] = jnp.zeros_like(gk)
        gv[...] = jnp.zeros_like(gv)
        for n in range(kept_probs.shape[0]):
            h = first_head + n
            cols = slice(h * HEAD_DIM, (h + 1) * HEAD_DIM)
            own = slice(n * HEAD_DIM, (n + 1) * HEAD_DIM)
            bias[...] = bias_rows(offsets[h : h + 1, :], block)
            sums[...] = jnp.zeros_like(sums)
            keys = projected[:, part + h * HEAD_DIM : part + (h + 1) * HEAD_DIM]
            values = projected[:, 2 * part + h * HEAD_DIM : 2 * part + (h + 1) * HEAD_DIM]

            def step(a, carry, n=n, h=h, cols=cols, own=own, keys=keys, values=values):
                rows = block_at(a, block)
                lanes = lanes_at(shards - 1 - a, block, total)
                queries = projected[rows, cols]
                gm = free[rows, cols]
                scores = mm(queries, keys, NT) * score_scale + bias[:, lanes]
                probs = jnp.exp(scores - logs[rows, h : h + 1])
                grad_probs = mm(gm, values, NT)
                dots = jnp.sum(probs * grad_probs, axis=-1, keepdims=True)
                grad_scores = (probs * (grad_probs - dots)).astype(bf16)
                sums[:, lanes] += grad_scores.astype(f32)
                gq[rows, own] = mm(grad_scores, keys) * score_scale
                gk[own, :] += mm(queries, grad_scores, TN)
                probs_low = probs.astype(bf16)
                gv[own, :] += mm(gm, probs_low, TN)
                rest = probs - probs_low.astype(f32)
                rest_low = rest.astype(bf16)
                last = (rest - rest_low.astype(f32)).astype(bf16)
                places = kept_places(targets[pl.ds(a ^ me, 1), :], slots)
                kept_probs[n, block_at(a ^ me, slots), :] = (
                    mm(places, probs_low) + mm(places, rest_low) + mm(places, last)
                )
                return carry

            steps(shards, slots <= 64, step)
            diagonals[h : h + 1, :] = diagonal_row(sums[...])

    return kernel


def out_grad_kernel(shards):
    def kernel(place, *refs):
        att = refs[:shards]
        out_w, out_free, kept_mixed, gm_all, *outs, att_all = refs[shards:]
        slots = att[0].shape[0]
        for t in range(shards):
            att_all[t * slots : (t + 1) * slots, :] = att[t][...]
        gm_all[...] = mm(att_all[...], out_w[...], NT).astype(bf16)
        total = out_free[...] + mm(kept_mixed[...], att_all[...], TN)
        if len(outs) == 1:
            outs[0][...] = total
            return
        keep, send, grid = outs
        grid[...] = total
        count, piece, _ = keep.shape
        for j in range(count):
            keep[j] = grid[block_at(place[1] ^ (2 * j), piece), :]
            send[j] = grid[block_at(place[1] ^ (2 * j + 1), piece), :].astype(bf16)

    return kernel


def late_kernel(shards, slots, experts, local_heads, calls):
    def kernel(place, *refs):
        early = [refs[5 * c : 5 * c + 5] for c in range(len(calls))]
        (
            gm_all, normed, projected, targets, onehot, kept_queries, router_grid,
            grad_projected, pieces,
            gq_all, scores_all, gk, gv, sums, diagonals, grid,
        ) = refs[5 * len(calls) :]
        me = place[0]
        total = normed.shape[0]
        block = total // shards
        part = local_heads * HEAD_DIM
        diagonals[...] = jnp.zeros_like(diagonals)
        all_rows = shards * slots
        chunk = min(all_rows, 2 * LANES)
        for c, (first_head, head_count) in enumerate(calls):
            gq_free, gk_free, gv_free, diagonals_free, kept_probs = early[c]
            gk[: head_count * HEAD_DIM, :] = gk_free[...]
            gv[: head_count * HEAD_DIM, :] = gv_free[...]
            for n in range(head_count):
                h = first_head + n
                cols = slice(h * HEAD_DIM, (h + 1) * HEAD_DIM)
                own = slice(n * HEAD_DIM, (n + 1) * HEAD_DIM)
                key_cols = slice(part + h * HEAD_DIM, part + (h + 1) * HEAD_DIM)
                value_cols = slice(2 * part + h * HEAD_DIM, 2 * part + (h + 1) * HEAD_DIM)
                keys = projected[:, key_cols]
                values = projected[:, value_cols]

                def step(i, carry, n=n, cols=cols, own=own, keys=keys, values=values):
                    rows = block_at(i, chunk)
                    gm = gm_all[rows, cols]
                    probs = kept_probs[n, rows, :]
                    grad_probs = mm(gm, values, NT)
                    dots = jnp.sum(probs * grad_probs, axis=-1, keepdims=True)
                    grad_scores = (probs * (grad_probs - dots)).astype(bf16)
                    gq_all[rows, cols] = (mm(grad_scores, keys) * score_scale).astype(bf16)
                    gk[own, :] += mm(kept_queries[rows, cols], grad_scores, TN)
                    gv[own, :] += mm(gm, probs.astype(bf16), TN)
                    scores_all[rows, :] = grad_scores
                    return carry

                if chunk == all_rows:
                    step(0, 0)
                else:
                    lax.fori_loop(0, all_rows // chunk, step, 0)
                sums[...] = jnp.zeros_like(sums)
                for t in range(shards):
                    lanes = pl.ds(pl.multiple_of((shards - 1 - (me ^ t)) * block, block), total)
                    places = kept_places(targets[t : t + 1, :], slots)
                    sums[:, lanes] += mm(places, scores_all[t * slots : (t + 1) * slots, :], TN)
                diagonals[h : h + 1, :] = diagonals_free[h : h + 1, :] + diagonal_row(sums[...])
                grad_projected[:, key_cols] = (gk[own, :] * score_scale).T.astype(bf16)
                grad_projected[:, value_cols] = gv[own, :].T.astype(bf16)
            for t in range(shards):
                rows = block_at(me ^ t, block)
                places = kept_places(targets[t : t + 1, :], slots)
                cols = slice(first_head * HEAD_DIM, (first_head + head_count) * HEAD_DIM)
                placed = mm(places, gq_all[t * slots : (t + 1) * slots, cols], TN)
                grad_projected[rows, cols] = (gq_free[rows, :] + placed).astype(bf16)
        low_onehot = onehot[...]
        grad_table = mm_left(diagonals[...], low_onehot, NT)
        width = 3 * part
        bucket_rows = low_onehot.shape[0] // shards
        used = local_heads * bucket_rows
        rows_own = grid.shape[0] // shards
        count, piece, _ = pieces.shape
        count = count // shards
        grid[:, :width] = mm(normed[...], grad_projected[...], TN)
        grid[:, width:] = jnp.zeros((grid.shape[0], grid.shape[1] - width), f32)
        grid[:, width + used : width + used + experts + 1] = router_grid[:, : experts + 1]
        for t in range(shards):
            row = jnp.concatenate(
                [
                    grad_table[h : h + 1, t * bucket_rows : (t + 1) * bucket_rows]
                    for h in range(local_heads)
                ],
                axis=1,
            )
            for p in range(count):
                at = t * rows_own + p * piece
                grid[at : at + 1, width : width + used] = row
        for p in range(count):
            for t in range(shards):
                at = t * rows_own + p * piece
                pieces[p * shards + t] = grid[at : at + piece, :].astype(bf16)

    return kernel


def normed_back_kernel(place, grad_projected, weights, *outs):
    me = place[0]
    block = outs[0].shape[0]
    for t in range(len(outs)):
        outs[t][...] = mm(grad_projected[block_at(me ^ t, block), :], weights[...], NT).astype(bf16)


def sums_kernel(shards, experts, part, used):
    def kernel(place, got, *refs):
        *out_terms, total, tables = refs
        count = got.shape[0] // shards
        width = 3 * part
        tables[...] = jnp.zeros_like(tables)
        router = None
        for t in range(shards):
            value = got[t].astype(f32)
            for p in range(1, count):
                value = value + got[p * shards + t].astype(f32)
            total[:, t * width : (t + 1) * width] = value[:, :width].astype(bf16)
            tables[t : t + 1, :used] = value[0:1, width : width + used]
            share = value[:, width + used : width + used + experts + 1]
            router = share if router is None else router + share
        at = shards * width
        value = out_terms[0][...]
        for term in out_terms[1:]:
            value = value + term[...].astype(f32)
        total[:, at : at + value.shape[1]] = value.astype(bf16)
        at += value.shape[1]
        total[:, at:] = jnp.zeros((total.shape[0], LANES), bf16)
        total[:, at : at + experts + 1] = router.astype(bf16)

    return kernel


def finish_kernel(shards, experts, blocks):
    def kernel(place, *refs):
        totals = refs[:blocks]
        wq, wk, wv, gain, gq, gk, gv, gout, grouter, gtwo, gone, grid = refs[blocks:]
        rows, width = gq.shape
        part = width // shards

        def put(at, value):
            for t in range(shards):
                cols = slice(t * part, (t + 1) * part)
                first = 3 * part * t
                gq[at, cols] = value[:, first : first + part]
                gk[at, cols] = value[:, first + part : first + 2 * part]
                gv[at, cols] = value[:, first + 2 * part : first + 3 * part]
            gout[at, :] = value[:, 3 * width : 4 * width]
            grid[at, :] = value[:, 4 * width :]

        if blocks > 1:
            piece = rows // blocks
            for r in range(blocks):
                at = block_at(place[1] ^ r, piece)
                put(at, totals[r][...].astype(f32))
        else:
            count, piece, _ = totals[0].shape
            for p in range(count):
                at = slice(p * piece, (p + 1) * piece)
                put(at, totals[0][p].astype(f32))
        turned = grid[...].T
        grouter[...] = turned[:experts]
        gtwo[...] = turned[experts : experts + 1]
        dots = (
            wq[...].astype(f32) * gq[...]
            + wk[...].astype(f32) * gk[...]
            + wv[...].astype(f32) * gv[...]
        )
        ones = jnp.ones((8, dots.shape[1]), bf16)
        gone[...] = mm_right(ones, dots, NT)[0:1] / gain[...].astype(f32)

    return kernel


def per_device(
    tokens, gain_attn, pos_table, buckets, w_query, w_key, w_value, w_attn_out, w_router, gain_ffn,
    w_in, w_out, expert_ids, slots, keep, grad_out,
):
    shards = lax.axis_size("shard")
    devices = lax.axis_size("expert")
    me = lax.axis_index("shard")
    place = jnp.stack([me, lax.axis_index("expert")]).astype(jnp.int32)
    block, width = tokens.shape[1:]
    total = block * shards
    rows_own = w_query.shape[0]
    local_heads = HEADS // shards
    part = local_heads * HEAD_DIM
    experts = w_router.shape[1]
    slot_rows = experts * PAIR
    kept_rows = experts * CAP
    bucket_rows = pos_table.shape[0]
    bucket_count = bucket_rows * shards
    piece = rows_own // devices
    own_tokens = tokens[0]
    own_grad = grad_out[0]

    extra = experts + 2
    extra += -(3 * part + extra) % LANES
    packed_width = 3 * part + extra
    *wts, target = call(
        pack_kernel, "pack_columns", place,
        [
            w_query, w_key, w_value, w_router.T, gain_attn.reshape(1, rows_own),
            gain_ffn.reshape(1, rows_own), pos_table, expert_ids, slots, keep,
        ],
        [like((rows_own + 16, packed_width), bf16)] * shards + [like((1, block), f32)],
        [pltpu.VMEM((extra + -extra % LANES, rows_own), f32), pltpu.VMEM((16, packed_width), f32)],
        flops=1e6,
    )
    held = {0: own_tokens}
    step = shards // 2
    held[step] = swap(own_tokens, "shard", step)
    held[step], *wts = lax.optimization_barrier((held[step], *wts))
    wts = exchange(wts, "shard")
    while step > 1:
        step //= 2
        for t in list(held):
            held[t ^ step] = swap(held[t], "shard", step)
    tok = [held[t] for t in range(shards)]

    later = jnp.concatenate([w_attn_out, own_grad], axis=0)
    later, _, _ = lax.optimization_barrier((later, wts, tok))
    later = {0: later}
    step = shards // 2
    while step >= 1:
        later[step] = swap(later[0], "shard", step)
        step //= 2

    bucket_row = jnp.pad(
        buckets, (0, 2 * total - buckets.shape[0]), constant_values=-1
    ).reshape(1, -1)
    (
        normed, weights, projected, mixed, logs, gains, router, table, onehot, targets, *mixes
    ) = call(
        forward_kernel(shards, experts, local_heads), "attention_forward", place,
        [*tok, *wts, bucket_row],
        [
            like((total, width), bf16),
            like((width, 3 * part), bf16),
            like((total, 3 * part), bf16),
            like((total, part), bf16),
            like((total, 8), f32),
            like((8, width), f32),
            like((width, LANES), bf16),
            like((8, bucket_count), f32),
            like((bucket_count, 2 * total), bf16),
            like((8, block), f32),
        ]
        + [like((block, part), bf16)] * shards,
        [
            pltpu.VMEM((width, LANES), f32),
            pltpu.VMEM((bucket_count, LANES), f32),
            pltpu.VMEM((block, 2 * total), f32),
        ],
        flops=4 * total * total * part + 6 * total * width * part,
        transcendentals=3 * total * total,
    )

    for t in range(shards):
        if t not in later:
            near = t & -t
            passed, _ = lax.optimization_barrier((later[t ^ near], mixes))
            later[t] = swap(passed, "shard", near)
    later = [later[t] for t in range(shards)]
    mixes = exchange(mixes, "shard")
    (
        residual, gating, sent, sent_low, grad_y_rows, probs_rows, chosen_rows, residual_rows
    ) = call(
        route_kernel(shards, experts), "route", place,
        [*mixes, *later, own_tokens, own_grad, gains, router, target, expert_ids],
        [
            like((block, width), f32),
            like((block, LANES), f32),
            like((experts * shards, PAIR, width), bf16),
            like((slot_rows, width), bf16),
            like((slot_rows, width), f32),
            like((slot_rows, LANES), f32),
            like((slot_rows, LANES), f32),
            like((slot_rows, width), f32),
        ],
        flops=4 * block * width * width,
    )
    arrived = lax.all_to_all(
        sent, ("expert", "shard"), split_axis=0, concat_axis=0, tiled=True
    )

    later, targets, mixed, projected, logs, table, onehot, _ = lax.optimization_barrier(
        (later, targets, mixed, projected, logs, table, onehot, sent)
    )
    free, out_free, kept_queries, kept_mixed = call(
        free_kernel(shards, kept_rows), "free_tokens", place,
        [*later, targets, w_attn_out, mixed, projected],
        [
            like((total, part), bf16),
            like((part, width), f32),
            like((shards * kept_rows, part), bf16),
            like((shards * kept_rows, part), bf16),
        ],
        flops=4 * total * width * part,
    )

    def early(first_head, head_count, after):
        free_in, after = lax.optimization_barrier((free, after))
        size = head_count * HEAD_DIM
        return call(
            early_kernel(shards, kept_rows, local_heads, first_head),
            "attention_backward_free", place,
            [projected, free_in, logs, table, onehot, targets],
            [
                like((total, size), f32),
                like((size, total), f32),
                like((size, total), f32),
                like((8, 2 * total), f32),
                like((head_count, shards * kept_rows, total), f32),
            ],
            [pltpu.VMEM((block, 2 * total), f32)] * 2,
            flops=40 * total * total * size,
            transcendentals=head_count * total * total,
        )

    calls = [(0, 1), (1, local_heads - 1)]
    early_first = early(*calls[0], sent)
    arrived, early_first, free, out_free, kept_queries, kept_mixed = lax.optimization_barrier(
        (arrived, early_first, free, out_free, kept_queries, kept_mixed)
    )

    all_rows = arrived.shape[0] * PAIR
    hidden_own = w_in.shape[2]
    back, rows_moved, act_moved, grads, grad_hidden = call(
        expert_kernel, "experts", place, [arrived, w_in[0], w_out[0]],
        [
            like(arrived.shape, bf16),
            like((all_rows, width), bf16),
            like((all_rows, hidden_own), bf16),
            like((all_rows, width), bf16),
            like((all_rows, hidden_own), bf16),
        ],
        flops=8 * all_rows * width * hidden_own,
    )
    returned = lax.all_to_all(
        back, ("expert", "shard"), split_axis=0, concat_axis=0, tiled=True
    )
    early_second = early(*calls[1], back)
    returned, early_second = lax.optimization_barrier((returned, early_second))

    att_rows, grad_delta, summed, router_grid = call(
        slot_back_kernel(shards, experts), "slot_back", place,
        [
            returned, grad_y_rows, probs_rows, chosen_rows, residual_rows, sent_low, gains, router
        ],
        [
            like((kept_rows, width), bf16),
            like((slot_rows, width), f32),
            like((slot_rows, width), bf16),
            like((width, LANES), f32),
        ],
        flops=1e9,
    )
    att = [att_rows] + [swap(att_rows, "shard", t) for t in range(1, shards)]
    all_kept = shards * kept_rows
    paired = devices == 8
    half = like((devices // 2, piece, width), f32)
    gm_all, *out_parts = call(
        out_grad_kernel(shards), "mixer_out_grad", place,
        [*att, w_attn_out, out_free, kept_mixed],
        [like((all_kept, part), bf16)]
        + ([half, like(half.shape, bf16)] if paired else [like((part, width), f32)]),
        ([pltpu.VMEM((part, width), f32)] if paired else [])
        + [pltpu.VMEM((all_kept, width), bf16)],
        flops=1e8,
    )
    if paired:
        summed_pair = out_parts[0] + swap(out_parts[1], "expert", 1).astype(f32)

    used = local_heads * bucket_rows
    piece_width = 3 * part + used + experts + 1
    piece_width += -piece_width % LANES
    grad_projected, pieces = call(
        late_kernel(shards, kept_rows, experts, local_heads, calls), "attention_backward_kept", place,
        [
            *early_first, *early_second, gm_all, normed, projected, targets, onehot, kept_queries,
            router_grid,
        ],
        [
            like((total, 3 * part), bf16),
            like((devices * shards, piece, piece_width), bf16),
        ],
        [
            pltpu.VMEM((all_kept, part), bf16),
            pltpu.VMEM((all_kept, total), bf16),
            pltpu.VMEM((part, total), f32),
            pltpu.VMEM((part, total), f32),
            pltpu.VMEM((block, 2 * total), f32),
            pltpu.VMEM((8, 2 * total), f32),
            pltpu.VMEM((width, piece_width), f32),
        ],
        flops=10 * all_kept * total * part + 6 * total * width * part,
    )

    got = lax.all_to_all(
        pieces, ("expert", "shard"), split_axis=0, concat_axis=0, tiled=True
    )
    normed_parts = call(
        normed_back_kernel, "normed_back", place, [grad_projected, weights],
        [like((block, width), bf16)] * shards, flops=6 * total * width * part,
    )
    if paired:
        summed_pair, *normed_parts = lax.optimization_barrier((summed_pair, *normed_parts))
        out_terms = [summed_pair[0]] + [
            swap(summed_pair[j].astype(bf16), "expert", 2 * j) for j in range(1, devices // 2)
        ]
    else:
        out_terms = [lax.psum_scatter(out_parts[0], "expert", scatter_dimension=0, tiled=True)]
    piece_total, tables = call(
        sums_kernel(shards, experts, part, used), "sums", place, [got, *out_terms],
        [
            like((piece, 4 * width + LANES), bf16),
            like((8, LANES), f32),
        ],
        flops=1e7,
    )
    all_total = share_piece(piece_total)

    rows_moved, act_moved, grads, grad_hidden, grad_delta, _ = lax.optimization_barrier(
        (rows_moved, act_moved, grads, grad_hidden, grad_delta, piece_total)
    )
    grad_first, grad_second = call(
        expert_grads_kernel, "expert_weight_grads", place,
        [rows_moved, act_moved, grads, grad_hidden],
        [like((1, width, hidden_own), f32), like((1, hidden_own, width), f32)],
        flops=4 * all_rows * width * hidden_own,
    )
    output, grad_residual = call(
        token_back_kernel(experts), "token_back", place,
        [residual, gating, summed, grad_delta, own_grad, target],
        [like((block, width), bf16), like((block, width), f32)],
        flops=1e8,
    )

    held = dict(enumerate(normed_parts))
    step = 1
    while len(held) > 1:
        if len(held) == 2:
            held[0], held[step], _ = lax.optimization_barrier((held[0], held[step], piece_total))
        held = {
            t: held[t].astype(f32) + swap(held[t ^ step].astype(bf16), "shard", step).astype(f32)
            for t in held
            if not t & step
        }
        step *= 2
    tokens_f = own_tokens.astype(f32)
    factor_one = rms_factor(tokens_f)
    grad_tokens = grad_residual + norm_back(
        held[0] * gains[0:1], tokens_f * factor_one, factor_one
    )

    total_table = tables[:shards, :used].reshape(shards, local_heads, bucket_rows)
    total_table = total_table.transpose(2, 0, 1).reshape(bucket_rows, HEADS)
    total_query, total_key, total_value, total_out, total_router, total_two, total_one = call(
        finish_kernel(shards, experts, len(all_total)), "finish", place,
        [*all_total, w_query, w_key, w_value, gain_attn.reshape(1, rows_own)],
        [like((rows_own, width), f32)] * 4
        + [like((experts, rows_own), f32)]
        + [like((1, rows_own), f32)] * 2,
        [pltpu.VMEM((rows_own, LANES), f32)],
        flops=1e7,
    )
    return (
        output[None],
        grad_tokens[None],
        total_one[0],
        total_table,
        total_query,
        total_key,
        total_value,
        total_out,
        total_router.T,
        total_two[0],
        grad_first,
        grad_second,
    )


def solution(mesh):
    in_specs = (
        P("expert", "shard", None),
        P("shard"),
        P("shard", None),
        P(),
        P("shard", None),
        P("shard", None),
        P("shard", None),
        P("shard", None),
        P("shard", None),
        P("shard"),
        P("expert", None, "shard"),
        P("expert", "shard", None),
        P("expert", "shard"),
        P("expert", "shard"),
        P("expert", "shard"),
        P("expert", "shard", None),
    )
    out_specs = (
        P("expert", "shard", None),
        P("expert", "shard", None),
        P("shard"),
        P("shard", None),
        P("shard", None),
        P("shard", None),
        P("shard", None),
        P("shard", None),
        P("shard", None),
        P("shard"),
        P("expert", None, "shard"),
        P("expert", "shard", None),
    )
    return jax.shard_map(
        per_device, mesh=mesh, in_specs=in_specs, out_specs=out_specs, check_vma=False
    )
```

```python
import jax
import jax.numpy as jnp
from jax import lax
from jax.experimental import pallas as pl
from jax.experimental.pallas import tpu as pltpu
from jax.sharding import PartitionSpec as P

HEADS = 12
HEAD_DIM = 64
CAP = 4
PAIR = 2 * CAP
LANES = 128

bf16 = jnp.bfloat16
f32 = jnp.float32
epsilon = 1e-06
score_scale = HEAD_DIM ** (-0.5)

NN = (((1,), (0,)), ((), ()))
NT = (((1,), (1,)), ((), ()))
TN = (((0,), (0,)), ((), ()))


def mm(a, b, dims=NN):
    return lax.dot_general(a, b, dims, preferred_element_type=f32)


def split(value):
    high = value.astype(bf16)
    rest = value - high.astype(f32)
    middle = rest.astype(bf16)
    return high, middle, (rest - middle.astype(f32)).astype(bf16)


def mm_left(a, b, dims=NN):
    return sum(mm(part, b, dims) for part in split(a))


def mm_right(a, b, dims=NN):
    return sum(mm(a, part, dims) for part in split(b))


def rms_factor(values):
    return lax.rsqrt(jnp.mean(values * values, axis=-1, keepdims=True) + epsilon)


def norm_back(grad_normed, normed_pre, factor):
    return factor * (
        grad_normed - normed_pre * jnp.mean(grad_normed * normed_pre, axis=-1, keepdims=True)
    )


def gelu_back(hidden, grad_act):
    return jax.vjp(jax.nn.gelu, hidden)[1](grad_act)[0]


def swap(value, axis, bits):
    count = lax.axis_size(axis)
    return lax.ppermute(value, axis, [(i, i ^ bits) for i in range(count)])


def gather_blocks(value, axis):
    held = {0: value}
    step = lax.axis_size(axis) // 2
    while step >= 1:
        for t in list(held):
            held[t ^ step] = swap(held[t], axis, step)
        step //= 2
    return [held[t] for t in range(len(held))]


def exchange(blocks, axis):
    return [blocks[0]] + [swap(blocks[t], axis, t) for t in range(1, len(blocks))]


def share_piece(piece):
    count = lax.axis_size("expert")
    if count != 8:
        return [lax.all_gather(piece, "expert", axis=0)]
    held = {0: piece}
    for t in (4, 2, 6):
        held[t] = swap(piece, "expert", t)
    for t in (0, 4, 2, 6):
        held[t ^ 1] = swap(held[t], "expert", 1)
    return [held[t] for t in range(count)]


VM = pl.BlockSpec(memory_space=pltpu.VMEM)
SM = pl.BlockSpec(memory_space=pltpu.SMEM)


def call(kernel, name, place, args, outs, scratch=(), flops=1e9, transcendentals=0):
    size = sum(a.size * a.dtype.itemsize for a in args)
    size += sum(o.size * o.dtype.itemsize for o in outs)
    return pl.pallas_call(
        kernel,
        out_shape=tuple(outs),
        in_specs=[SM] + [VM] * len(args),
        out_specs=tuple([VM] * len(outs)),
        scratch_shapes=list(scratch),
        compiler_params=pltpu.CompilerParams(vmem_limit_bytes=56 * 2**20),
        cost_estimate=pl.CostEstimate(
            flops=int(flops), bytes_accessed=int(size), transcendentals=int(transcendentals)
        ),
        name=name,
    )(place, *args)


def like(shape, dtype):
    return jax.ShapeDtypeStruct(shape, dtype)


def block_at(index, size):
    if isinstance(index, int):
        return slice(index * size, (index + 1) * size)
    return pl.ds(pl.multiple_of(index * size, size), size)


def lanes_at(index, size, count):
    if isinstance(index, int):
        return slice(index * size, index * size + count)
    return pl.ds(pl.multiple_of(index * size, size), count)


def steps(count, unroll, step):
    if unroll:
        for a in range(count):
            step(a, 0)
    else:
        lax.fori_loop(0, count, step, 0)


def pack_kernel(
    place, wq, wk, wv, router, both_gains, heads, ids, slots, keep, *rest
):
    outs, target, tall, flat = rest[:-3], rest[-3], rest[-2], rest[-1]
    me = place[0]
    shards = len(outs)
    rows, width = wq.shape
    part = width // shards
    experts = router.shape[0]
    extra = outs[0].shape[1] - 3 * part
    tall[...] = jnp.zeros_like(tall)
    tall[:experts, :] = router[...].astype(f32)
    tall[experts : experts + 2, :] = both_gains[...].astype(f32)
    small = tall[...].T[:, :extra].astype(bf16)
    slot = ids[...] * CAP + slots[...]
    target[...] = jnp.where(keep[...] > 0, slot, -1).astype(f32)
    flat[...] = jnp.zeros_like(flat)
    flat[: heads.shape[0], : heads.shape[1]] = heads[...].astype(f32)
    flat[heads.shape[0] : heads.shape[0] + 1, : target.shape[1]] = target[...]
    last = flat[...].astype(bf16)
    for t in range(shards):
        for owner in range(shards):

            @pl.when((me ^ t) == owner)
            def _(t=t, owner=owner):
                cols = slice(owner * part, (owner + 1) * part)
                joined = jnp.concatenate(
                    [wq[:, cols], wk[:, cols], wv[:, cols], small], axis=1
                )
                outs[t][:rows, :] = joined

        outs[t][rows:, :] = last


def bias_rows(offsets_row, count):
    width = offsets_row.shape[1]
    rows = jnp.broadcast_to(offsets_row, (8, width))
    rows = pltpu.roll(rows, width - (count - 1), 1)
    place = lax.broadcasted_iota(jnp.int32, (8, width), 0)
    for bit in (1, 2, 4):
        rows = jnp.where((place & bit) != 0, pltpu.roll(rows, bit, 1), rows)
    while rows.shape[0] < count:
        rows = jnp.concatenate([rows, pltpu.roll(rows, rows.shape[0], 1)], axis=0)
    return rows


def diagonal_row(grid):
    total, width = grid.shape
    count = total
    while count > 8:
        count //= 2
        grid = grid[:count] + pltpu.roll(grid[count:], width - count, 1)
    place = lax.broadcasted_iota(jnp.int32, (8, width), 0)
    for bit in (4, 2, 1):
        grid = jnp.where((place & bit) != 0, pltpu.roll(grid, width - bit, 1), grid)
    return pltpu.roll(jnp.sum(grid, axis=0, keepdims=True), total - 1, 1)


def forward_kernel(shards, experts, local_heads):
    def kernel(place, *refs):
        tok = refs[:shards]
        wts = refs[shards : 2 * shards]
        buckets = refs[2 * shards]
        rest = refs[2 * shards + 1 :]
        (
            normed, weights, projected, mixed, logs, gains, router, table, onehot, targets
        ) = rest[:10]
        mixes = rest[10 : 10 + shards]
        small_f, heads_f, bias = rest[10 + shards :]
        me = place[0]
        block = tok[0].shape[0]
        total = block * shards
        part = local_heads * HEAD_DIM
        rows_own = weights.shape[0] // shards
        used = min(wts[0].shape[1] - 3 * part, LANES)
        bucket_rows = onehot.shape[0] // shards
        small_f[...] = jnp.zeros_like(small_f)
        targets[...] = jnp.zeros_like(targets)
        for t in range(shards):
            weights[block_at(me ^ t, rows_own), :] = wts[t][:rows_own, : 3 * part]
            small_f[block_at(me ^ t, rows_own), :used] = wts[t][
                :rows_own, 3 * part : 3 * part + used
            ].astype(f32)
            last = wts[t][rows_own:, :block].astype(f32)
            heads_f[block_at(me ^ t, bucket_rows), :] = last[:bucket_rows, :LANES]
            targets[t : t + 1, :] = last[bucket_rows : bucket_rows + 1]
        router[...] = small_f[...].astype(bf16)
        turned = small_f[...].T
        gains[...] = jnp.concatenate(
            [turned[experts : experts + 2], jnp.zeros((6, turned.shape[1]), f32)], axis=0
        )
        gain = gains[0:1, :]
        for t in range(shards):
            tokens_f = tok[t][...].astype(f32)
            normed[block_at(me ^ t, block), :] = (tokens_f * rms_factor(tokens_f) * gain).astype(bf16)
        projected[...] = mm(normed[...], weights[...]).astype(bf16)
        onehot[...] = (
            lax.broadcasted_iota(jnp.int32, onehot.shape, 0) == buckets[0:1, :]
        ).astype(bf16)
        small_f[:LANES, : onehot.shape[0]] = heads_f[...].T
        table[...] = jnp.zeros_like(table)
        for h in range(local_heads):
            table[h : h + 1, :] = small_f[pl.ds(me * local_heads + h, 1), : onehot.shape[0]]
        offsets = mm(table[...].astype(bf16), onehot[...])
        for h in range(local_heads):
            cols = slice(h * HEAD_DIM, (h + 1) * HEAD_DIM)
            bias[...] = bias_rows(offsets[h : h + 1, :], block)
            keys = projected[:, part + h * HEAD_DIM : part + (h + 1) * HEAD_DIM]
            values = projected[:, 2 * part + h * HEAD_DIM : 2 * part + (h + 1) * HEAD_DIM]

            def step(a, carry, cols=cols, keys=keys, values=values, h=h):
                rows = block_at(a, block)
                scores = mm(projected[rows, cols], keys, NT) * score_scale
                scores = scores + bias[:, lanes_at(shards - 1 - a, block, total)]
                peak = jnp.max(scores, axis=-1, keepdims=True)
                raised = jnp.exp(scores - peak)
                norm = jnp.sum(raised, axis=-1, keepdims=True)
                probs_low = (raised * (1.0 / norm)).astype(bf16)
                mixed[rows, cols] = mm(probs_low, values).astype(bf16)
                logs[rows, h : h + 1] = peak + jnp.log(norm)
                return carry

            steps(shards, True, step)
        for t in range(shards):
            mixes[t][...] = mixed[block_at(me ^ t, block), :]

    return kernel


def slot_places(target_row, slot_rows):
    row = lax.broadcasted_iota(jnp.int32, (slot_rows, target_row.shape[1]), 0)
    slot = (row >> 3) * CAP + (row & (CAP - 1))
    return (slot.astype(f32) == target_row).astype(f32)


def kept_places(target_row, slots):
    row = lax.broadcasted_iota(jnp.int32, (slots, target_row.shape[1]), 0)
    return (row.astype(f32) == target_row).astype(bf16)


def is_grad_row(shape):
    return (lax.broadcasted_iota(jnp.int32, shape, 0) & CAP) != 0


def route_kernel(shards, experts):
    def kernel(place, *refs):
        mix = refs[:shards]
        outw = refs[shards : 2 * shards]
        tokens, grad_out, gains, router, target, ids = refs[2 * shards : 2 * shards + 6]
        residual, gating, sent, sent_low, grad_y_rows, probs_rows, chosen_rows, residual_rows = refs[
            2 * shards + 6 :
        ]
        value = tokens[...].astype(f32)
        for t in range(shards):
            value = value + mm(mix[t][...], outw[t][: mix[t].shape[1], :])
        residual[...] = value
        ffn_in = (value * rms_factor(value) * gains[1:2, :]).astype(bf16)
        logits = mm(ffn_in, router[...])
        lane = lax.broadcasted_iota(jnp.int32, logits.shape, 1)
        logits = jnp.where(lane < experts, logits, -1e30)
        raised = jnp.exp(logits - jnp.max(logits, axis=-1, keepdims=True))
        raised = jnp.where(lane < experts, raised, 0.0)
        probs = raised / jnp.sum(raised, axis=-1, keepdims=True)
        expert = lax.broadcasted_iota(jnp.int32, (LANES, ids.shape[1]), 0)
        chosen = (expert == ids[...]).astype(f32).T
        gating[...] = jnp.broadcast_to(
            jnp.sum(probs * chosen, axis=-1, keepdims=True), gating.shape
        )
        slot_rows = experts * PAIR
        places = slot_places(target[...], slot_rows)
        places_low = places.astype(bf16)
        rows = mm(places_low, ffn_in)
        grad_y = mm(places_low, grad_out[...])
        probs_r = mm_right(places_low, probs)
        chosen_r = mm(places_low, chosen.astype(bf16))
        gate_r = jnp.sum(probs_r * chosen_r, axis=-1, keepdims=True)
        joined = jnp.where(is_grad_row(rows.shape), gate_r * grad_y, rows)
        for e in range(experts):
            piece = joined[e * PAIR : (e + 1) * PAIR].astype(bf16)
            for t in range(shards):
                sent[e * shards + t] = piece
        sent_low[...] = rows.astype(bf16)
        grad_y_rows[...] = grad_y
        probs_rows[...] = probs_r
        chosen_rows[...] = chosen_r
        residual_rows[...] = mm_right(places_low, value)

    return kernel


def expert_kernel(place, arrived, first, second, back, rows_moved, act_moved, grads, grad_hidden):
    blocks = arrived.shape[0]
    width = arrived.shape[2]
    chunk = min(32, blocks)

    def step(c):
        at = pl.ds(c * chunk, chunk)
        flat = pl.ds(pl.multiple_of(c * chunk * PAIR, chunk * PAIR), chunk * PAIR)
        both = arrived[at].astype(f32).reshape(chunk * PAIR, width)
        is_grad = is_grad_row(both.shape)
        both_low = both.astype(bf16)
        hidden = mm(both_low, first[...])
        act = jax.nn.gelu(hidden)
        act_low = act.astype(bf16)
        grad_low = jnp.where(is_grad, both, 0.0).astype(bf16)
        grad_act = mm(grad_low, second[...], NT)
        grad_h = gelu_back(pltpu.roll(hidden, CAP, 0), grad_act)
        grad_h = jnp.where(is_grad, grad_h, 0.0).astype(bf16)
        out = jnp.where(is_grad, mm(grad_h, first[...], NT), mm(act_low, second[...]))
        back[at] = out.reshape(chunk, PAIR, width).astype(bf16)
        rows_moved[flat, :] = pltpu.roll(both, CAP, 0).astype(bf16)
        act_moved[flat, :] = pltpu.roll(act_low.astype(f32), CAP, 0).astype(bf16)
        grads[flat, :] = grad_low
        grad_hidden[flat, :] = grad_h

    if blocks == chunk:
        step(0)
    else:
        pl.loop(0, blocks // chunk)(step)


def expert_grads_kernel(place, rows_moved, act_moved, grads, grad_hidden, grad_first, grad_second):
    grad_first[0] = mm(rows_moved[...], grad_hidden[...], TN)
    grad_second[0] = mm(act_moved[...], grads[...], TN)


def slot_sums(returned, shards, experts):
    width = returned.shape[2]
    value = returned[...].astype(f32).reshape(experts, shards, PAIR, width)
    total = value[:, 0]
    for t in range(1, shards):
        total = total + value[:, t]
    return total.reshape(experts * PAIR, width).astype(bf16)


def slot_back_kernel(shards, experts):
    def kernel(
        place, returned, grad_y_rows, probs_rows, chosen_rows, residual_rows, sent_low, gains, router,
        att_rows, grad_delta, summed, grid
    ):
        total = slot_sums(returned, shards, experts)
        summed[...] = total
        total = total.astype(f32)
        is_grad = is_grad_row(total.shape)
        out_rows = pltpu.roll(total, CAP, 0)
        grad_y = grad_y_rows[...]
        probs = probs_rows[...]
        chosen = chosen_rows[...]
        gate = jnp.sum(probs * chosen, axis=-1, keepdims=True)
        grad_gate = jnp.sum(grad_y * out_rows, axis=-1, keepdims=True)
        grad_logits = grad_gate * gate * (chosen - probs)
        grad_logits = jnp.where(is_grad_row(grad_logits.shape), grad_logits, 0.0)
        grad_ffn = jnp.where(is_grad, total, 0.0) + mm_left(
            grad_logits, router[...], NT
        )
        values = residual_rows[...]
        factor = rms_factor(values)
        normed = values * factor
        delta = norm_back(grad_ffn * gains[1:2, :], normed, factor)
        delta = jnp.where(is_grad, delta, 0.0)
        grad_delta[...] = delta
        att = jnp.where(is_grad, grad_y + delta, 0.0).astype(bf16)
        slot = lax.broadcasted_iota(jnp.int32, (att_rows.shape[0], total.shape[0]), 0)
        row = lax.broadcasted_iota(jnp.int32, (att_rows.shape[0], total.shape[0]), 1)
        pick = row == ((slot >> 2) * PAIR + CAP + (slot & (CAP - 1)))
        att_rows[...] = mm(pick.astype(f32).astype(bf16), att).astype(bf16)
        lane = lax.broadcasted_iota(jnp.int32, (total.shape[0], LANES), 1)
        one = (lane == experts).astype(bf16)
        grid[...] = mm_right(sent_low[...], grad_logits, TN) + mm_left(grad_ffn * normed, one, TN)

    return kernel


def token_back_kernel(experts):
    def kernel(
        place, residual, gating, summed, grad_delta, grad_out, target, output, grad_residual
    ):
        places = slot_places(target[...], experts * PAIR)
        is_grad = is_grad_row(places.shape)
        rows = jnp.where(is_grad, 0.0, places).astype(bf16)
        token_out = mm(rows, summed[...], TN)
        output[...] = (residual[...] + gating[:, 0:1] * token_out).astype(bf16)
        grad_residual[...] = grad_out[...].astype(f32) + mm_right(
            jnp.where(is_grad, places, 0.0).astype(bf16), grad_delta[...], TN
        )

    return kernel


def free_kernel(shards, slots):
    def kernel(place, *refs):
        blocks = refs[:shards]
        targets, out_w, mixed, projected, free, out_free, kept_queries, kept_mixed = refs[shards:]
        me = place[0]
        block = targets.shape[1]
        part = mixed.shape[1]
        taken = targets[...].T
        total_out = jnp.zeros(out_free.shape, f32)
        for t in range(shards):
            rows = block_at(me ^ t, block)
            grads = blocks[t][part:, :]
            grads = jnp.where(taken[:, t : t + 1] >= 0, 0.0, grads.astype(f32)).astype(bf16)
            free[rows, :] = mm(grads, out_w[...], NT).astype(bf16)
            total_out = total_out + mm(mixed[rows, :], grads, TN)
            places = kept_places(targets[t : t + 1, :], slots)
            at = slice(t * slots, (t + 1) * slots)
            kept_queries[at, :] = mm(places, projected[rows, :part]).astype(bf16)
            kept_mixed[at, :] = mm(places, mixed[rows, :]).astype(bf16)
        out_free[...] = total_out

    return kernel


def early_kernel(shards, slots, local_heads, first_head):
    def kernel(
        place, projected, free, logs, table, onehot, targets,
        gq, gk, gv, diagonals, kept_probs, bias, sums,
    ):
        me = place[0]
        total = projected.shape[0]
        block = total // shards
        part = local_heads * HEAD_DIM
        offsets = mm(table[...].astype(bf16), onehot[...])
        diagonals[...] = jnp.zeros_like(diagonals)
        gk[...] = jnp.zeros_like(gk)
        gv[...] = jnp.zeros_like(gv)
        for n in range(kept_probs.shape[0]):
            h = first_head + n
            cols = slice(h * HEAD_DIM, (h + 1) * HEAD_DIM)
            own = slice(n * HEAD_DIM, (n + 1) * HEAD_DIM)
            bias[...] = bias_rows(offsets[h : h + 1, :], block)
            sums[...] = jnp.zeros_like(sums)
            keys = projected[:, part + h * HEAD_DIM : part + (h + 1) * HEAD_DIM]
            values = projected[:, 2 * part + h * HEAD_DIM : 2 * part + (h + 1) * HEAD_DIM]

            def step(a, carry, n=n, h=h, cols=cols, own=own, keys=keys, values=values):
                rows = block_at(a, block)
                lanes = lanes_at(shards - 1 - a, block, total)
                queries = projected[rows, cols]
                gm = free[rows, cols]
                scores = mm(queries, keys, NT) * score_scale + bias[:, lanes]
                probs = jnp.exp(scores - logs[rows, h : h + 1])
                grad_probs = mm(gm, values, NT)
                dots = jnp.sum(probs * grad_probs, axis=-1, keepdims=True)
                grad_scores = (probs * (grad_probs - dots)).astype(bf16)
                sums[:, lanes] += grad_scores.astype(f32)
                gq[rows, own] = mm(grad_scores, keys) * score_scale
                gk[own, :] += mm(queries, grad_scores, TN)
                probs_low = probs.astype(bf16)
                gv[own, :] += mm(gm, probs_low, TN)
                rest = probs - probs_low.astype(f32)
                rest_low = rest.astype(bf16)
                last = (rest - rest_low.astype(f32)).astype(bf16)
                places = kept_places(targets[pl.ds(a ^ me, 1), :], slots)
                kept_probs[n, block_at(a ^ me, slots), :] = (
                    mm(places, probs_low) + mm(places, rest_low) + mm(places, last)
                )
                return carry

            steps(shards, slots <= 64, step)
            diagonals[h : h + 1, :] = diagonal_row(sums[...])

    return kernel


def out_grad_kernel(shards):
    def kernel(place, *refs):
        att = refs[:shards]
        out_w, out_free, kept_mixed, gm_all, *outs, att_all = refs[shards:]
        slots = att[0].shape[0]
        for t in range(shards):
            att_all[t * slots : (t + 1) * slots, :] = att[t][...]
        gm_all[...] = mm(att_all[...], out_w[...], NT).astype(bf16)
        total = out_free[...] + mm(kept_mixed[...], att_all[...], TN)
        if len(outs) == 1:
            outs[0][...] = total
            return
        keep, send, grid = outs
        grid[...] = total
        count, piece, _ = keep.shape
        for j in range(count):
            keep[j] = grid[block_at(place[1] ^ (2 * j), piece), :]
            send[j] = grid[block_at(place[1] ^ (2 * j + 1), piece), :].astype(bf16)

    return kernel


def late_kernel(shards, slots, experts, local_heads, calls):
    def kernel(place, *refs):
        early = [refs[5 * c : 5 * c + 5] for c in range(len(calls))]
        (
            gm_all, normed, projected, targets, onehot, kept_queries, router_grid,
            grad_projected, pieces,
            gq_all, scores_all, gk, gv, sums, diagonals, grid,
        ) = refs[5 * len(calls) :]
        me = place[0]
        total = normed.shape[0]
        block = total // shards
        part = local_heads * HEAD_DIM
        diagonals[...] = jnp.zeros_like(diagonals)
        all_rows = shards * slots
        chunk = min(all_rows, 2 * LANES)
        for c, (first_head, head_count) in enumerate(calls):
            gq_free, gk_free, gv_free, diagonals_free, kept_probs = early[c]
            gk[: head_count * HEAD_DIM, :] = gk_free[...]
            gv[: head_count * HEAD_DIM, :] = gv_free[...]
            for n in range(head_count):
                h = first_head + n
                cols = slice(h * HEAD_DIM, (h + 1) * HEAD_DIM)
                own = slice(n * HEAD_DIM, (n + 1) * HEAD_DIM)
                key_cols = slice(part + h * HEAD_DIM, part + (h + 1) * HEAD_DIM)
                value_cols = slice(2 * part + h * HEAD_DIM, 2 * part + (h + 1) * HEAD_DIM)
                keys = projected[:, key_cols]
                values = projected[:, value_cols]

                def step(i, carry, n=n, cols=cols, own=own, keys=keys, values=values):
                    rows = block_at(i, chunk)
                    gm = gm_all[rows, cols]
                    probs = kept_probs[n, rows, :]
                    grad_probs = mm(gm, values, NT)
                    dots = jnp.sum(probs * grad_probs, axis=-1, keepdims=True)
                    grad_scores = (probs * (grad_probs - dots)).astype(bf16)
                    gq_all[rows, cols] = (mm(grad_scores, keys) * score_scale).astype(bf16)
                    gk[own, :] += mm(kept_queries[rows, cols], grad_scores, TN)
                    gv[own, :] += mm(gm, probs.astype(bf16), TN)
                    scores_all[rows, :] = grad_scores
                    return carry

                if chunk == all_rows:
                    step(0, 0)
                else:
                    lax.fori_loop(0, all_rows // chunk, step, 0)
                sums[...] = jnp.zeros_like(sums)
                for t in range(shards):
                    lanes = pl.ds(pl.multiple_of((shards - 1 - (me ^ t)) * block, block), total)
                    places = kept_places(targets[t : t + 1, :], slots)
                    sums[:, lanes] += mm(places, scores_all[t * slots : (t + 1) * slots, :], TN)
                diagonals[h : h + 1, :] = diagonals_free[h : h + 1, :] + diagonal_row(sums[...])
                grad_projected[:, key_cols] = (gk[own, :] * score_scale).T.astype(bf16)
                grad_projected[:, value_cols] = gv[own, :].T.astype(bf16)
            for t in range(shards):
                rows = block_at(me ^ t, block)
                places = kept_places(targets[t : t + 1, :], slots)
                cols = slice(first_head * HEAD_DIM, (first_head + head_count) * HEAD_DIM)
                placed = mm(places, gq_all[t * slots : (t + 1) * slots, cols], TN)
                grad_projected[rows, cols] = (gq_free[rows, :] + placed).astype(bf16)
        low_onehot = onehot[...]
        grad_table = mm_left(diagonals[...], low_onehot, NT)
        width = 3 * part
        bucket_rows = low_onehot.shape[0] // shards
        used = local_heads * bucket_rows
        rows_own = grid.shape[0] // shards
        count, piece, _ = pieces.shape
        count = count // shards
        grid[:, :width] = mm(normed[...], grad_projected[...], TN)
        grid[:, width:] = jnp.zeros((grid.shape[0], grid.shape[1] - width), f32)
        grid[:, width + used : width + used + experts + 1] = router_grid[:, : experts + 1]
        for t in range(shards):
            row = jnp.concatenate(
                [
                    grad_table[h : h + 1, t * bucket_rows : (t + 1) * bucket_rows]
                    for h in range(local_heads)
                ],
                axis=1,
            )
            for p in range(count):
                at = t * rows_own + p * piece
                grid[at : at + 1, width : width + used] = row
        for p in range(count):
            for t in range(shards):
                at = t * rows_own + p * piece
                pieces[p * shards + t] = grid[at : at + piece, :].astype(bf16)

    return kernel


def normed_back_kernel(place, grad_projected, weights, *outs):
    me = place[0]
    block = outs[0].shape[0]
    for t in range(len(outs)):
        outs[t][...] = mm(grad_projected[block_at(me ^ t, block), :], weights[...], NT).astype(bf16)


def sums_kernel(shards, experts, part, used):
    def kernel(place, got, *refs):
        *out_terms, total, tables = refs
        count = got.shape[0] // shards
        width = 3 * part
        tables[...] = jnp.zeros_like(tables)
        router = None
        for t in range(shards):
            value = got[t].astype(f32)
            for p in range(1, count):
                value = value + got[p * shards + t].astype(f32)
            total[:, t * width : (t + 1) * width] = value[:, :width].astype(bf16)
            tables[t : t + 1, :used] = value[0:1, width : width + used]
            share = value[:, width + used : width + used + experts + 1]
            router = share if router is None else router + share
        at = shards * width
        value = out_terms[0][...]
        for term in out_terms[1:]:
            value = value + term[...].astype(f32)
        total[:, at : at + value.shape[1]] = value.astype(bf16)
        at += value.shape[1]
        total[:, at:] = jnp.zeros((total.shape[0], LANES), bf16)
        total[:, at : at + experts + 1] = router.astype(bf16)

    return kernel


def finish_kernel(shards, experts, blocks):
    def kernel(place, *refs):
        totals = refs[:blocks]
        wq, wk, wv, gain, gq, gk, gv, gout, grouter, gtwo, gone, grid = refs[blocks:]
        rows, width = gq.shape
        part = width // shards

        def put(at, value):
            for t in range(shards):
                cols = slice(t * part, (t + 1) * part)
                first = 3 * part * t
                gq[at, cols] = value[:, first : first + part]
                gk[at, cols] = value[:, first + part : first + 2 * part]
                gv[at, cols] = value[:, first + 2 * part : first + 3 * part]
            gout[at, :] = value[:, 3 * width : 4 * width]
            grid[at, :] = value[:, 4 * width :]

        if blocks > 1:
            piece = rows // blocks
            for r in range(blocks):
                at = block_at(place[1] ^ r, piece)
                put(at, totals[r][...].astype(f32))
        else:
            count, piece, _ = totals[0].shape
            for p in range(count):
                at = slice(p * piece, (p + 1) * piece)
                put(at, totals[0][p].astype(f32))
        turned = grid[...].T
        grouter[...] = turned[:experts]
        gtwo[...] = turned[experts : experts + 1]
        dots = (
            wq[...].astype(f32) * gq[...]
            + wk[...].astype(f32) * gk[...]
            + wv[...].astype(f32) * gv[...]
        )
        ones = jnp.ones((8, dots.shape[1]), bf16)
        gone[...] = mm_right(ones, dots, NT)[0:1] / gain[...].astype(f32)

    return kernel


def per_device(
    tokens, gain_attn, pos_table, buckets, w_query, w_key, w_value, w_attn_out, w_router, gain_ffn,
    w_in, w_out, expert_ids, slots, keep, grad_out,
):
    shards = lax.axis_size("shard")
    devices = lax.axis_size("expert")
    me = lax.axis_index("shard")
    place = jnp.stack([me, lax.axis_index("expert")]).astype(jnp.int32)
    block, width = tokens.shape[1:]
    total = block * shards
    rows_own = w_query.shape[0]
    local_heads = HEADS // shards
    part = local_heads * HEAD_DIM
    experts = w_router.shape[1]
    slot_rows = experts * PAIR
    kept_rows = experts * CAP
    bucket_rows = pos_table.shape[0]
    bucket_count = bucket_rows * shards
    piece = rows_own // devices
    own_tokens = tokens[0]
    own_grad = grad_out[0]

    extra = experts + 2
    extra += -(3 * part + extra) % LANES
    packed_width = 3 * part + extra
    *wts, target = call(
        pack_kernel, "pack_columns", place,
        [
            w_query, w_key, w_value, w_router.T, jnp.stack([gain_attn, gain_ffn]), pos_table,
            expert_ids, slots, keep,
        ],
        [like((rows_own + 16, packed_width), bf16)] * shards + [like((1, block), f32)],
        [pltpu.VMEM((extra + -extra % LANES, rows_own), f32), pltpu.VMEM((16, packed_width), f32)],
        flops=1e6,
    )
    held = {0: own_tokens}
    step = shards // 2
    held[step] = swap(own_tokens, "shard", step)
    held[step], _ = lax.optimization_barrier((held[step], wts))
    wts = exchange(wts, "shard")
    while step > 1:
        step //= 2
        for t in list(held):
            held[t ^ step] = swap(held[t], "shard", step)
    tok = [held[t] for t in range(shards)]

    later = jnp.concatenate([w_attn_out, own_grad], axis=0)
    later, _, _ = lax.optimization_barrier((later, wts, tok))
    later = {0: later}
    step = shards // 2
    while step >= 1:
        later[step] = swap(later[0], "shard", step)
        step //= 2

    bucket_row = jnp.pad(
        buckets, (0, 2 * total - buckets.shape[0]), constant_values=-1
    ).reshape(1, -1)
    (
        normed, weights, projected, mixed, logs, gains, router, table, onehot, targets, *mixes
    ) = call(
        forward_kernel(shards, experts, local_heads), "attention_forward", place,
        [*tok, *wts, bucket_row],
        [
            like((total, width), bf16),
            like((width, 3 * part), bf16),
            like((total, 3 * part), bf16),
            like((total, part), bf16),
            like((total, 8), f32),
            like((8, width), f32),
            like((width, LANES), bf16),
            like((8, bucket_count), f32),
            like((bucket_count, 2 * total), bf16),
            like((8, block), f32),
        ]
        + [like((block, part), bf16)] * shards,
        [
            pltpu.VMEM((width, LANES), f32),
            pltpu.VMEM((bucket_count, LANES), f32),
            pltpu.VMEM((block, 2 * total), f32),
        ],
        flops=4 * total * total * part + 6 * total * width * part,
        transcendentals=3 * total * total,
    )

    for t in range(shards):
        if t not in later:
            near = t & -t
            passed, _ = lax.optimization_barrier((later[t ^ near], mixes))
            later[t] = swap(passed, "shard", near)
    later = [later[t] for t in range(shards)]
    mixes = exchange(mixes, "shard")

    free, out_free, kept_queries, kept_mixed = call(
        free_kernel(shards, kept_rows), "free_tokens", place,
        [*later, targets, w_attn_out, mixed, projected],
        [
            like((total, part), bf16),
            like((part, width), f32),
            like((shards * kept_rows, part), bf16),
            like((shards * kept_rows, part), bf16),
        ],
        flops=4 * total * width * part,
    )
    mixes, free, out_free, kept_queries, kept_mixed = lax.optimization_barrier(
        (mixes, free, out_free, kept_queries, kept_mixed)
    )
    (
        residual, gating, sent, sent_low, grad_y_rows, probs_rows, chosen_rows, residual_rows
    ) = call(
        route_kernel(shards, experts), "route", place,
        [*mixes, *later, own_tokens, own_grad, gains, router, target, expert_ids],
        [
            like((block, width), f32),
            like((block, LANES), f32),
            like((experts * shards, PAIR, width), bf16),
            like((slot_rows, width), bf16),
            like((slot_rows, width), f32),
            like((slot_rows, LANES), f32),
            like((slot_rows, LANES), f32),
            like((slot_rows, width), f32),
        ],
        flops=4 * block * width * width,
    )
    arrived = lax.all_to_all(
        sent, ("expert", "shard"), split_axis=0, concat_axis=0, tiled=True
    )

    def early(first_head, head_count, after):
        free_in, after = lax.optimization_barrier((free, after))
        size = head_count * HEAD_DIM
        return call(
            early_kernel(shards, kept_rows, local_heads, first_head),
            "attention_backward_free", place,
            [projected, free_in, logs, table, onehot, targets],
            [
                like((total, size), f32),
                like((size, total), f32),
                like((size, total), f32),
                like((8, 2 * total), f32),
                like((head_count, shards * kept_rows, total), f32),
            ],
            [pltpu.VMEM((block, 2 * total), f32)] * 2,
            flops=40 * total * total * size,
            transcendentals=head_count * total * total,
        )

    calls = [(0, local_heads - 1), (local_heads - 1, 1)]
    early_first = early(*calls[0], sent)
    arrived, early_first = lax.optimization_barrier((arrived, early_first))

    all_rows = arrived.shape[0] * PAIR
    hidden_own = w_in.shape[2]
    back, rows_moved, act_moved, grads, grad_hidden = call(
        expert_kernel, "experts", place, [arrived, w_in[0], w_out[0]],
        [
            like(arrived.shape, bf16),
            like((all_rows, width), bf16),
            like((all_rows, hidden_own), bf16),
            like((all_rows, width), bf16),
            like((all_rows, hidden_own), bf16),
        ],
        flops=8 * all_rows * width * hidden_own,
    )
    returned = lax.all_to_all(
        back, ("expert", "shard"), split_axis=0, concat_axis=0, tiled=True
    )
    early_second = early(*calls[1], back)
    returned, early_second = lax.optimization_barrier((returned, early_second))

    att_rows, grad_delta, summed, router_grid = call(
        slot_back_kernel(shards, experts), "slot_back", place,
        [
            returned, grad_y_rows, probs_rows, chosen_rows, residual_rows, sent_low, gains, router
        ],
        [
            like((kept_rows, width), bf16),
            like((slot_rows, width), f32),
            like((slot_rows, width), bf16),
            like((width, LANES), f32),
        ],
        flops=1e9,
    )
    att = [att_rows] + [swap(att_rows, "shard", t) for t in range(1, shards)]
    all_kept = shards * kept_rows
    paired = devices == 8
    half = like((devices // 2, piece, width), f32)
    gm_all, *out_parts = call(
        out_grad_kernel(shards), "mixer_out_grad", place,
        [*att, w_attn_out, out_free, kept_mixed],
        [like((all_kept, part), bf16)]
        + ([half, like(half.shape, bf16)] if paired else [like((part, width), f32)]),
        ([pltpu.VMEM((part, width), f32)] if paired else [])
        + [pltpu.VMEM((all_kept, width), bf16)],
        flops=1e8,
    )
    if paired:
        out_parts[1] = swap(out_parts[1], "expert", 1)

    used = local_heads * bucket_rows
    piece_width = 3 * part + used + experts + 1
    piece_width += -piece_width % LANES
    grad_projected, pieces = call(
        late_kernel(shards, kept_rows, experts, local_heads, calls), "attention_backward_kept", place,
        [
            *early_first, *early_second, gm_all, normed, projected, targets, onehot, kept_queries,
            router_grid,
        ],
        [
            like((total, 3 * part), bf16),
            like((devices * shards, piece, piece_width), bf16),
        ],
        [
            pltpu.VMEM((all_kept, part), bf16),
            pltpu.VMEM((all_kept, total), bf16),
            pltpu.VMEM((part, total), f32),
            pltpu.VMEM((part, total), f32),
            pltpu.VMEM((block, 2 * total), f32),
            pltpu.VMEM((8, 2 * total), f32),
            pltpu.VMEM((width, piece_width), f32),
        ],
        flops=10 * all_kept * total * part + 6 * total * width * part,
    )

    pieces, grad_projected, out_parts, rows_moved, act_moved, grads, grad_hidden, grad_delta = (
        lax.optimization_barrier(
            (
                pieces, grad_projected, out_parts, rows_moved, act_moved, grads, grad_hidden,
                grad_delta,
            )
        )
    )
    if paired:
        summed_pair = out_parts[0] + out_parts[1].astype(f32)
    got = lax.all_to_all(
        pieces, ("expert", "shard"), split_axis=0, concat_axis=0, tiled=True
    )
    normed_parts = call(
        normed_back_kernel, "normed_back", place, [grad_projected, weights],
        [like((block, width), bf16)] * shards, flops=6 * total * width * part,
    )
    if paired:
        out_terms = [summed_pair[0]] + [
            swap(summed_pair[j].astype(bf16), "expert", 2 * j) for j in range(1, devices // 2)
        ]
    else:
        out_terms = [lax.psum_scatter(out_parts[0], "expert", scatter_dimension=0, tiled=True)]
    grad_first, grad_second = call(
        expert_grads_kernel, "expert_weight_grads", place,
        [rows_moved, act_moved, grads, grad_hidden],
        [like((1, width, hidden_own), f32), like((1, hidden_own, width), f32)],
        flops=4 * all_rows * width * hidden_own,
    )
    output, grad_residual = call(
        token_back_kernel(experts), "token_back", place,
        [residual, gating, summed, grad_delta, own_grad, target],
        [like((block, width), bf16), like((block, width), f32)],
        flops=1e8,
    )
    got, grad_first, grad_second, output, grad_residual = lax.optimization_barrier(
        (got, grad_first, grad_second, output, grad_residual)
    )
    piece_total, tables = call(
        sums_kernel(shards, experts, part, used), "sums", place, [got, *out_terms],
        [
            like((piece, 4 * width + LANES), bf16),
            like((8, LANES), f32),
        ],
        flops=1e7,
    )
    all_total = share_piece(piece_total)

    held = dict(enumerate(normed_parts))
    step = 1
    while len(held) > 1:
        if len(held) == 2:
            held[0], held[step], _ = lax.optimization_barrier((held[0], held[step], piece_total))
        held = {
            t: held[t].astype(f32) + swap(held[t ^ step].astype(bf16), "shard", step).astype(f32)
            for t in held
            if not t & step
        }
        step *= 2
    tokens_f = own_tokens.astype(f32)
    factor_one = rms_factor(tokens_f)
    grad_tokens = grad_residual + norm_back(
        held[0] * gains[0:1], tokens_f * factor_one, factor_one
    )

    total_table = tables[:shards, :used].reshape(shards, local_heads, bucket_rows)
    total_table = total_table.transpose(2, 0, 1).reshape(bucket_rows, HEADS)
    all_total[0], grad_tokens = lax.optimization_barrier((all_total[0], grad_tokens))
    total_query, total_key, total_value, total_out, total_router, total_two, total_one = call(
        finish_kernel(shards, experts, len(all_total)), "finish", place,
        [*all_total, w_query, w_key, w_value, gain_attn.reshape(1, rows_own)],
        [like((rows_own, width), f32)] * 4
        + [like((experts, rows_own), f32)]
        + [like((1, rows_own), f32)] * 2,
        [pltpu.VMEM((rows_own, LANES), f32)],
        flops=1e7,
    )
    return (
        output[None],
        grad_tokens[None],
        total_one[0],
        total_table,
        total_query,
        total_key,
        total_value,
        total_out,
        total_router.T,
        total_two[0],
        grad_first,
        grad_second,
    )


def solution(mesh):
    in_specs = (
        P("expert", "shard", None),
        P("shard"),
        P("shard", None),
        P(),
        P("shard", None),
        P("shard", None),
        P("shard", None),
        P("shard", None),
        P("shard", None),
        P("shard"),
        P("expert", None, "shard"),
        P("expert", "shard", None),
        P("expert", "shard"),
        P("expert", "shard"),
        P("expert", "shard"),
        P("expert", "shard", None),
    )
    out_specs = (
        P("expert", "shard", None),
        P("expert", "shard", None),
        P("shard"),
        P("shard", None),
        P("shard", None),
        P("shard", None),
        P("shard", None),
        P("shard", None),
        P("shard", None),
        P("shard"),
        P("expert", None, "shard"),
        P("expert", "shard", None),
    )
    return jax.shard_map(
        per_device, mesh=mesh, in_specs=in_specs, out_specs=out_specs, check_vma=False
    )
```

```python
import jax
import jax.numpy as jnp
from jax import lax
from jax.experimental import pallas as pl
from jax.experimental.pallas import tpu as pltpu
from jax.sharding import PartitionSpec as P

HEADS = 12
HEAD_DIM = 64
CAP = 4
PAIR = 2 * CAP
LANES = 128

bf16 = jnp.bfloat16
f32 = jnp.float32
epsilon = 1e-06
score_scale = HEAD_DIM ** (-0.5)

NN = (((1,), (0,)), ((), ()))
NT = (((1,), (1,)), ((), ()))
TN = (((0,), (0,)), ((), ()))


def mm(a, b, dims=NN):
    return lax.dot_general(a, b, dims, preferred_element_type=f32)


def split(value):
    high = value.astype(bf16)
    rest = value - high.astype(f32)
    middle = rest.astype(bf16)
    return high, middle, (rest - middle.astype(f32)).astype(bf16)


def mm_left(a, b, dims=NN):
    return sum(mm(part, b, dims) for part in split(a))


def mm_right(a, b, dims=NN):
    return sum(mm(a, part, dims) for part in split(b))


def rms_factor(values):
    return lax.rsqrt(jnp.mean(values * values, axis=-1, keepdims=True) + epsilon)


def norm_back(grad_normed, normed_pre, factor):
    return factor * (
        grad_normed - normed_pre * jnp.mean(grad_normed * normed_pre, axis=-1, keepdims=True)
    )


def gelu_back(hidden, grad_act):
    return jax.vjp(jax.nn.gelu, hidden)[1](grad_act)[0]


def swap(value, axis, bits):
    count = lax.axis_size(axis)
    return lax.ppermute(value, axis, [(i, i ^ bits) for i in range(count)])


def gather_blocks(value, axis):
    held = {0: value}
    step = lax.axis_size(axis) // 2
    while step >= 1:
        for t in list(held):
            held[t ^ step] = swap(held[t], axis, step)
        step //= 2
    return [held[t] for t in range(len(held))]


def exchange(blocks, axis):
    return [blocks[0]] + [swap(blocks[t], axis, t) for t in range(1, len(blocks))]


def share_piece(piece):
    count = lax.axis_size("expert")
    if count != 8:
        return [lax.all_gather(piece, "expert", axis=0)]
    held = {0: piece}
    for t in (4, 2, 6):
        held[t] = swap(piece, "expert", t)
    for t in (0, 4, 2, 6):
        held[t ^ 1] = swap(held[t], "expert", 1)
    return [held[t] for t in range(count)]


VM = pl.BlockSpec(memory_space=pltpu.VMEM)
SM = pl.BlockSpec(memory_space=pltpu.SMEM)


def call(kernel, name, place, args, outs, scratch=(), flops=1e9, transcendentals=0):
    size = sum(a.size * a.dtype.itemsize for a in args)
    size += sum(o.size * o.dtype.itemsize for o in outs)
    return pl.pallas_call(
        kernel,
        out_shape=tuple(outs),
        in_specs=[SM] + [VM] * len(args),
        out_specs=tuple([VM] * len(outs)),
        scratch_shapes=list(scratch),
        compiler_params=pltpu.CompilerParams(vmem_limit_bytes=56 * 2**20),
        cost_estimate=pl.CostEstimate(
            flops=int(flops), bytes_accessed=int(size), transcendentals=int(transcendentals)
        ),
        name=name,
    )(place, *args)


def like(shape, dtype):
    return jax.ShapeDtypeStruct(shape, dtype)


def block_at(index, size):
    if isinstance(index, int):
        return slice(index * size, (index + 1) * size)
    return pl.ds(pl.multiple_of(index * size, size), size)


def lanes_at(index, size, count):
    if isinstance(index, int):
        return slice(index * size, index * size + count)
    return pl.ds(pl.multiple_of(index * size, size), count)


def steps(count, unroll, step):
    if unroll:
        for a in range(count):
            step(a, 0)
    else:
        lax.fori_loop(0, count, step, 0)


def pack_kernel(
    place, wq, wk, wv, router, both_gains, heads, ids, slots, keep, *rest
):
    outs, target, tall, flat = rest[:-3], rest[-3], rest[-2], rest[-1]
    me = place[0]
    shards = len(outs)
    rows, width = wq.shape
    part = width // shards
    experts = router.shape[0]
    extra = outs[0].shape[1] - 3 * part
    tall[...] = jnp.zeros_like(tall)
    tall[:experts, :] = router[...].astype(f32)
    tall[experts : experts + 2, :] = both_gains[...].astype(f32)
    small = tall[...].T[:, :extra].astype(bf16)
    slot = ids[...] * CAP + slots[...]
    target[...] = jnp.where(keep[...] > 0, slot, -1).astype(f32)
    flat[...] = jnp.zeros_like(flat)
    flat[: heads.shape[0], : heads.shape[1]] = heads[...].astype(f32)
    flat[heads.shape[0] : heads.shape[0] + 1, : target.shape[1]] = target[...]
    last = flat[...].astype(bf16)
    for t in range(shards):
        for owner in range(shards):

            @pl.when((me ^ t) == owner)
            def _(t=t, owner=owner):
                cols = slice(owner * part, (owner + 1) * part)
                joined = jnp.concatenate(
                    [wq[:, cols], wk[:, cols], wv[:, cols], small], axis=1
                )
                outs[t][:rows, :] = joined

        outs[t][rows:, :] = last


def bias_rows(offsets_row, count):
    width = offsets_row.shape[1]
    rows = jnp.broadcast_to(offsets_row, (8, width))
    rows = pltpu.roll(rows, width - (count - 1), 1)
    place = lax.broadcasted_iota(jnp.int32, (8, width), 0)
    for bit in (1, 2, 4):
        rows = jnp.where((place & bit) != 0, pltpu.roll(rows, bit, 1), rows)
    while rows.shape[0] < count:
        rows = jnp.concatenate([rows, pltpu.roll(rows, rows.shape[0], 1)], axis=0)
    return rows


def diagonal_row(grid):
    total, width = grid.shape
    count = total
    while count > 8:
        count //= 2
        grid = grid[:count] + pltpu.roll(grid[count:], width - count, 1)
    place = lax.broadcasted_iota(jnp.int32, (8, width), 0)
    for bit in (4, 2, 1):
        grid = jnp.where((place & bit) != 0, pltpu.roll(grid, width - bit, 1), grid)
    return pltpu.roll(jnp.sum(grid, axis=0, keepdims=True), total - 1, 1)


def forward_kernel(shards, experts, local_heads):
    def kernel(place, *refs):
        tok = refs[:shards]
        wts = refs[shards : 2 * shards]
        buckets = refs[2 * shards]
        rest = refs[2 * shards + 1 :]
        (
            normed, weights, projected, mixed, logs, gains, router, table, onehot, targets
        ) = rest[:10]
        mixes = rest[10 : 10 + shards]
        small_f, heads_f, bias = rest[10 + shards :]
        me = place[0]
        block = tok[0].shape[0]
        total = block * shards
        part = local_heads * HEAD_DIM
        rows_own = weights.shape[0] // shards
        used = min(wts[0].shape[1] - 3 * part, LANES)
        bucket_rows = onehot.shape[0] // shards
        small_f[...] = jnp.zeros_like(small_f)
        targets[...] = jnp.zeros_like(targets)
        for t in range(shards):
            weights[block_at(me ^ t, rows_own), :] = wts[t][:rows_own, : 3 * part]
            small_f[block_at(me ^ t, rows_own), :used] = wts[t][
                :rows_own, 3 * part : 3 * part + used
            ].astype(f32)
            last = wts[t][rows_own:, :block].astype(f32)
            heads_f[block_at(me ^ t, bucket_rows), :] = last[:bucket_rows, :LANES]
            targets[t : t + 1, :] = last[bucket_rows : bucket_rows + 1]
        router[...] = small_f[...].astype(bf16)
        turned = small_f[...].T
        gains[...] = jnp.concatenate(
            [turned[experts : experts + 2], jnp.zeros((6, turned.shape[1]), f32)], axis=0
        )
        gain = gains[0:1, :]
        for t in range(shards):
            tokens_f = tok[t][...].astype(f32)
            normed[block_at(me ^ t, block), :] = (tokens_f * rms_factor(tokens_f) * gain).astype(bf16)
        projected[...] = mm(normed[...], weights[...]).astype(bf16)
        onehot[...] = (
            lax.broadcasted_iota(jnp.int32, onehot.shape, 0) == buckets[0:1, :]
        ).astype(bf16)
        small_f[:LANES, : onehot.shape[0]] = heads_f[...].T
        table[...] = jnp.zeros_like(table)
        for h in range(local_heads):
            table[h : h + 1, :] = small_f[pl.ds(me * local_heads + h, 1), : onehot.shape[0]]
        offsets = mm(table[...].astype(bf16), onehot[...])
        for h in range(local_heads):
            cols = slice(h * HEAD_DIM, (h + 1) * HEAD_DIM)
            bias[...] = bias_rows(offsets[h : h + 1, :], block)
            keys = projected[:, part + h * HEAD_DIM : part + (h + 1) * HEAD_DIM]
            values = projected[:, 2 * part + h * HEAD_DIM : 2 * part + (h + 1) * HEAD_DIM]

            def step(a, carry, cols=cols, keys=keys, values=values, h=h):
                rows = block_at(a, block)
                scores = mm(projected[rows, cols], keys, NT) * score_scale
                scores = scores + bias[:, lanes_at(shards - 1 - a, block, total)]
                peak = jnp.max(scores, axis=-1, keepdims=True)
                raised = jnp.exp(scores - peak)
                norm = jnp.sum(raised, axis=-1, keepdims=True)
                probs_low = (raised * (1.0 / norm)).astype(bf16)
                mixed[rows, cols] = mm(probs_low, values).astype(bf16)
                logs[rows, h : h + 1] = peak + jnp.log(norm)
                return carry

            steps(shards, True, step)
        for t in range(shards):
            mixes[t][...] = mixed[block_at(me ^ t, block), :]

    return kernel


def slot_places(target_row, slot_rows):
    row = lax.broadcasted_iota(jnp.int32, (slot_rows, target_row.shape[1]), 0)
    slot = (row >> 3) * CAP + (row & (CAP - 1))
    return (slot.astype(f32) == target_row).astype(f32)


def kept_places(target_row, slots):
    row = lax.broadcasted_iota(jnp.int32, (slots, target_row.shape[1]), 0)
    return (row.astype(f32) == target_row).astype(bf16)


def is_grad_row(shape):
    return (lax.broadcasted_iota(jnp.int32, shape, 0) & CAP) != 0


def route_kernel(shards, experts):
    def kernel(place, *refs):
        mix = refs[:shards]
        outw = refs[shards : 2 * shards]
        tokens, grad_out, gains, router, target, ids = refs[2 * shards : 2 * shards + 6]
        residual, gating, sent, sent_low, grad_y_rows, probs_rows, chosen_rows, residual_rows = refs[
            2 * shards + 6 :
        ]
        value = tokens[...].astype(f32)
        for t in range(shards):
            value = value + mm(mix[t][...], outw[t][: mix[t].shape[1], :])
        residual[...] = value
        ffn_in = (value * rms_factor(value) * gains[1:2, :]).astype(bf16)
        logits = mm(ffn_in, router[...])
        lane = lax.broadcasted_iota(jnp.int32, logits.shape, 1)
        logits = jnp.where(lane < experts, logits, -1e30)
        raised = jnp.exp(logits - jnp.max(logits, axis=-1, keepdims=True))
        raised = jnp.where(lane < experts, raised, 0.0)
        probs = raised / jnp.sum(raised, axis=-1, keepdims=True)
        expert = lax.broadcasted_iota(jnp.int32, (LANES, ids.shape[1]), 0)
        chosen = (expert == ids[...]).astype(f32).T
        gating[...] = jnp.broadcast_to(
            jnp.sum(probs * chosen, axis=-1, keepdims=True), gating.shape
        )
        slot_rows = experts * PAIR
        places = slot_places(target[...], slot_rows)
        places_low = places.astype(bf16)
        rows = mm(places_low, ffn_in)
        grad_y = mm(places_low, grad_out[...])
        probs_r = mm_right(places_low, probs)
        chosen_r = mm(places_low, chosen.astype(bf16))
        gate_r = jnp.sum(probs_r * chosen_r, axis=-1, keepdims=True)
        joined = jnp.where(is_grad_row(rows.shape), gate_r * grad_y, rows)
        for e in range(experts):
            piece = joined[e * PAIR : (e + 1) * PAIR].astype(bf16)
            for t in range(shards):
                sent[e * shards + t] = piece
        sent_low[...] = rows.astype(bf16)
        grad_y_rows[...] = grad_y
        probs_rows[...] = probs_r
        chosen_rows[...] = chosen_r
        residual_rows[...] = mm_right(places_low, value)

    return kernel


def expert_kernel(place, arrived, first, second, back, rows_moved, act_moved, grads, grad_hidden):
    blocks = arrived.shape[0]
    width = arrived.shape[2]
    chunk = min(32, blocks)

    def step(c):
        at = pl.ds(c * chunk, chunk)
        flat = pl.ds(pl.multiple_of(c * chunk * PAIR, chunk * PAIR), chunk * PAIR)
        both = arrived[at].astype(f32).reshape(chunk * PAIR, width)
        is_grad = is_grad_row(both.shape)
        both_low = both.astype(bf16)
        hidden = mm(both_low, first[...])
        act = jax.nn.gelu(hidden)
        act_low = act.astype(bf16)
        grad_low = jnp.where(is_grad, both, 0.0).astype(bf16)
        grad_act = mm(grad_low, second[...], NT)
        grad_h = gelu_back(pltpu.roll(hidden, CAP, 0), grad_act)
        grad_h = jnp.where(is_grad, grad_h, 0.0).astype(bf16)
        out = jnp.where(is_grad, mm(grad_h, first[...], NT), mm(act_low, second[...]))
        back[at] = out.reshape(chunk, PAIR, width).astype(bf16)
        rows_moved[flat, :] = pltpu.roll(both, CAP, 0).astype(bf16)
        act_moved[flat, :] = pltpu.roll(act_low.astype(f32), CAP, 0).astype(bf16)
        grads[flat, :] = grad_low
        grad_hidden[flat, :] = grad_h

    if blocks == chunk:
        step(0)
    else:
        pl.loop(0, blocks // chunk)(step)


def expert_grads_kernel(place, rows_moved, act_moved, grads, grad_hidden, grad_first, grad_second):
    grad_first[0] = mm(rows_moved[...], grad_hidden[...], TN)
    grad_second[0] = mm(act_moved[...], grads[...], TN)


def slot_sums(returned, shards, experts):
    width = returned.shape[2]
    value = returned[...].astype(f32).reshape(experts, shards, PAIR, width)
    total = value[:, 0]
    for t in range(1, shards):
        total = total + value[:, t]
    return total.reshape(experts * PAIR, width).astype(bf16)


def slot_back_kernel(shards, experts):
    def kernel(
        place, returned, grad_y_rows, probs_rows, chosen_rows, residual_rows, sent_low, gains, router,
        att_rows, grad_delta, summed, grid
    ):
        total = slot_sums(returned, shards, experts)
        summed[...] = total
        total = total.astype(f32)
        is_grad = is_grad_row(total.shape)
        out_rows = pltpu.roll(total, CAP, 0)
        grad_y = grad_y_rows[...]
        probs = probs_rows[...]
        chosen = chosen_rows[...]
        gate = jnp.sum(probs * chosen, axis=-1, keepdims=True)
        grad_gate = jnp.sum(grad_y * out_rows, axis=-1, keepdims=True)
        grad_logits = grad_gate * gate * (chosen - probs)
        grad_logits = jnp.where(is_grad_row(grad_logits.shape), grad_logits, 0.0)
        grad_ffn = jnp.where(is_grad, total, 0.0) + mm_left(
            grad_logits, router[...], NT
        )
        values = residual_rows[...]
        factor = rms_factor(values)
        normed = values * factor
        delta = norm_back(grad_ffn * gains[1:2, :], normed, factor)
        delta = jnp.where(is_grad, delta, 0.0)
        grad_delta[...] = delta
        att = jnp.where(is_grad, grad_y + delta, 0.0).astype(bf16)
        slot = lax.broadcasted_iota(jnp.int32, (att_rows.shape[0], total.shape[0]), 0)
        row = lax.broadcasted_iota(jnp.int32, (att_rows.shape[0], total.shape[0]), 1)
        pick = row == ((slot >> 2) * PAIR + CAP + (slot & (CAP - 1)))
        att_rows[...] = mm(pick.astype(f32).astype(bf16), att).astype(bf16)
        lane = lax.broadcasted_iota(jnp.int32, (total.shape[0], LANES), 1)
        one = (lane == experts).astype(bf16)
        grid[...] = mm_right(sent_low[...], grad_logits, TN) + mm_left(grad_ffn * normed, one, TN)

    return kernel


def token_back_kernel(experts):
    def kernel(
        place, residual, gating, summed, grad_delta, grad_out, target, output, grad_residual
    ):
        places = slot_places(target[...], experts * PAIR)
        is_grad = is_grad_row(places.shape)
        rows = jnp.where(is_grad, 0.0, places).astype(bf16)
        token_out = mm(rows, summed[...], TN)
        output[...] = (residual[...] + gating[:, 0:1] * token_out).astype(bf16)
        grad_residual[...] = grad_out[...].astype(f32) + mm_right(
            jnp.where(is_grad, places, 0.0).astype(bf16), grad_delta[...], TN
        )

    return kernel


def free_kernel(shards, slots):
    def kernel(place, *refs):
        blocks = refs[:shards]
        targets, out_w, mixed, projected, free, out_free, kept_queries, kept_mixed = refs[shards:]
        me = place[0]
        block = targets.shape[1]
        part = mixed.shape[1]
        taken = targets[...].T
        total_out = jnp.zeros(out_free.shape, f32)
        for t in range(shards):
            rows = block_at(me ^ t, block)
            grads = blocks[t][part:, :]
            grads = jnp.where(taken[:, t : t + 1] >= 0, 0.0, grads.astype(f32)).astype(bf16)
            free[rows, :] = mm(grads, out_w[...], NT).astype(bf16)
            total_out = total_out + mm(mixed[rows, :], grads, TN)
            places = kept_places(targets[t : t + 1, :], slots)
            at = slice(t * slots, (t + 1) * slots)
            kept_queries[at, :] = mm(places, projected[rows, :part]).astype(bf16)
            kept_mixed[at, :] = mm(places, mixed[rows, :]).astype(bf16)
        out_free[...] = total_out

    return kernel


def early_kernel(shards, slots, local_heads, first_head):
    def kernel(
        place, projected, free, logs, table, onehot, targets,
        gq, gk, gv, diagonals, kept_probs, bias, sums,
    ):
        me = place[0]
        total = projected.shape[0]
        block = total // shards
        part = local_heads * HEAD_DIM
        offsets = mm(table[...].astype(bf16), onehot[...])
        diagonals[...] = jnp.zeros_like(diagonals)
        gk[...] = jnp.zeros_like(gk)
        gv[...] = jnp.zeros_like(gv)
        for n in range(kept_probs.shape[0]):
            h = first_head + n
            cols = slice(h * HEAD_DIM, (h + 1) * HEAD_DIM)
            own = slice(n * HEAD_DIM, (n + 1) * HEAD_DIM)
            bias[...] = bias_rows(offsets[h : h + 1, :], block)
            sums[...] = jnp.zeros_like(sums)
            keys = projected[:, part + h * HEAD_DIM : part + (h + 1) * HEAD_DIM]
            values = projected[:, 2 * part + h * HEAD_DIM : 2 * part + (h + 1) * HEAD_DIM]

            def step(a, carry, n=n, h=h, cols=cols, own=own, keys=keys, values=values):
                rows = block_at(a, block)
                lanes = lanes_at(shards - 1 - a, block, total)
                queries = projected[rows, cols]
                gm = free[rows, cols]
                scores = mm(queries, keys, NT) * score_scale + bias[:, lanes]
                probs = jnp.exp(scores - logs[rows, h : h + 1])
                grad_probs = mm(gm, values, NT)
                dots = jnp.sum(probs * grad_probs, axis=-1, keepdims=True)
                grad_scores = (probs * (grad_probs - dots)).astype(bf16)
                sums[:, lanes] += grad_scores.astype(f32)
                gq[rows, own] = mm(grad_scores, keys) * score_scale
                gk[own, :] += mm(queries, grad_scores, TN)
                probs_low = probs.astype(bf16)
                gv[own, :] += mm(gm, probs_low, TN)
                rest = probs - probs_low.astype(f32)
                rest_low = rest.astype(bf16)
                last = (rest - rest_low.astype(f32)).astype(bf16)
                places = kept_places(targets[pl.ds(a ^ me, 1), :], slots)
                kept_probs[n, block_at(a ^ me, slots), :] = (
                    mm(places, probs_low) + mm(places, rest_low) + mm(places, last)
                )
                return carry

            steps(shards, slots <= 64, step)
            diagonals[h : h + 1, :] = diagonal_row(sums[...])

    return kernel


def out_grad_kernel(shards):
    def kernel(place, *refs):
        att = refs[:shards]
        out_w, out_free, kept_mixed, gm_all, *outs, att_all = refs[shards:]
        slots = att[0].shape[0]
        for t in range(shards):
            att_all[t * slots : (t + 1) * slots, :] = att[t][...]
        gm_all[...] = mm(att_all[...], out_w[...], NT).astype(bf16)
        total = out_free[...] + mm(kept_mixed[...], att_all[...], TN)
        if len(outs) == 1:
            outs[0][...] = total
            return
        keep, send, grid = outs
        grid[...] = total
        count, piece, _ = keep.shape
        for j in range(count):
            keep[j] = grid[block_at(place[1] ^ (2 * j), piece), :]
            send[j] = grid[block_at(place[1] ^ (2 * j + 1), piece), :].astype(bf16)

    return kernel


def late_kernel(shards, slots, experts, local_heads, calls):
    def kernel(place, *refs):
        early = [refs[5 * c : 5 * c + 5] for c in range(len(calls))]
        (
            gm_all, normed, projected, targets, onehot, kept_queries, router_grid,
            grad_projected, pieces,
            gq_all, scores_all, gk, gv, sums, diagonals, grid,
        ) = refs[5 * len(calls) :]
        me = place[0]
        total = normed.shape[0]
        block = total // shards
        part = local_heads * HEAD_DIM
        diagonals[...] = jnp.zeros_like(diagonals)
        all_rows = shards * slots
        chunk = min(all_rows, 2 * LANES)
        for c, (first_head, head_count) in enumerate(calls):
            gq_free, gk_free, gv_free, diagonals_free, kept_probs = early[c]
            gk[: head_count * HEAD_DIM, :] = gk_free[...]
            gv[: head_count * HEAD_DIM, :] = gv_free[...]
            for n in range(head_count):
                h = first_head + n
                cols = slice(h * HEAD_DIM, (h + 1) * HEAD_DIM)
                own = slice(n * HEAD_DIM, (n + 1) * HEAD_DIM)
                key_cols = slice(part + h * HEAD_DIM, part + (h + 1) * HEAD_DIM)
                value_cols = slice(2 * part + h * HEAD_DIM, 2 * part + (h + 1) * HEAD_DIM)
                keys = projected[:, key_cols]
                values = projected[:, value_cols]

                def step(i, carry, n=n, cols=cols, own=own, keys=keys, values=values):
                    rows = block_at(i, chunk)
                    gm = gm_all[rows, cols]
                    probs = kept_probs[n, rows, :]
                    grad_probs = mm(gm, values, NT)
                    dots = jnp.sum(probs * grad_probs, axis=-1, keepdims=True)
                    grad_scores = (probs * (grad_probs - dots)).astype(bf16)
                    gq_all[rows, cols] = (mm(grad_scores, keys) * score_scale).astype(bf16)
                    gk[own, :] += mm(kept_queries[rows, cols], grad_scores, TN)
                    gv[own, :] += mm(gm, probs.astype(bf16), TN)
                    scores_all[rows, :] = grad_scores
                    return carry

                if chunk == all_rows:
                    step(0, 0)
                else:
                    lax.fori_loop(0, all_rows // chunk, step, 0)
                sums[...] = jnp.zeros_like(sums)
                for t in range(shards):
                    lanes = pl.ds(pl.multiple_of((shards - 1 - (me ^ t)) * block, block), total)
                    places = kept_places(targets[t : t + 1, :], slots)
                    sums[:, lanes] += mm(places, scores_all[t * slots : (t + 1) * slots, :], TN)
                diagonals[h : h + 1, :] = diagonals_free[h : h + 1, :] + diagonal_row(sums[...])
                grad_projected[:, key_cols] = (gk[own, :] * score_scale).T.astype(bf16)
                grad_projected[:, value_cols] = gv[own, :].T.astype(bf16)
            for t in range(shards):
                rows = block_at(me ^ t, block)
                places = kept_places(targets[t : t + 1, :], slots)
                cols = slice(first_head * HEAD_DIM, (first_head + head_count) * HEAD_DIM)
                placed = mm(places, gq_all[t * slots : (t + 1) * slots, cols], TN)
                grad_projected[rows, cols] = (gq_free[rows, :] + placed).astype(bf16)
        low_onehot = onehot[...]
        grad_table = mm_left(diagonals[...], low_onehot, NT)
        width = 3 * part
        bucket_rows = low_onehot.shape[0] // shards
        used = local_heads * bucket_rows
        rows_own = grid.shape[0] // shards
        count, piece, _ = pieces.shape
        count = count // shards
        grid[:, :width] = mm(normed[...], grad_projected[...], TN)
        grid[:, width:] = jnp.zeros((grid.shape[0], grid.shape[1] - width), f32)
        grid[:, width + used : width + used + experts + 1] = router_grid[:, : experts + 1]
        for t in range(shards):
            row = jnp.concatenate(
                [
                    grad_table[h : h + 1, t * bucket_rows : (t + 1) * bucket_rows]
                    for h in range(local_heads)
                ],
                axis=1,
            )
            for p in range(count):
                at = t * rows_own + p * piece
                grid[at : at + 1, width : width + used] = row
        for p in range(count):
            for t in range(shards):
                at = t * rows_own + p * piece
                pieces[p * shards + t] = grid[at : at + piece, :].astype(bf16)

    return kernel


def normed_back_kernel(place, grad_projected, weights, *outs):
    me = place[0]
    block = outs[0].shape[0]
    for t in range(len(outs)):
        outs[t][...] = mm(grad_projected[block_at(me ^ t, block), :], weights[...], NT).astype(bf16)


def sums_kernel(shards, experts, part, used):
    def kernel(place, got, *refs):
        *out_terms, total, tables = refs
        count = got.shape[0] // shards
        width = 3 * part
        tables[...] = jnp.zeros_like(tables)
        router = None
        for t in range(shards):
            value = got[t].astype(f32)
            for p in range(1, count):
                value = value + got[p * shards + t].astype(f32)
            total[:, t * width : (t + 1) * width] = value[:, :width].astype(bf16)
            tables[t : t + 1, :used] = value[0:1, width : width + used]
            share = value[:, width + used : width + used + experts + 1]
            router = share if router is None else router + share
        at = shards * width
        value = out_terms[0][...]
        for term in out_terms[1:]:
            value = value + term[...].astype(f32)
        total[:, at : at + value.shape[1]] = value.astype(bf16)
        at += value.shape[1]
        total[:, at:] = jnp.zeros((total.shape[0], LANES), bf16)
        total[:, at : at + experts + 1] = router.astype(bf16)

    return kernel


def finish_kernel(shards, experts, blocks):
    def kernel(place, *refs):
        totals = refs[:blocks]
        wq, wk, wv, gain, gq, gk, gv, gout, grouter, gtwo, gone, grid = refs[blocks:]
        rows, width = gq.shape
        part = width // shards

        def put(at, value):
            for t in range(shards):
                cols = slice(t * part, (t + 1) * part)
                first = 3 * part * t
                gq[at, cols] = value[:, first : first + part]
                gk[at, cols] = value[:, first + part : first + 2 * part]
                gv[at, cols] = value[:, first + 2 * part : first + 3 * part]
            gout[at, :] = value[:, 3 * width : 4 * width]
            grid[at, :] = value[:, 4 * width :]

        if blocks > 1:
            piece = rows // blocks
            for r in range(blocks):
                at = block_at(place[1] ^ r, piece)
                put(at, totals[r][...].astype(f32))
        else:
            count, piece, _ = totals[0].shape
            for p in range(count):
                at = slice(p * piece, (p + 1) * piece)
                put(at, totals[0][p].astype(f32))
        turned = grid[...].T
        grouter[...] = turned[:experts]
        gtwo[...] = turned[experts : experts + 1]
        dots = (
            wq[...].astype(f32) * gq[...]
            + wk[...].astype(f32) * gk[...]
            + wv[...].astype(f32) * gv[...]
        )
        ones = jnp.ones((8, dots.shape[1]), bf16)
        gone[...] = mm_right(ones, dots, NT)[0:1] / gain[...].astype(f32)

    return kernel


def per_device(
    tokens, gain_attn, pos_table, buckets, w_query, w_key, w_value, w_attn_out, w_router, gain_ffn,
    w_in, w_out, expert_ids, slots, keep, grad_out,
):
    shards = lax.axis_size("shard")
    devices = lax.axis_size("expert")
    me = lax.axis_index("shard")
    place = jnp.stack([me, lax.axis_index("expert")]).astype(jnp.int32)
    block, width = tokens.shape[1:]
    total = block * shards
    rows_own = w_query.shape[0]
    local_heads = HEADS // shards
    part = local_heads * HEAD_DIM
    experts = w_router.shape[1]
    slot_rows = experts * PAIR
    kept_rows = experts * CAP
    bucket_rows = pos_table.shape[0]
    bucket_count = bucket_rows * shards
    piece = rows_own // devices
    own_tokens = tokens[0]
    own_grad = grad_out[0]

    extra = experts + 2
    extra += -(3 * part + extra) % LANES
    packed_width = 3 * part + extra
    *wts, target = call(
        pack_kernel, "pack_columns", place,
        [
            w_query, w_key, w_value, w_router.T, jnp.stack([gain_attn, gain_ffn]), pos_table,
            expert_ids, slots, keep,
        ],
        [like((rows_own + 16, packed_width), bf16)] * shards + [like((1, block), f32)],
        [pltpu.VMEM((extra + -extra % LANES, rows_own), f32), pltpu.VMEM((16, packed_width), f32)],
        flops=1e6,
    )
    held = {0: own_tokens}
    step = shards // 2
    held[step] = swap(own_tokens, "shard", step)
    wts = exchange(wts, "shard")
    held[step], _ = lax.optimization_barrier((held[step], wts[1:]))
    while step > 1:
        step //= 2
        for t in list(held):
            held[t ^ step] = swap(held[t], "shard", step)
    tok = [held[t] for t in range(shards)]

    later = jnp.concatenate([w_attn_out, own_grad], axis=0)
    later, _, _ = lax.optimization_barrier((later, wts, tok))
    later = {0: later}
    step = shards // 2
    while step >= 1:
        later[step] = swap(later[0], "shard", step)
        step //= 2

    bucket_row = jnp.pad(
        buckets, (0, 2 * total - buckets.shape[0]), constant_values=-1
    ).reshape(1, -1)
    (
        normed, weights, projected, mixed, logs, gains, router, table, onehot, targets, *mixes
    ) = call(
        forward_kernel(shards, experts, local_heads), "attention_forward", place,
        [*tok, *wts, bucket_row],
        [
            like((total, width), bf16),
            like((width, 3 * part), bf16),
            like((total, 3 * part), bf16),
            like((total, part), bf16),
            like((total, 8), f32),
            like((8, width), f32),
            like((width, LANES), bf16),
            like((8, bucket_count), f32),
            like((bucket_count, 2 * total), bf16),
            like((8, block), f32),
        ]
        + [like((block, part), bf16)] * shards,
        [
            pltpu.VMEM((width, LANES), f32),
            pltpu.VMEM((bucket_count, LANES), f32),
            pltpu.VMEM((block, 2 * total), f32),
        ],
        flops=4 * total * total * part + 6 * total * width * part,
        transcendentals=3 * total * total,
    )

    for t in range(shards):
        if t not in later:
            near = t & -t
            passed, _ = lax.optimization_barrier((later[t ^ near], mixes))
            later[t] = swap(passed, "shard", near)
    later = [later[t] for t in range(shards)]
    mixes = exchange(mixes, "shard")

    free, out_free, kept_queries, kept_mixed = call(
        free_kernel(shards, kept_rows), "free_tokens", place,
        [*later, targets, w_attn_out, mixed, projected],
        [
            like((total, part), bf16),
            like((part, width), f32),
            like((shards * kept_rows, part), bf16),
            like((shards * kept_rows, part), bf16),
        ],
        flops=4 * total * width * part,
    )
    mixes, free, out_free, kept_queries, kept_mixed = lax.optimization_barrier(
        (mixes, free, out_free, kept_queries, kept_mixed)
    )
    (
        residual, gating, sent, sent_low, grad_y_rows, probs_rows, chosen_rows, residual_rows
    ) = call(
        route_kernel(shards, experts), "route", place,
        [*mixes, *later, own_tokens, own_grad, gains, router, target, expert_ids],
        [
            like((block, width), f32),
            like((block, LANES), f32),
            like((experts * shards, PAIR, width), bf16),
            like((slot_rows, width), bf16),
            like((slot_rows, width), f32),
            like((slot_rows, LANES), f32),
            like((slot_rows, LANES), f32),
            like((slot_rows, width), f32),
        ],
        flops=4 * block * width * width,
    )
    arrived = lax.all_to_all(
        sent, ("expert", "shard"), split_axis=0, concat_axis=0, tiled=True
    )

    def early(first_head, head_count, after):
        free_in, after = lax.optimization_barrier((free, after))
        size = head_count * HEAD_DIM
        return call(
            early_kernel(shards, kept_rows, local_heads, first_head),
            "attention_backward_free", place,
            [projected, free_in, logs, table, onehot, targets],
            [
                like((total, size), f32),
                like((size, total), f32),
                like((size, total), f32),
                like((8, 2 * total), f32),
                like((head_count, shards * kept_rows, total), f32),
            ],
            [pltpu.VMEM((block, 2 * total), f32)] * 2,
            flops=40 * total * total * size,
            transcendentals=head_count * total * total,
        )

    calls = [(0, local_heads - 1), (local_heads - 1, 1)]
    early_first = early(*calls[0], sent)
    arrived, early_first = lax.optimization_barrier((arrived, early_first))

    all_rows = arrived.shape[0] * PAIR
    hidden_own = w_in.shape[2]
    back, rows_moved, act_moved, grads, grad_hidden = call(
        expert_kernel, "experts", place, [arrived, w_in[0], w_out[0]],
        [
            like(arrived.shape, bf16),
            like((all_rows, width), bf16),
            like((all_rows, hidden_own), bf16),
            like((all_rows, width), bf16),
            like((all_rows, hidden_own), bf16),
        ],
        flops=8 * all_rows * width * hidden_own,
    )
    returned = lax.all_to_all(
        back, ("expert", "shard"), split_axis=0, concat_axis=0, tiled=True
    )
    early_second = early(*calls[1], back)
    returned, early_second = lax.optimization_barrier((returned, early_second))

    att_rows, grad_delta, summed, router_grid = call(
        slot_back_kernel(shards, experts), "slot_back", place,
        [
            returned, grad_y_rows, probs_rows, chosen_rows, residual_rows, sent_low, gains, router
        ],
        [
            like((kept_rows, width), bf16),
            like((slot_rows, width), f32),
            like((slot_rows, width), bf16),
            like((width, LANES), f32),
        ],
        flops=1e9,
    )
    att = [att_rows] + [swap(att_rows, "shard", t) for t in range(1, shards)]
    all_kept = shards * kept_rows
    paired = devices == 8
    half = like((devices // 2, piece, width), f32)
    gm_all, *out_parts = call(
        out_grad_kernel(shards), "mixer_out_grad", place,
        [*att, w_attn_out, out_free, kept_mixed],
        [like((all_kept, part), bf16)]
        + ([half, like(half.shape, bf16)] if paired else [like((part, width), f32)]),
        ([pltpu.VMEM((part, width), f32)] if paired else [])
        + [pltpu.VMEM((all_kept, width), bf16)],
        flops=1e8,
    )
    if paired:
        out_parts[1] = swap(out_parts[1], "expert", 1)

    used = local_heads * bucket_rows
    piece_width = 3 * part + used + experts + 1
    piece_width += -piece_width % LANES
    grad_projected, pieces = call(
        late_kernel(shards, kept_rows, experts, local_heads, calls), "attention_backward_kept", place,
        [
            *early_first, *early_second, gm_all, normed, projected, targets, onehot, kept_queries,
            router_grid,
        ],
        [
            like((total, 3 * part), bf16),
            like((devices * shards, piece, piece_width), bf16),
        ],
        [
            pltpu.VMEM((all_kept, part), bf16),
            pltpu.VMEM((all_kept, total), bf16),
            pltpu.VMEM((part, total), f32),
            pltpu.VMEM((part, total), f32),
            pltpu.VMEM((block, 2 * total), f32),
            pltpu.VMEM((8, 2 * total), f32),
            pltpu.VMEM((width, piece_width), f32),
        ],
        flops=10 * all_kept * total * part + 6 * total * width * part,
    )

    pieces, grad_projected, out_parts, rows_moved, act_moved, grads, grad_hidden, grad_delta = (
        lax.optimization_barrier(
            (
                pieces, grad_projected, out_parts, rows_moved, act_moved, grads, grad_hidden,
                grad_delta,
            )
        )
    )
    if paired:
        summed_pair = out_parts[0] + out_parts[1].astype(f32)
    got = lax.all_to_all(
        pieces, ("expert", "shard"), split_axis=0, concat_axis=0, tiled=True
    )
    normed_parts = call(
        normed_back_kernel, "normed_back", place, [grad_projected, weights],
        [like((block, width), bf16)] * shards, flops=6 * total * width * part,
    )
    if paired:
        out_terms = [summed_pair[0]] + [
            swap(summed_pair[j].astype(bf16), "expert", 2 * j) for j in range(1, devices // 2)
        ]
    else:
        out_terms = [lax.psum_scatter(out_parts[0], "expert", scatter_dimension=0, tiled=True)]
    grad_first, grad_second = call(
        expert_grads_kernel, "expert_weight_grads", place,
        [rows_moved, act_moved, grads, grad_hidden],
        [like((1, width, hidden_own), f32), like((1, hidden_own, width), f32)],
        flops=4 * all_rows * width * hidden_own,
    )
    output, grad_residual = call(
        token_back_kernel(experts), "token_back", place,
        [residual, gating, summed, grad_delta, own_grad, target],
        [like((block, width), bf16), like((block, width), f32)],
        flops=1e8,
    )
    got, grad_first, grad_second, output, grad_residual = lax.optimization_barrier(
        (got, grad_first, grad_second, output, grad_residual)
    )
    piece_total, tables = call(
        sums_kernel(shards, experts, part, used), "sums", place, [got, *out_terms],
        [
            like((piece, 4 * width + LANES), bf16),
            like((8, LANES), f32),
        ],
        flops=1e7,
    )
    all_total = share_piece(piece_total)

    held = dict(enumerate(normed_parts))
    step = 1
    while len(held) > 1:
        if len(held) == 2:
            held[0], held[step], _ = lax.optimization_barrier((held[0], held[step], grad_first))
        held = {
            t: held[t].astype(f32) + swap(held[t ^ step].astype(bf16), "shard", step).astype(f32)
            for t in held
            if not t & step
        }
        step *= 2
    tokens_f = own_tokens.astype(f32)
    factor_one = rms_factor(tokens_f)
    grad_tokens = grad_residual + norm_back(
        held[0] * gains[0:1], tokens_f * factor_one, factor_one
    )

    total_table = tables[:shards, :used].reshape(shards, local_heads, bucket_rows)
    total_table = total_table.transpose(2, 0, 1).reshape(bucket_rows, HEADS)
    all_total[0], grad_tokens = lax.optimization_barrier((all_total[0], grad_tokens))
    total_query, total_key, total_value, total_out, total_router, total_two, total_one = call(
        finish_kernel(shards, experts, len(all_total)), "finish", place,
        [*all_total, w_query, w_key, w_value, gain_attn.reshape(1, rows_own)],
        [like((rows_own, width), f32)] * 4
        + [like((experts, rows_own), f32)]
        + [like((1, rows_own), f32)] * 2,
        [pltpu.VMEM((rows_own, LANES), f32)],
        flops=1e7,
    )
    return (
        output[None],
        grad_tokens[None],
        total_one[0],
        total_table,
        total_query,
        total_key,
        total_value,
        total_out,
        total_router.T,
        total_two[0],
        grad_first,
        grad_second,
    )


def solution(mesh):
    in_specs = (
        P("expert", "shard", None),
        P("shard"),
        P("shard", None),
        P(),
        P("shard", None),
        P("shard", None),
        P("shard", None),
        P("shard", None),
        P("shard", None),
        P("shard"),
        P("expert", None, "shard"),
        P("expert", "shard", None),
        P("expert", "shard"),
        P("expert", "shard"),
        P("expert", "shard"),
        P("expert", "shard", None),
    )
    out_specs = (
        P("expert", "shard", None),
        P("expert", "shard", None),
        P("shard"),
        P("shard", None),
        P("shard", None),
        P("shard", None),
        P("shard", None),
        P("shard", None),
        P("shard", None),
        P("shard"),
        P("expert", None, "shard"),
        P("expert", "shard", None),
    )
    return jax.shard_map(
        per_device, mesh=mesh, in_specs=in_specs, out_specs=out_specs, check_vma=False
    )
```
